256 devices in a mesh: inst: 32 (over z, y), tensor: 8 (over x, core).
Axes of the slice: x: 4, y: 4, z: 8, core: 2. Of those that a mesh axis runs over, the one named last changes fastest.
Arguments:
- queries: bfloat16 [32, 4, 8192], P('inst', None, 'tensor'), may hold values from -6 to 6
- new_states: bfloat16 [32, 4, 8192], P('inst', None, 'tensor'), may hold values from -24 to 24
- key_weight: bfloat16 [8192, 1024], P(None, 'tensor'), may hold values from -0.0625 to 0.0625
- value_weight: bfloat16 [8192, 1024], P(None, 'tensor'), may hold values from -0.0625 to 0.0625
- key_pool: bfloat16 [2048, 256, 1024], P('inst', None, 'tensor'), may hold values from -512 to 512
- value_pool: bfloat16 [2048, 256, 1024], P('inst', None, 'tensor'), may hold values from -6 to 6
- lengths: int32 [32], replicated, may hold values from 2048 to 16384, as said below
- page_table: int32 [32, 64], replicated, may hold values from -1 to 2047, as said below
Outputs:
- attention: bfloat16 [32, 4, 8192], P('inst', None, 'tensor')
The draws below stay inside these ranges and needn't reach their ends.
Inputs may be any that keep to these rules, and one draw needn't show every extreme that they name: `lengths`: half of the requests have at most 8192 tokens and the others more; one request has exactly 16384. `page_table`: entry [r, j] is the pool slot (instance index times 64 plus a slot of that instance) of page j of request r for j < ceil(lengths[r] / 256), and -1 beyond; no slot is named twice. Request r is served by instance r; a request of at most 8192 tokens has all its pages there; each longer request of n pages has n // 4 consecutive pages on one other instance, which serves a request of at most 8192 tokens, and the rest on instance r; an instance holds lent pages of at most one request. Some request lends to the instance 32 // 2 indices away and some request lends to the instance one index below it.
All inputs are finite; a program needn't handle non-finite values.
Results may differ from the reference program's by a relative error of at most 0.0072.
Values may be sent and summed in bfloat16 or wider, within the bound.
A program may use at most 128 MiB of HBM per device.

```python
import math
import jax
import jax.numpy as jnp
from jax import lax

D = 8192
H = 64
KVH = 8
HD = 128
STEPS = 4
PAGE = 256
MAXP = 64
REQS = 32
POOL = 2048


def plan_tables(key):
    plan_key = jax.random.fold_in(key, 101)
    order_key, short_key, long_key, run_key, slot_key, pick_key = jax.random.split(plan_key, 6)
    request_count = REQS
    half_count = request_count // 2
    max_tokens = MAXP * PAGE
    first_long = jax.random.randint(pick_key, (), 0, request_count).astype(jnp.int32)
    far_lender = (first_long + half_count) % request_count
    near_lender = (first_long + 1) % request_count
    second_long = (first_long + 2) % request_count
    request_ids = jnp.arange(request_count, dtype=jnp.int32)
    special = (request_ids == first_long) | (request_ids == far_lender) | (request_ids == near_lender) | (request_ids == second_long)
    shuffled = jax.random.permutation(order_key, request_count).astype(jnp.int32)
    sort_scores = shuffled + request_count * special.astype(jnp.int32)
    others = jnp.argsort(sort_scores, stable=True).astype(jnp.int32)[:request_count - 4]
    fill_slots = jnp.concatenate([jnp.arange(2, half_count, dtype=jnp.int32), jnp.arange(half_count + 2, request_count, dtype=jnp.int32)])
    rank_order = jnp.zeros((request_count,), jnp.int32).at[fill_slots].set(others)
    rank_order = rank_order.at[0].set(far_lender).at[1].set(near_lender)
    rank_order = rank_order.at[half_count].set(first_long).at[half_count + 1].set(second_long)
    positions = jnp.argsort(rank_order).astype(jnp.int32)
    short_length = jax.random.randint(short_key, (request_count,), max_tokens // 8, max_tokens // 2 + 1)
    long_length = jax.random.randint(long_key, (request_count,), max_tokens // 2 + 1, max_tokens + 1)
    is_long = positions >= half_count
    lengths = jnp.where(is_long, long_length, short_length)
    lengths = jnp.where(positions == half_count, max_tokens, lengths)
    page_count = (lengths + PAGE - 1) // PAGE
    lent_count = jnp.where(is_long, page_count // 4, 0)
    run_start = jax.random.randint(run_key, (request_count,), 0, page_count - lent_count + 1)
    lender = rank_order[jnp.clip(positions - half_count, 0, half_count - 1)]
    slot_orders = jax.vmap(lambda subkey: jax.random.permutation(subkey, MAXP))(jax.random.split(slot_key, request_count))
    first_choice = slot_orders[:, 0:1]
    slot_orders = jnp.where(slot_orders == MAXP - 1, first_choice, slot_orders)
    slot_orders = slot_orders.at[:, 0].set(MAXP - 1)
    page_index = jnp.arange(MAXP, dtype=jnp.int32)[None, :]
    in_run = (page_index >= run_start[:, None]) & (page_index < (run_start + lent_count)[:, None])
    own_index = jnp.where(page_index < run_start[:, None], page_index, page_index - lent_count[:, None])
    lent_index = page_count[lender][:, None] + page_index - run_start[:, None]
    home_inst = jnp.arange(request_count, dtype=jnp.int32)[:, None]
    where_inst = jnp.where(in_run, lender[:, None], home_inst)
    occupant = jnp.clip(jnp.where(in_run, lent_index, own_index), 0, MAXP - 1)
    local_slot = slot_orders[where_inst, occupant]
    table = jnp.where(page_index < page_count[:, None], where_inst * MAXP + local_slot, -1)
    return (lengths.astype(jnp.int32), table.astype(jnp.int32))


def query_base(key):
    query_key = jax.random.fold_in(key, 202)
    return jax.random.truncated_normal(query_key, -6.0, 6.0, (REQS, STEPS, H * HD), jnp.float32)


def draw_lengths(key, part):
    shared = plan_tables(key)
    return shared[0]


def draw_page_table(key, part):
    shared = plan_tables(key)
    return shared[1]


def draw_queries(key, part):
    return query_base(key).astype(jnp.bfloat16)


def draw_key_pool(key, part):
    key = jax.random.fold_in(key, 5)
    entry_key = jax.random.fold_in(key, 0)
    pool_shape = (REQS * MAXP, PAGE, KVH * HD)
    entries = jax.random.truncated_normal(entry_key, -6.0, 6.0, pool_shape, jnp.float32)
    return entries.astype(jnp.bfloat16)


def steps_of(key, shape, cuts, low, top_value):
    loudness, own = 1.0, jax.random.fold_in(key, 6)
    for dim, parts in cuts:
        draws = jnp.exp(jax.random.uniform(jax.random.fold_in(own, dim), (parts,), jnp.float32, low / len(cuts), top_value / len(cuts)))
        loudness = loudness * jnp.repeat(draws, shape[dim] // parts).reshape([-1 if axis == dim else 1 for axis in range(len(shape))])
    return loudness


def normal_values(rng, extent, spread, most, cuts=(), kind=jnp.bfloat16):
    values = jax.random.normal(rng, extent, jnp.float32) * spread
    if len(cuts) > 0:
        values = steps_of(rng, extent, cuts, -0.22, 0.18) * values
    return jnp.clip(values, min=-most, max=most).astype(kind)


def setup_inputs(seed: int = 0) -> dict:
    splits = jax.random.split(jax.random.key(seed), 9)
    queries = draw_queries(jax.random.fold_in(splits[8], 71), 0)
    new_states = normal_values(splits[1], (REQS, STEPS, D), 4.0, 24.0, ((0, 32), (2, 8)))
    key_weight = normal_values(splits[2], (D, KVH * HD), D ** -0.5, 0.0625, ((1, 8),))
    value_weight = normal_values(splits[3], (D, KVH * HD), D ** -0.5, 0.0625, ((1, 8),))
    key_pool = draw_key_pool(jax.random.fold_in(splits[8], 71), 0)
    value_pool = normal_values(splits[5], (POOL, PAGE, KVH * HD), 1.0, 6.0, ((0, 32), (2, 8)))
    lengths = draw_lengths(jax.random.fold_in(splits[8], 71), 0)
    page_table = draw_page_table(jax.random.fold_in(splits[8], 71), 0)
    return dict(queries=queries, new_states=new_states, key_weight=key_weight, value_weight=value_weight, key_pool=key_pool, value_pool=value_pool, lengths=lengths, page_table=page_table)


negative_fill = -1e+30

def reference(queries, new_states, key_weight, value_weight, key_pool, value_pool, lengths, page_table):
    group_size = H // KVH
    score_scale = 1.0 / math.sqrt(HD)
    token_total = MAXP * PAGE

    def one_request(request):
        states = new_states[request]
        new_keys = jnp.dot(states, key_weight, preferred_element_type=jnp.float32).astype(jnp.bfloat16)
        new_values = jnp.dot(states, value_weight, preferred_element_type=jnp.float32).astype(jnp.bfloat16)
        new_keys = lax.optimization_barrier(new_keys).astype(jnp.float32).reshape(STEPS, KVH, HD)
        new_values = lax.optimization_barrier(new_values).astype(jnp.float32).reshape(STEPS, KVH, HD)
        page_ids = jnp.maximum(page_table[request], 0).astype(jnp.int32)
        context_keys = jnp.take(key_pool, page_ids, axis=0).reshape(token_total, KVH, HD).astype(jnp.float32)
        context_values = jnp.take(value_pool, page_ids, axis=0).reshape(token_total, KVH, HD).astype(jnp.float32)
        request_query = queries[request].reshape(STEPS, KVH, group_size, HD).astype(jnp.float32)
        cache_scores = jnp.einsum('skgd,pkd->kgsp', request_query, context_keys) * score_scale
        valid_mask = jnp.arange(token_total, dtype=jnp.int32) < lengths[request]
        cache_scores = jnp.where(valid_mask, cache_scores, negative_fill)
        new_scores = jnp.einsum('skgd,tkd->kgst', request_query, new_keys) * score_scale
        causal = jnp.arange(STEPS, dtype=jnp.int32)[None, :] <= jnp.arange(STEPS, dtype=jnp.int32)[:, None]
        new_scores = jnp.where(causal, new_scores, negative_fill)
        highest = jnp.maximum(cache_scores.max(axis=3), new_scores.max(axis=3))
        cache_weights = jnp.where(valid_mask, jnp.exp(cache_scores - highest[..., None]), 0.0)
        new_weights = jnp.where(causal, jnp.exp(new_scores - highest[..., None]), 0.0)
        weight_total = cache_weights.sum(axis=3) + new_weights.sum(axis=3)
        cache_rounded = lax.optimization_barrier(cache_weights.astype(jnp.bfloat16)).astype(jnp.float32)
        new_rounded = lax.optimization_barrier(new_weights.astype(jnp.bfloat16)).astype(jnp.float32)
        numerator = jnp.einsum('kgsp,pkd->kgsd', cache_rounded, context_values)
        numerator = numerator + jnp.einsum('kgst,tkd->kgsd', new_rounded, new_values)
        result = numerator / weight_total[..., None]
        return jnp.transpose(result, (2, 0, 1, 3)).reshape(STEPS, H * HD).astype(jnp.bfloat16)
    return lax.map(one_request, jnp.arange(REQS, dtype=jnp.int32))
```

```python
import math

import jax
import jax.numpy as jnp
from jax import lax
from jax.experimental import pallas as pl
from jax.experimental.pallas import tpu as pltpu
from jax.sharding import PartitionSpec as P

HD = 128
STEPS = 4
GROUP = 8
ROWS = STEPS * GROUP
PAGE = 256
SLOTS = 64
CHUNK = 8
CHUNKS = SLOTS // CHUNK
LENT = 16
NY = 4
NZ = 8
NT = 8
NEG = -1e30
LOG2E_SCALE = math.log2(math.e) / math.sqrt(HD)
F32 = jnp.float32
BF16 = jnp.bfloat16
MESH = pl.DeviceIdType.MESH
NT_DIMS = (((1,), (1,)), ((), ()))


def kernel(
    len_smem, tab_smem, tab_ref, q_hbm, st_hbm, kw_hbm, vw_hbm, k_hbm, v_hbm,
    out_ref,
    q_raw, st_raw, rows_f32, k_buf, v_buf, kw_buf, vw_buf, s_buf, bias_buf,
    st_all, q_z, q2_send, q2_recv, p_z, p2_send, p2_recv,
    small_sem, k_sem, v_sem, w_sem,
    st_send_sem, st_recv_sem, qz_send_sem, qz_recv_sem, q2_send_sem, q2_recv_sem,
    pz_send_sem, pz_recv_sem, p2_send_sem, p2_recv_sem,
):
    inst = lax.axis_index("inst")
    tensor = lax.axis_index("tensor")
    z = inst // NY
    y = inst % NY
    z_peer = [((z + d) % NZ) * NY + y for d in range(NZ)]
    y_peer = [z * NY + (y + e) % NY for e in range(NY)]
    t_peer = [(tensor + d) % NT for d in range(NT)]

    barrier = pltpu.get_barrier_semaphore()
    for d in range(1, NZ):
        pl.semaphore_signal(barrier, inc=1, device_id=(z_peer[d], tensor), device_id_type=MESH)
    for e in range(1, NY):
        pl.semaphore_signal(barrier, inc=1, device_id=(y_peer[e], tensor), device_id_type=MESH)
    for d in range(1, NT):
        pl.semaphore_signal(barrier, inc=1, device_id=(inst, t_peer[d]), device_id_type=MESH)

    q_copy = pltpu.make_async_copy(q_hbm, q_raw, small_sem.at[0])
    st_copy = pltpu.make_async_copy(st_hbm, st_raw, small_sem.at[1])
    q_copy.start()
    st_copy.start()

    def k_copy(c):
        part = pl.ds(c * CHUNK, CHUNK)
        return pltpu.make_async_copy(k_hbm.at[part], k_buf.at[part], k_sem.at[c])

    def v_copy(c):
        part = pl.ds(c * CHUNK, CHUNK)
        return pltpu.make_async_copy(v_hbm.at[part], v_buf.at[part], v_sem.at[c])

    for c in range(CHUNKS):
        k_copy(c).start()
    for c in range(CHUNKS):
        v_copy(c).start()
    w_copies = [
        pltpu.make_async_copy(kw_hbm, kw_buf, w_sem.at[0]),
        pltpu.make_async_copy(vw_hbm, vw_buf, w_sem.at[1]),
    ]
    for copy in w_copies:
        copy.start()

    def to_rows(raw):
        wide = raw[0].astype(F32)
        for g in range(GROUP):
            rows_f32[g * STEPS:(g + 1) * STEPS, :] = wide[:, g * HD:(g + 1) * HD]
        return rows_f32[...].astype(BF16)

    q_copy.wait()
    q_z[0] = to_rows(q_raw)
    st_copy.wait()
    st_all[0] = to_rows(st_raw)

    pl.semaphore_wait(barrier, NZ + NY + NT - 3)

    qz_copies = [
        pltpu.make_async_remote_copy(
            src_ref=q_z.at[0], dst_ref=q_z.at[d], send_sem=qz_send_sem.at[d], recv_sem=qz_recv_sem.at[d],
            device_id=(z_peer[d], tensor), device_id_type=MESH)
        for d in range(1, NZ)
    ]
    st_copies = [
        pltpu.make_async_remote_copy(
            src_ref=st_all.at[0], dst_ref=st_all.at[d], send_sem=st_send_sem.at[d], recv_sem=st_recv_sem.at[d],
            device_id=(inst, t_peer[d]), device_id_type=MESH)
        for d in range(1, NT)
    ]
    for copy in qz_copies + st_copies:
        copy.start()

    table = tab_ref[...]
    holder = table >> 6
    row_id = lax.broadcasted_iota(jnp.int32, table.shape, 0)
    page_id = lax.broadcasted_iota(jnp.int32, table.shape, 1)
    lent_code = jnp.where((table >= 0) & (holder != row_id), row_id * SLOTS + (SLOTS - 1) - page_id, -1)
    lent_holder = jnp.where((table >= 0) & (holder != row_id), holder, -1)
    guest_code = [jnp.max(jnp.where(holder == y_peer[e], lent_code, -1)) for e in range(NY)]
    lender = [jnp.max(jnp.where(row_id == y_peer[e], lent_holder, -1)) for e in range(NY)]

    own_length = len_smem[0, inst]
    own_row = jnp.broadcast_to(tab_ref[pl.ds(inst, 1), :] - inst * SLOTS, (SLOTS, SLOTS))
    slot_id = lax.broadcasted_iota(jnp.int32, (SLOTS, SLOTS), 0)
    page_of = lax.broadcasted_iota(jnp.int32, (SLOTS, SLOTS), 1)
    counted = jnp.clip(own_length - page_of * PAGE, 0, PAGE).astype(F32)
    valid = jnp.sum(jnp.where(own_row == slot_id, counted, 0.0), axis=1, keepdims=True)
    token = lax.broadcasted_iota(jnp.int32, (SLOTS, PAGE), 1).astype(F32)
    bias_buf[...] = jnp.where(token < valid, 0.0, NEG)

    query = q_z[0]

    def scores_chunk(c, top):
        k_copy(c).wait()
        for p in range(CHUNK):
            slot = c * CHUNK + p
            s = lax.dot_general(query, k_buf[slot], NT_DIMS, preferred_element_type=F32)
            s = s + bias_buf[pl.ds(slot, 1), :]
            s_buf[c, :, p * PAGE:(p + 1) * PAGE] = s
            top = jnp.maximum(top, jnp.maximum(s[:, :HD], s[:, HD:]))
        return top

    top = lax.fori_loop(0, CHUNKS, scores_chunk, jnp.full((ROWS, HD), NEG, F32))
    own_top = jnp.max(top, axis=1, keepdims=True) * LOG2E_SCALE

    for copy in qz_copies:
        copy.wait_recv()
    for e in range(NY):
        picked = q_z[(z - (guest_code[e] >> 8)) & (NZ - 1)]
        if e == 0:
            q2_recv[0] = picked
        else:
            q2_send[e] = picked
    q2_copies = [
        pltpu.make_async_remote_copy(
            src_ref=q2_send.at[e], dst_ref=q2_recv.at[e], send_sem=q2_send_sem.at[e], recv_sem=q2_recv_sem.at[e],
            device_id=(y_peer[e], tensor), device_id_type=MESH)
        for e in range(1, NY)
    ]
    for copy in q2_copies:
        copy.start()

    def lanes_sum(w):
        total = w[:, :HD]
        for b in range(1, w.shape[1] // HD):
            total = total + w[:, b * HD:(b + 1) * HD]
        return total

    def values_chunk(c, carry):
        total, numerator = carry
        v_copy(c).wait()
        half = CHUNK // 2
        for h in range(2):
            s = s_buf[c, :, h * half * PAGE:(h + 1) * half * PAGE]
            w = jnp.exp2(s * LOG2E_SCALE - own_top)
            total = total + lanes_sum(w)
            v = v_buf[pl.ds(c * CHUNK + h * half, half)].reshape(half * PAGE, HD)
            numerator = numerator + jnp.dot(w.astype(BF16), v, preferred_element_type=F32)
        return total, numerator

    total, own_out = lax.fori_loop(
        0, CHUNKS, values_chunk, (jnp.zeros((ROWS, HD), F32), jnp.zeros((ROWS, HD), F32)))
    own_total = jnp.sum(total, axis=1, keepdims=True)

    guest = guest_code[0] >> 6
    first_page = (SLOTS - 1) - (guest_code[0] & (SLOTS - 1))
    guest_row = jnp.maximum(guest, 0)
    guest_length = jnp.where(guest >= 0, len_smem[0, guest_row], 0)
    guest_pages = ((guest_length + PAGE - 1) // PAGE) // 4
    page_token = lax.broadcasted_iota(jnp.int32, (1, PAGE), 1)
    slots = []
    limits = []
    for i in range(LENT):
        page = jnp.minimum(first_page + i, SLOTS - 1)
        slots.append(jnp.clip(tab_smem[guest_row, page] - inst * SLOTS, 0, SLOTS - 1))
        limits.append(jnp.where(i < guest_pages, guest_length - page * PAGE, 0))

    for copy in q2_copies:
        copy.wait_recv()
    guest_query = q2_recv[(y - guest) & (NY - 1)]
    guest_top = jnp.full((ROWS, HD), NEG, F32)
    for i in range(LENT):
        s = lax.dot_general(guest_query, k_buf[slots[i]], NT_DIMS, preferred_element_type=F32)
        s = jnp.where(page_token < limits[i], s, NEG)
        s_buf[i // CHUNK, :, (i % CHUNK) * PAGE:(i % CHUNK + 1) * PAGE] = s
        guest_top = jnp.maximum(guest_top, jnp.maximum(s[:, :HD], s[:, HD:]))
    guest_top = jnp.max(guest_top, axis=1, keepdims=True) * LOG2E_SCALE
    total = jnp.zeros((ROWS, HD), F32)
    guest_out = jnp.zeros((ROWS, HD), F32)
    for i in range(LENT):
        s = s_buf[i // CHUNK, :, (i % CHUNK) * PAGE:(i % CHUNK + 1) * PAGE]
        w = jnp.exp2(s * LOG2E_SCALE - guest_top)
        total = total + lanes_sum(w)
        guest_out = guest_out + jnp.dot(w.astype(BF16), v_buf[slots[i]], preferred_element_type=F32)
    guest_total = jnp.sum(total, axis=1, keepdims=True)
    level = jnp.broadcast_to(guest_top + jnp.log2(guest_total), (ROWS, HD))
    lane = lax.broadcasted_iota(jnp.int32, (ROWS, HD), 1)
    high = level.astype(BF16).astype(F32)
    middle = (level - high).astype(BF16).astype(F32)
    low = level - high - middle
    place = lane & 63
    coded = jnp.where(place == 0, high, jnp.where(place == 1, middle, jnp.where(place == 2, low, 0.0)))
    half_rows = ROWS // 2
    coded = jnp.where(lane[:half_rows] < 64, coded[:half_rows], coded[half_rows:])
    p_z[0, :ROWS, :] = (guest_out / guest_total).astype(BF16)
    p_z[0, ROWS:, :] = coded.astype(BF16)
    pz_copies = [
        pltpu.make_async_remote_copy(
            src_ref=p_z.at[0], dst_ref=p_z.at[d], send_sem=pz_send_sem.at[d], recv_sem=pz_recv_sem.at[d],
            device_id=(z_peer[d], tensor), device_id_type=MESH)
        for d in range(1, NZ)
    ]
    for copy in pz_copies:
        copy.start()

    for copy in w_copies:
        copy.wait()
    for copy in st_copies:
        copy.wait_recv()
    row16 = lax.broadcasted_iota(jnp.int32, (16, HD), 0) // STEPS

    def project(d, acc):
        source = (tensor - d + NT) % NT
        for h in range(2):
            x = st_all[d, h * 16:(h + 1) * 16, :].astype(F32)
            left = jnp.concatenate([jnp.where(row16 == g, x, 0.0) for g in range(4)], axis=1).astype(BF16)
            weight = jnp.concatenate(
                [kw_buf[source, h * 512:(h + 1) * 512, :], vw_buf[source, h * 512:(h + 1) * 512, :]], axis=1)
            acc = acc + jnp.dot(left, weight, preferred_element_type=F32)
        return acc

    acc = lax.fori_loop(0, NT, project, jnp.zeros((16, 2 * HD), F32))
    acc = acc[:8] + acc[8:]
    acc = acc[:4] + acc[4:]
    padded = jnp.concatenate([acc, jnp.zeros((12, 2 * HD), F32)], axis=0).astype(BF16)
    new_keys = padded[:, :HD]
    new_values = padded[:, HD:]
    s = lax.dot_general(query, new_keys, NT_DIMS, preferred_element_type=F32)
    step = lax.broadcasted_iota(jnp.int32, (ROWS, 16), 0) % STEPS
    other = lax.broadcasted_iota(jnp.int32, (ROWS, 16), 1)
    s = jnp.where(other <= step, s * LOG2E_SCALE, NEG)
    merged_top = jnp.maximum(own_top, jnp.max(s, axis=1, keepdims=True))
    w = jnp.exp2(s - merged_top)
    kept = jnp.exp2(own_top - merged_top)
    merged_total = own_total * kept + jnp.sum(w, axis=1, keepdims=True)
    merged_out = own_out * kept + jnp.dot(w.astype(BF16), new_values, preferred_element_type=F32)

    for copy in pz_copies:
        copy.wait_recv()
    for e in range(NY):
        picked = p_z[(z - (lender[e] >> 2)) & (NZ - 1)]
        if e == 0:
            p2_recv[0] = picked
        else:
            p2_send[e] = picked
    p2_copies = [
        pltpu.make_async_remote_copy(
            src_ref=p2_send.at[e], dst_ref=p2_recv.at[e], send_sem=p2_send_sem.at[e], recv_sem=p2_recv_sem.at[e],
            device_id=(y_peer[e], tensor), device_id_type=MESH)
        for e in range(1, NY)
    ]
    for copy in p2_copies:
        copy.start()
    for copy in p2_copies:
        copy.wait_recv()
    lent = p2_recv[(y - lender[0]) & (NY - 1)].astype(F32)
    coded = lent[ROWS:]
    lane16 = lane[:half_rows]
    level = jnp.concatenate([
        jnp.sum(jnp.where(lane16 < 64, coded, 0.0), axis=1, keepdims=True),
        jnp.sum(jnp.where(lane16 < 64, 0.0, coded), axis=1, keepdims=True)], axis=0)
    level = jnp.where(lender[0] >= 0, level, NEG)
    highest = jnp.maximum(merged_top, level)
    kept = jnp.exp2(merged_top - highest)
    added = jnp.exp2(level - highest)
    out_ref[...] = (merged_out * kept + lent[:ROWS] * added) / (merged_total * kept + added)

    for copy in qz_copies + st_copies + q2_copies + pz_copies + p2_copies:
        copy.wait_send()


def on_device(queries, new_states, key_weight, value_weight, key_pool, value_pool, lengths, page_table):
    hbm = pl.BlockSpec(memory_space=pltpu.HBM)
    dma = pltpu.SemaphoreType.DMA
    out = pl.pallas_call(
        kernel,
        out_shape=jax.ShapeDtypeStruct((ROWS, HD), F32),
        in_specs=[
            pl.BlockSpec(memory_space=pltpu.SMEM),
            pl.BlockSpec(memory_space=pltpu.SMEM),
            pl.BlockSpec(memory_space=pltpu.VMEM),
            hbm, hbm, hbm, hbm, hbm, hbm,
        ],
        out_specs=pl.BlockSpec(memory_space=pltpu.VMEM),
        scratch_shapes=[
            pltpu.VMEM((1, STEPS, GROUP * HD), BF16),
            pltpu.VMEM((1, STEPS, GROUP * HD), BF16),
            pltpu.VMEM((ROWS, HD), F32),
            pltpu.VMEM((SLOTS, PAGE, HD), BF16),
            pltpu.VMEM((SLOTS, PAGE, HD), BF16),
            pltpu.VMEM((NT, GROUP * HD, HD), BF16),
            pltpu.VMEM((NT, GROUP * HD, HD), BF16),
            pltpu.VMEM((CHUNKS, ROWS, CHUNK * PAGE), F32),
            pltpu.VMEM((SLOTS, PAGE), F32),
            pltpu.VMEM((NT, ROWS, HD), BF16),
            pltpu.VMEM((NZ, ROWS, HD), BF16),
            pltpu.VMEM((NY, ROWS, HD), BF16),
            pltpu.VMEM((NY, ROWS, HD), BF16),
            pltpu.VMEM((NZ, ROWS + 16, HD), BF16),
            pltpu.VMEM((NY, ROWS + 16, HD), BF16),
            pltpu.VMEM((NY, ROWS + 16, HD), BF16),
            dma((2,)), dma((CHUNKS,)), dma((CHUNKS,)), dma((2,)),
            dma((NT,)), dma((NT,)), dma((NZ,)), dma((NZ,)), dma((NY,)), dma((NY,)),
            dma((NZ,)), dma((NZ,)), dma((NY,)), dma((NY,)),
        ],
        compiler_params=pltpu.CompilerParams(
            collective_id=0, has_side_effects=True, vmem_limit_bytes=48 * 1024 * 1024),
    )(
        lengths.reshape(1, -1), page_table, page_table, queries, new_states,
        key_weight.reshape(NT, GROUP * HD, HD), value_weight.reshape(NT, GROUP * HD, HD),
        key_pool, value_pool,
    )
    return (
        jnp.transpose(out.reshape(GROUP, STEPS, HD), (1, 0, 2))
        .reshape(1, STEPS, GROUP * HD)
        .astype(BF16)
    )


def solution(mesh):
    placed = (
        P("inst", None, "tensor"),
        P("inst", None, "tensor"),
        P(None, "tensor"),
        P(None, "tensor"),
        P("inst", None, "tensor"),
        P("inst", None, "tensor"),
        P(),
        P(),
    )
    return jax.shard_map(
        on_device, mesh=mesh, in_specs=placed, out_specs=P("inst", None, "tensor"), check_vma=False
    )
```

```python
import math

import jax
import jax.numpy as jnp
from jax import lax
from jax.experimental import pallas as pl
from jax.experimental.pallas import tpu as pltpu
from jax.sharding import PartitionSpec as P

HD = 128
STEPS = 4
GROUP = 8
ROWS = STEPS * GROUP
PAGE = 256
SLOTS = 64
CHUNK = 8
CHUNKS = SLOTS // CHUNK
LENT = 16
NY = 4
NZ = 8
NT = 8
NEG = -1e30
VMEM_BYTES = 60 * 1024 * 1024
Z_ORDER = (4, 3, 5, 2, 6, 1, 7)
Y_ORDER = (2, 1, 3)
T_ORDER = (4, 5, 3, 2, 6, 7, 1)
LOG2E_SCALE = math.log2(math.e) / math.sqrt(HD)
F32 = jnp.float32
BF16 = jnp.bfloat16
MESH = pl.DeviceIdType.MESH
NT_DIMS = (((1,), (1,)), ((), ()))


def kernel(
    len_hbm, tab_hbm, q_hbm, st_hbm, kw_hbm, vw_hbm, k_hbm, v_hbm,
    out_ref,
    len_smem, tab_smem, tab_ref, k_buf, v_buf, kw_buf, vw_buf, s_buf, guest_buf, bias_buf,
    st_all, q_z, q2_send, q2_recv, p_z, p2_send, p2_recv,
    small_sem, k_sem, v_sem, w_sem,
    st_send_sem, st_recv_sem, qz_send_sem, qz_recv_sem, q2_send_sem, q2_recv_sem,
    pz_send_sem, pz_recv_sem, p2_send_sem, p2_recv_sem,
):
    inst = lax.axis_index("inst")
    tensor = lax.axis_index("tensor")
    z = inst // NY
    y = inst % NY
    z_peer = [((z + d) % NZ) * NY + y for d in range(NZ)]
    y_peer = [z * NY + (y + e) % NY for e in range(NY)]
    t_peer = [(tensor + d) % NT for d in range(NT)]

    barrier = pltpu.get_barrier_semaphore()
    for d in Z_ORDER:
        pl.semaphore_signal(barrier, inc=1, device_id=(z_peer[d], tensor), device_id_type=MESH)
    for e in Y_ORDER:
        pl.semaphore_signal(barrier, inc=1, device_id=(y_peer[e], tensor), device_id_type=MESH)
    for d in T_ORDER:
        pl.semaphore_signal(barrier, inc=1, device_id=(inst, t_peer[d]), device_id_type=MESH)

    small_copies = [
        pltpu.make_async_copy(tab_hbm, tab_ref, small_sem.at[0]),
        pltpu.make_async_copy(q_hbm, q_z.at[0], small_sem.at[1]),
        pltpu.make_async_copy(st_hbm, st_all.at[0], small_sem.at[2]),
        pltpu.make_async_copy(len_hbm, len_smem, small_sem.at[3]),
        pltpu.make_async_copy(tab_hbm, tab_smem, small_sem.at[4]),
    ]
    for copy in small_copies:
        copy.start()

    def k_copy(c):
        part = pl.ds(c * CHUNK, CHUNK)
        return pltpu.make_async_copy(k_hbm.at[part], k_buf.at[part], k_sem.at[c])

    def v_copy(c):
        part = pl.ds(c * CHUNK, CHUNK)
        return pltpu.make_async_copy(v_hbm.at[part], v_buf.at[part], v_sem.at[c])

    for c in range(CHUNKS):
        k_copy(c).start()
    for c in range(CHUNKS):
        v_copy(c).start()
    w_copies = [
        pltpu.make_async_copy(kw_hbm, kw_buf, w_sem.at[0]),
        pltpu.make_async_copy(vw_hbm, vw_buf, w_sem.at[1]),
    ]
    for copy in w_copies:
        copy.start()

    small_copies[1].wait()
    small_copies[2].wait()
    pl.semaphore_wait(barrier, NZ + NY + NT - 3)

    qz_copies = [
        pltpu.make_async_remote_copy(
            src_ref=q_z.at[0], dst_ref=q_z.at[d], send_sem=qz_send_sem.at[d], recv_sem=qz_recv_sem.at[d],
            device_id=(z_peer[d], tensor), device_id_type=MESH)
        for d in Z_ORDER
    ]
    st_copies = [
        pltpu.make_async_remote_copy(
            src_ref=st_all.at[0], dst_ref=st_all.at[d], send_sem=st_send_sem.at[d], recv_sem=st_recv_sem.at[d],
            device_id=(inst, t_peer[d]), device_id_type=MESH)
        for d in T_ORDER
    ]
    for copy in qz_copies + st_copies:
        copy.start()

    small_copies[0].wait()
    small_copies[3].wait()
    small_copies[4].wait()
    table = tab_ref[...]
    holder = table >> 6
    row_id = lax.broadcasted_iota(jnp.int32, table.shape, 0)
    page_id = lax.broadcasted_iota(jnp.int32, table.shape, 1)
    lent = (table >= 0) & (holder != row_id)
    lent_code = jnp.where(lent, row_id * SLOTS + (SLOTS - 1) - page_id, -1)
    lent_holder = jnp.where(lent, holder, -1)
    guest_code = [jnp.max(jnp.where(holder == y_peer[e], lent_code, -1)) for e in range(NY)]
    lender = [jnp.max(jnp.where(row_id == y_peer[e], lent_holder, -1)) for e in range(NY)]

    own_length = len_smem[0, inst]
    own_row = jnp.broadcast_to(tab_ref[pl.ds(inst, 1), :] - inst * SLOTS, (SLOTS, SLOTS))
    slot_id = lax.broadcasted_iota(jnp.int32, (SLOTS, SLOTS), 0)
    page_of = lax.broadcasted_iota(jnp.int32, (SLOTS, SLOTS), 1)
    counted = jnp.clip(own_length - page_of * PAGE, 0, PAGE).astype(F32)
    valid = jnp.sum(jnp.where(own_row == slot_id, counted, 0.0), axis=1, keepdims=True)
    token = lax.broadcasted_iota(jnp.int32, (SLOTS, PAGE), 1).astype(F32)
    bias_buf[...] = jnp.where(token < valid, 0.0, NEG)

    guest = guest_code[0] >> 6
    first_page = (SLOTS - 1) - (guest_code[0] & (SLOTS - 1))
    guest_row = jnp.maximum(guest, 0)
    guest_length = jnp.where(guest >= 0, len_smem[0, guest_row], 0)
    guest_pages = ((guest_length + PAGE - 1) // PAGE) // 4
    page_token = lax.broadcasted_iota(jnp.int32, (1, PAGE), 1)
    slots = []
    limits = []
    for i in range(LENT):
        page = jnp.minimum(first_page + i, SLOTS - 1)
        slots.append(jnp.clip(tab_smem[guest_row, page] - inst * SLOTS, 0, SLOTS - 1))
        limits.append(jnp.where(i < guest_pages, guest_length - page * PAGE, 0))

    query = q_z[0]

    def scores_chunk(c, top):
        k_copy(c).wait()
        for p in range(CHUNK):
            slot = c * CHUNK + p
            s = lax.dot_general(query, k_buf[slot], NT_DIMS, preferred_element_type=F32)
            s = s + bias_buf[pl.ds(slot, 1), :]
            s_buf[c, :, p * PAGE:(p + 1) * PAGE] = s
            top = jnp.maximum(top, jnp.maximum(s[:, :HD], s[:, HD:]))
        return top

    def lanes_sum(w):
        total = w[:, :HD]
        for b in range(1, w.shape[1] // HD):
            total = total + w[:, b * HD:(b + 1) * HD]
        return total

    def values_chunk(c, carry):
        total, numerator = carry
        v_copy(c).wait()
        half = CHUNK // 2
        for h in range(2):
            s = s_buf[c, :, h * half * PAGE:(h + 1) * half * PAGE]
            w = jnp.exp2(s * LOG2E_SCALE - own_top)
            total = total + lanes_sum(w)
            v = v_buf[pl.ds(c * CHUNK + h * half, half)].reshape(half * PAGE, HD)
            numerator = numerator + jnp.dot(w.astype(BF16), v, preferred_element_type=F32)
        return total, numerator

    top = jnp.full((ROWS, HD), NEG, F32)
    top = lax.fori_loop(0, CHUNKS, scores_chunk, top)

    for copy in qz_copies:
        copy.wait_recv()
    q2_copies = []
    for e in Y_ORDER + (0,):
        picked = q_z[(z - (guest_code[e] >> 8)) & (NZ - 1)]
        if e == 0:
            q2_recv[0] = picked
        else:
            q2_send[e] = picked
            copy = pltpu.make_async_remote_copy(
                src_ref=q2_send.at[e], dst_ref=q2_recv.at[e], send_sem=q2_send_sem.at[e], recv_sem=q2_recv_sem.at[e],
                device_id=(y_peer[e], tensor), device_id_type=MESH)
            copy.start()
            q2_copies.append(copy)

    own_top = jnp.max(top, axis=1, keepdims=True) * LOG2E_SCALE

    carry = (jnp.zeros((ROWS, HD), F32), jnp.zeros((ROWS, HD), F32))
    carry = lax.fori_loop(0, CHUNKS, values_chunk, carry)
    total, own_out = carry
    own_total = jnp.sum(total, axis=1, keepdims=True)

    for copy in q2_copies:
        copy.wait_recv()
    guest_query = q2_recv[(y - guest) & (NY - 1)]
    guest_top = jnp.full((ROWS, HD), NEG, F32)
    for i in range(LENT):
        s = lax.dot_general(guest_query, k_buf[slots[i]], NT_DIMS, preferred_element_type=F32)
        s = jnp.where(page_token < limits[i], s, NEG)
        guest_buf[:, i * PAGE:(i + 1) * PAGE] = s
        guest_top = jnp.maximum(guest_top, jnp.maximum(s[:, :HD], s[:, HD:]))
    guest_top = jnp.max(guest_top, axis=1, keepdims=True) * LOG2E_SCALE
    total = jnp.zeros((ROWS, HD), F32)
    guest_out = jnp.zeros((ROWS, HD), F32)
    for i in range(LENT):
        s = guest_buf[:, i * PAGE:(i + 1) * PAGE]
        w = jnp.exp2(s * LOG2E_SCALE - guest_top)
        total = total + lanes_sum(w)
        guest_out = guest_out + jnp.dot(w.astype(BF16), v_buf[slots[i]], preferred_element_type=F32)
    guest_total = jnp.sum(total, axis=1, keepdims=True)
    level = jnp.broadcast_to(guest_top + jnp.log2(guest_total), (ROWS, HD))
    lane = lax.broadcasted_iota(jnp.int32, (ROWS, HD), 1)
    high = level.astype(BF16).astype(F32)
    middle = (level - high).astype(BF16).astype(F32)
    low = level - high - middle
    place = lane & 63
    coded = jnp.where(place == 0, high, jnp.where(place == 1, middle, jnp.where(place == 2, low, 0.0)))
    half_rows = ROWS // 2
    coded = jnp.where(lane[:half_rows] < 64, coded[:half_rows], coded[half_rows:])
    p_z[0, :ROWS, :] = (guest_out / guest_total).astype(BF16)
    p_z[0, ROWS:, :] = coded.astype(BF16)
    pz_copies = [
        pltpu.make_async_remote_copy(
            src_ref=p_z.at[0], dst_ref=p_z.at[d], send_sem=pz_send_sem.at[d], recv_sem=pz_recv_sem.at[d],
            device_id=(z_peer[d], tensor), device_id_type=MESH)
        for d in Z_ORDER
    ]
    for copy in pz_copies:
        copy.start()

    for copy in w_copies:
        copy.wait()
    for copy in st_copies:
        copy.wait_recv()
    row16 = lax.broadcasted_iota(jnp.int32, (16, HD), 0) // STEPS

    def project(d, acc):
        source = (tensor - d + NT) % NT
        for h in range(2):
            x = st_all[d, h * 16:(h + 1) * 16, :].astype(F32)
            left = jnp.concatenate([jnp.where(row16 == g, x, 0.0) for g in range(4)], axis=1).astype(BF16)
            weight = jnp.concatenate(
                [kw_buf[source, h * 512:(h + 1) * 512, :], vw_buf[source, h * 512:(h + 1) * 512, :]], axis=1)
            acc = acc + jnp.dot(left, weight, preferred_element_type=F32)
        return acc

    acc = lax.fori_loop(0, NT, project, jnp.zeros((16, 2 * HD), F32))
    acc = acc[:8] + acc[8:]
    acc = acc[:4] + acc[4:]
    padded = jnp.concatenate([acc, jnp.zeros((12, 2 * HD), F32)], axis=0).astype(BF16)
    new_keys = padded[:, :HD]
    new_values = padded[:, HD:]
    s = lax.dot_general(query, new_keys, NT_DIMS, preferred_element_type=F32)
    step = lax.broadcasted_iota(jnp.int32, (ROWS, 16), 0) % STEPS
    other = lax.broadcasted_iota(jnp.int32, (ROWS, 16), 1)
    s = jnp.where(other <= step, s * LOG2E_SCALE, NEG)
    merged_top = jnp.maximum(own_top, jnp.max(s, axis=1, keepdims=True))
    w = jnp.exp2(s - merged_top)
    kept = jnp.exp2(own_top - merged_top)
    merged_total = own_total * kept + jnp.sum(w, axis=1, keepdims=True)
    merged_out = own_out * kept + jnp.dot(w.astype(BF16), new_values, preferred_element_type=F32)

    for copy in pz_copies:
        copy.wait_recv()
    p2_copies = []
    for e in Y_ORDER + (0,):
        picked = p_z[(z - (lender[e] >> 2)) & (NZ - 1)]
        if e == 0:
            p2_recv[0] = picked
        else:
            p2_send[e] = picked
            copy = pltpu.make_async_remote_copy(
                src_ref=p2_send.at[e], dst_ref=p2_recv.at[e], send_sem=p2_send_sem.at[e], recv_sem=p2_recv_sem.at[e],
                device_id=(y_peer[e], tensor), device_id_type=MESH)
            copy.start()
            p2_copies.append(copy)

    for copy in p2_copies:
        copy.wait_recv()
    lent_part = p2_recv[(y - lender[0]) & (NY - 1)].astype(F32)
    coded = lent_part[ROWS:]
    lane16 = lane[:half_rows]
    level = jnp.concatenate([
        jnp.sum(jnp.where(lane16 < 64, coded, 0.0), axis=1, keepdims=True),
        jnp.sum(jnp.where(lane16 < 64, 0.0, coded), axis=1, keepdims=True)], axis=0)
    level = jnp.where(lender[0] >= 0, level, NEG)
    highest = jnp.maximum(merged_top, level)
    kept = jnp.exp2(merged_top - highest)
    added = jnp.exp2(level - highest)
    out_ref[...] = ((merged_out * kept + lent_part[:ROWS] * added) / (merged_total * kept + added)).astype(out_ref.dtype)

    for copy in qz_copies + st_copies + q2_copies + pz_copies + p2_copies:
        copy.wait_send()


def on_device(queries, new_states, key_weight, value_weight, key_pool, value_pool, lengths, page_table):
    hbm = pl.BlockSpec(memory_space=pltpu.HBM)
    dma = pltpu.SemaphoreType.DMA

    def rows_of(x):
        return jnp.transpose(x.reshape(STEPS, GROUP, HD), (1, 0, 2)).reshape(ROWS, HD)

    out = pl.pallas_call(
        kernel,
        out_shape=pltpu.VMEM((ROWS, HD), F32),
        in_specs=[hbm] * 8,
        out_specs=pl.BlockSpec(memory_space=pltpu.VMEM),
        scratch_shapes=[
            pltpu.SMEM((1, 32), jnp.int32),
            pltpu.SMEM((32, SLOTS), jnp.int32),
            pltpu.VMEM((32, SLOTS), jnp.int32),
            pltpu.VMEM((SLOTS, PAGE, HD), BF16),
            pltpu.VMEM((SLOTS, PAGE, HD), BF16),
            pltpu.VMEM((NT, GROUP * HD, HD), BF16),
            pltpu.VMEM((NT, GROUP * HD, HD), BF16),
            pltpu.VMEM((CHUNKS, ROWS, CHUNK * PAGE), F32),
            pltpu.VMEM((ROWS, LENT * PAGE), F32),
            pltpu.VMEM((SLOTS, PAGE), F32),
            pltpu.VMEM((NT, ROWS, HD), BF16),
            pltpu.VMEM((NZ, ROWS, HD), BF16),
            pltpu.VMEM((NY, ROWS, HD), BF16),
            pltpu.VMEM((NY, ROWS, HD), BF16),
            pltpu.VMEM((NZ, ROWS + 16, HD), BF16),
            pltpu.VMEM((NY, ROWS + 16, HD), BF16),
            pltpu.VMEM((NY, ROWS + 16, HD), BF16),
            dma((5,)), dma((CHUNKS,)), dma((CHUNKS,)), dma((2,)),
            dma((NT,)), dma((NT,)), dma((NZ,)), dma((NZ,)), dma((NY,)), dma((NY,)),
            dma((NZ,)), dma((NZ,)), dma((NY,)), dma((NY,)),
        ],
        compiler_params=pltpu.CompilerParams(
            collective_id=0, has_side_effects=True, vmem_limit_bytes=VMEM_BYTES),
    )(
        lengths.reshape(1, -1), page_table, rows_of(queries), rows_of(new_states),
        key_weight.reshape(NT, GROUP * HD, HD), value_weight.reshape(NT, GROUP * HD, HD),
        key_pool, value_pool,
    )
    return (
        jnp.transpose(out.reshape(GROUP, STEPS, HD), (1, 0, 2))
        .reshape(1, STEPS, GROUP * HD)
        .astype(BF16)
    )


def solution(mesh):
    placed = (
        P("inst", None, "tensor"),
        P("inst", None, "tensor"),
        P(None, "tensor"),
        P(None, "tensor"),
        P("inst", None, "tensor"),
        P("inst", None, "tensor"),
        P(),
        P(),
    )
    return jax.shard_map(
        on_device, mesh=mesh, in_specs=placed, out_specs=P("inst", None, "tensor"), check_vma=False
    )
```

```python
import math

import jax
import jax.numpy as jnp
from jax import lax
from jax.experimental import pallas as pl
from jax.experimental.pallas import tpu as pltpu
from jax.sharding import PartitionSpec as P

HD = 128
STEPS = 4
GROUP = 8
ROWS = STEPS * GROUP
PAGE = 256
SLOTS = 64
CHUNK = 8
CHUNKS = SLOTS // CHUNK
PARTS = 4
PART = SLOTS // PARTS
LENT = 16
NY = 4
NZ = 8
NT = 8
NEG = -1e30
VMEM_BYTES = 60 * 1024 * 1024
Z_ORDER = (4, 3, 5, 2, 6, 1, 7)
Y_ORDER = (2, 1, 3)
T_ORDER = (4, 5, 3, 2, 6, 7, 1)
LOG2E_SCALE = math.log2(math.e) / math.sqrt(HD)
F32 = jnp.float32
BF16 = jnp.bfloat16
MESH = pl.DeviceIdType.MESH
NT_DIMS = (((1,), (1,)), ((), ()))


def remote_copy(src, dst, send_sem, recv_sem, target):
    return pltpu.make_async_remote_copy(
        src_ref=src, dst_ref=dst, send_sem=send_sem, recv_sem=recv_sem, device_id=target, device_id_type=MESH)


def lanes_sum(w):
    total = w[:, :HD]
    for b in range(1, w.shape[1] // HD):
        total = total + w[:, b * HD:(b + 1) * HD]
    return total


def kernel(
    len_hbm, tab_hbm, q_hbm, st_hbm, kw_hbm, vw_hbm, k_hbm, v_hbm,
    out_ref,
    len_smem, tab_smem, tab_ref, k_buf, v_buf, kw_buf, vw_buf, s_buf, guest_buf, bias_buf,
    st_all, q_own, q_relay_even, q_relay_odd, q_send, q_recv, p_own, p_relay_even, p_relay_odd, p_send, p_recv,
    small_sem, k_sem, v_sem, w_sem, st_send_sem, st_recv_sem,
    q1_send_sem, q1_recv_sem, q2_send_sem, q2_recv_sem,
    p1_send_sem, p1_recv_sem, p2_send_sem, p2_recv_sem,
):
    inst = lax.axis_index("inst")
    tensor = lax.axis_index("tensor")
    z = inst // NY
    y = inst % NY
    odd = tensor % 2
    even_t = tensor - odd
    odd_t = even_t + 1
    is_relay = odd == 1
    z_peer = [((z + d) % NZ) * NY + y for d in range(NZ)]
    y_peer = [z * NY + (y + e) % NY for e in range(NY)]
    t_peer = [(tensor + d) % NT for d in range(NT)]

    barrier = pltpu.get_barrier_semaphore()

    @pl.when(is_relay)
    def _():
        for d in Z_ORDER:
            pl.semaphore_signal(barrier, inc=1, device_id=(z_peer[d], even_t), device_id_type=MESH)
            pl.semaphore_signal(barrier, inc=1, device_id=(z_peer[d], odd_t), device_id_type=MESH)

    for e in Y_ORDER:
        pl.semaphore_signal(barrier, inc=1, device_id=(y_peer[e], odd_t), device_id_type=MESH)
    for d in T_ORDER:
        pl.semaphore_signal(barrier, inc=1, device_id=(inst, t_peer[d]), device_id_type=MESH)

    small_copies = [
        pltpu.make_async_copy(q_hbm, q_own, small_sem.at[0]),
        pltpu.make_async_copy(st_hbm, st_all.at[0], small_sem.at[1]),
        pltpu.make_async_copy(tab_hbm, tab_ref, small_sem.at[2]),
        pltpu.make_async_copy(len_hbm, len_smem, small_sem.at[3]),
        pltpu.make_async_copy(tab_hbm, tab_smem, small_sem.at[4]),
    ]
    for copy in small_copies:
        copy.start()

    def k_copy(c):
        part = pl.ds(c * PART, PART)
        return pltpu.make_async_copy(k_hbm.at[part], k_buf.at[part], k_sem.at[c])

    def v_copy(c):
        part = pl.ds(c * PART, PART)
        return pltpu.make_async_copy(v_hbm.at[part], v_buf.at[part], v_sem.at[c])

    w_copies = [
        pltpu.make_async_copy(kw_hbm, kw_buf, w_sem.at[0]),
        pltpu.make_async_copy(vw_hbm, vw_buf, w_sem.at[1]),
    ]
    for c in range(PARTS):
        k_copy(c).start()
    for c in range(PARTS):
        v_copy(c).start()
    for copy in w_copies:
        copy.start()

    small_copies[0].wait()
    small_copies[1].wait()
    query = q_own[...]
    q_relay_odd[0] = query
    pl.semaphore_wait(barrier, NZ + NT - 2 + (NY + NY - 2) * odd)

    def relay_copy(own, relay, d, p, send_sem, recv_sem):
        return remote_copy(own, relay[p].at[d], send_sem.at[d], recv_sem.at[p, d], (z_peer[d], odd_t))

    def to_relays(own, relay, send_sem, recv_sem):
        @pl.when(is_relay)
        def _():
            for d in Z_ORDER:
                relay_copy(own, relay, d, 1, send_sem, recv_sem).start()

        @pl.when(jnp.logical_not(is_relay))
        def _():
            for d in Z_ORDER + (0,):
                relay_copy(own, relay, d, 0, send_sem, recv_sem).start()

    def to_relays_done(own, relay, send_sem, recv_sem):
        for d in Z_ORDER:
            relay_copy(own, relay, d, 0, send_sem, recv_sem).wait_send()

        @pl.when(jnp.logical_not(is_relay))
        def _():
            relay_copy(own, relay, 0, 0, send_sem, recv_sem).wait_send()

    def relayed(relay, source, sent, received, arrive_sem, send_sem, recv_sem):
        @pl.when(is_relay)
        def _():
            for p in (1, 0):
                for d in Z_ORDER + (0,) * (1 - p):
                    relay_copy(sent.at[p, 0], relay, d, p, arrive_sem.at[p], arrive_sem).wait_recv()
                for e in Y_ORDER + (0,):
                    picked = relay[p][source[e]]
                    if p == 1 and e == 0:
                        received[0] = picked
                    else:
                        sent[p, e] = picked
                        remote_copy(
                            sent.at[p, e], received.at[e], send_sem.at[p, e], recv_sem.at[e], (y_peer[e], even_t + p)
                        ).start()

    def relay_done(sent, received, send_sem, recv_sem):
        for p in range(2):
            for e in Y_ORDER + (0,) * (1 - p):
                remote_copy(
                    sent.at[p, e], received.at[e], send_sem.at[p, e], recv_sem.at[e], (y_peer[e], even_t + p)
                ).wait_send()

    def arrived(received, recv_sem):
        for e in Y_ORDER:
            remote_copy(
                received.at[e], received.at[e], recv_sem.at[e], recv_sem.at[e], (y_peer[e], odd_t)
            ).wait_recv()

        @pl.when(jnp.logical_not(is_relay))
        def _():
            remote_copy(
                received.at[0], received.at[0], recv_sem.at[0], recv_sem.at[0], (inst, odd_t)
            ).wait_recv()

    q_relay = (q_relay_even, q_relay_odd)
    to_relays(q_own, q_relay, q1_send_sem, q1_recv_sem)
    st_copies = [
        remote_copy(st_all.at[0], st_all.at[d], st_send_sem.at[d], st_recv_sem.at[d], (inst, t_peer[d]))
        for d in T_ORDER
    ]
    for copy in st_copies:
        copy.start()

    for copy in small_copies[2:]:
        copy.wait()
    table = tab_ref[...]
    holder = table >> 6
    row_id = lax.broadcasted_iota(jnp.int32, table.shape, 0)
    page_id = lax.broadcasted_iota(jnp.int32, table.shape, 1)
    lent = (table >= 0) & (holder != row_id)
    lent_code = jnp.where(lent, row_id * SLOTS + (SLOTS - 1) - page_id, -1)
    lent_holder = jnp.where(lent, holder, -1)
    guest_code = [jnp.max(jnp.where(holder == y_peer[e], lent_code, -1)) for e in range(NY)]
    lender = [jnp.max(jnp.where(row_id == y_peer[e], lent_holder, -1)) for e in range(NY)]

    own_length = len_smem[0, inst]
    own_row = jnp.broadcast_to(tab_ref[pl.ds(inst, 1), :] - inst * SLOTS, (SLOTS, SLOTS))
    slot_id = lax.broadcasted_iota(jnp.int32, (SLOTS, SLOTS), 0)
    page_of = lax.broadcasted_iota(jnp.int32, (SLOTS, SLOTS), 1)
    counted = jnp.clip(own_length - page_of * PAGE, 0, PAGE).astype(F32)
    valid = jnp.sum(jnp.where(own_row == slot_id, counted, 0.0), axis=1, keepdims=True)
    token = lax.broadcasted_iota(jnp.int32, (SLOTS, PAGE), 1).astype(F32)
    bias_buf[...] = jnp.where(token < valid, 0.0, NEG)

    guest = guest_code[0] >> 6
    first_page = (SLOTS - 1) - (guest_code[0] & (SLOTS - 1))
    guest_row = jnp.maximum(guest, 0)
    guest_length = jnp.where(guest >= 0, len_smem[0, guest_row], 0)
    guest_pages = ((guest_length + PAGE - 1) // PAGE) // 4
    page_token = lax.broadcasted_iota(jnp.int32, (1, PAGE), 1)
    slots = []
    limits = []
    for i in range(LENT):
        page = jnp.minimum(first_page + i, SLOTS - 1)
        slots.append(jnp.clip(tab_smem[guest_row, page] - inst * SLOTS, 0, SLOTS - 1))
        limits.append(jnp.where(i < guest_pages, guest_length - page * PAGE, 0))

    def scores_chunk(c, top):
        for p in range(CHUNK):
            slot = c * CHUNK + p
            s = lax.dot_general(query, k_buf[slot], NT_DIMS, preferred_element_type=F32)
            s = s + bias_buf[pl.ds(slot, 1), :]
            s_buf[c, :, p * PAGE:(p + 1) * PAGE] = s
            top = jnp.maximum(top, jnp.maximum(s[:, :HD], s[:, HD:]))
        return top

    def values_chunk(c, carry):
        total, numerator = carry
        half = CHUNK // 2
        for h in range(2):
            s = s_buf[c, :, h * half * PAGE:(h + 1) * half * PAGE]
            w = jnp.exp2(s * LOG2E_SCALE - own_top)
            total = total + lanes_sum(w)
            v = v_buf[pl.ds(c * CHUNK + h * half, half)].reshape(half * PAGE, HD)
            numerator = numerator + jnp.dot(w.astype(BF16), v, preferred_element_type=F32)
        return total, numerator

    per_part = CHUNKS // PARTS
    top = jnp.full((ROWS, HD), NEG, F32)
    for c in range(PARTS):
        k_copy(c).wait()
        top = lax.fori_loop(c * per_part, (c + 1) * per_part, scores_chunk, top)
    own_top = jnp.max(top, axis=1, keepdims=True) * LOG2E_SCALE

    relayed(
        q_relay, [(z - (guest_code[e] >> 8)) & (NZ - 1) for e in range(NY)], q_send, q_recv,
        q1_recv_sem, q2_send_sem, q2_recv_sem)

    carry = (jnp.zeros((ROWS, HD), F32), jnp.zeros((ROWS, HD), F32))
    for c in range(PARTS):
        v_copy(c).wait()
        carry = lax.fori_loop(c * per_part, (c + 1) * per_part, values_chunk, carry)
    total, own_out = carry
    own_total = jnp.sum(total, axis=1, keepdims=True)

    arrived(q_recv, q2_recv_sem)
    guest_query = q_recv[(y - guest) & (NY - 1)]
    guest_top = jnp.full((ROWS, HD), NEG, F32)
    for i in range(LENT):
        s = lax.dot_general(guest_query, k_buf[slots[i]], NT_DIMS, preferred_element_type=F32)
        s = jnp.where(page_token < limits[i], s, NEG)
        guest_buf[:, i * PAGE:(i + 1) * PAGE] = s
        guest_top = jnp.maximum(guest_top, jnp.maximum(s[:, :HD], s[:, HD:]))
    guest_top = jnp.max(guest_top, axis=1, keepdims=True) * LOG2E_SCALE
    total = jnp.zeros((ROWS, HD), F32)
    guest_out = jnp.zeros((ROWS, HD), F32)
    for i in range(LENT):
        s = guest_buf[:, i * PAGE:(i + 1) * PAGE]
        w = jnp.exp2(s * LOG2E_SCALE - guest_top)
        total = total + lanes_sum(w)
        guest_out = guest_out + jnp.dot(w.astype(BF16), v_buf[slots[i]], preferred_element_type=F32)
    guest_total = jnp.sum(total, axis=1, keepdims=True)
    level = jnp.broadcast_to(guest_top + jnp.log2(guest_total), (ROWS, HD))
    lane = lax.broadcasted_iota(jnp.int32, (ROWS, HD), 1)
    high = level.astype(BF16).astype(F32)
    middle = (level - high).astype(BF16).astype(F32)
    low = level - high - middle
    place = lane & 63
    coded = jnp.where(place == 0, high, jnp.where(place == 1, middle, jnp.where(place == 2, low, 0.0)))
    half_rows = ROWS // 2
    coded = jnp.where(lane[:half_rows] < 64, coded[:half_rows], coded[half_rows:])
    result = jnp.concatenate([guest_out / guest_total, coded], axis=0).astype(BF16)
    p_own[...] = result
    p_relay = (p_relay_even, p_relay_odd)
    to_relays(p_own, p_relay, p1_send_sem, p1_recv_sem)
    p_relay_odd[0] = result

    for copy in w_copies:
        copy.wait()
    for copy in st_copies:
        copy.wait_recv()
    row16 = lax.broadcasted_iota(jnp.int32, (16, HD), 0) // STEPS

    def project(d, acc):
        source = (tensor - d + NT) % NT
        for h in range(2):
            x = st_all[d, h * 16:(h + 1) * 16, :].astype(F32)
            left = jnp.concatenate([jnp.where(row16 == g, x, 0.0) for g in range(4)], axis=1).astype(BF16)
            weight = jnp.concatenate(
                [kw_buf[source, h * 512:(h + 1) * 512, :], vw_buf[source, h * 512:(h + 1) * 512, :]], axis=1)
            acc = acc + jnp.dot(left, weight, preferred_element_type=F32)
        return acc

    acc = lax.fori_loop(0, NT, project, jnp.zeros((16, 2 * HD), F32))
    acc = acc[:8] + acc[8:]
    acc = acc[:4] + acc[4:]
    padded = jnp.concatenate([acc, jnp.zeros((12, 2 * HD), F32)], axis=0).astype(BF16)
    new_keys = padded[:, :HD]
    new_values = padded[:, HD:]
    s = lax.dot_general(query, new_keys, NT_DIMS, preferred_element_type=F32)
    step = lax.broadcasted_iota(jnp.int32, (ROWS, 16), 0) % STEPS
    other = lax.broadcasted_iota(jnp.int32, (ROWS, 16), 1)
    s = jnp.where(other <= step, s * LOG2E_SCALE, NEG)
    merged_top = jnp.maximum(own_top, jnp.max(s, axis=1, keepdims=True))
    w = jnp.exp2(s - merged_top)
    kept = jnp.exp2(own_top - merged_top)
    merged_total = own_total * kept + jnp.sum(w, axis=1, keepdims=True)
    merged_out = own_out * kept + jnp.dot(w.astype(BF16), new_values, preferred_element_type=F32)

    relayed(
        p_relay, [(z - (lender[e] >> 2)) & (NZ - 1) for e in range(NY)], p_send, p_recv,
        p1_recv_sem, p2_send_sem, p2_recv_sem)
    arrived(p_recv, p2_recv_sem)
    lent_part = p_recv[(y - lender[0]) & (NY - 1)].astype(F32)
    coded = lent_part[ROWS:]
    lane16 = lane[:half_rows]
    level = jnp.concatenate([
        jnp.sum(jnp.where(lane16 < 64, coded, 0.0), axis=1, keepdims=True),
        jnp.sum(jnp.where(lane16 < 64, 0.0, coded), axis=1, keepdims=True)], axis=0)
    level = jnp.where(lender[0] >= 0, level, NEG)
    highest = jnp.maximum(merged_top, level)
    kept = jnp.exp2(merged_top - highest)
    added = jnp.exp2(level - highest)
    out_ref[...] = (merged_out * kept + lent_part[:ROWS] * added) / (merged_total * kept + added)

    for copy in st_copies:
        copy.wait_send()
    to_relays_done(q_own, q_relay, q1_send_sem, q1_recv_sem)
    to_relays_done(p_own, p_relay, p1_send_sem, p1_recv_sem)

    @pl.when(is_relay)
    def _():
        relay_done(q_send, q_recv, q2_send_sem, q2_recv_sem)
        relay_done(p_send, p_recv, p2_send_sem, p2_recv_sem)


def on_device(queries, new_states, key_weight, value_weight, key_pool, value_pool, lengths, page_table):
    hbm = pl.BlockSpec(memory_space=pltpu.HBM)
    dma = pltpu.SemaphoreType.DMA

    def rows_of(x):
        return jnp.transpose(x.reshape(STEPS, GROUP, HD), (1, 0, 2)).reshape(ROWS, HD)

    out = pl.pallas_call(
        kernel,
        out_shape=pltpu.VMEM((ROWS, HD), F32),
        in_specs=[hbm] * 8,
        out_specs=pl.BlockSpec(memory_space=pltpu.VMEM),
        scratch_shapes=[
            pltpu.SMEM((1, 32), jnp.int32),
            pltpu.SMEM((32, SLOTS), jnp.int32),
            pltpu.VMEM((32, SLOTS), jnp.int32),
            pltpu.VMEM((SLOTS, PAGE, HD), BF16),
            pltpu.VMEM((SLOTS, PAGE, HD), BF16),
            pltpu.VMEM((NT, GROUP * HD, HD), BF16),
            pltpu.VMEM((NT, GROUP * HD, HD), BF16),
            pltpu.VMEM((CHUNKS, ROWS, CHUNK * PAGE), F32),
            pltpu.VMEM((ROWS, LENT * PAGE), F32),
            pltpu.VMEM((SLOTS, PAGE), F32),
            pltpu.VMEM((NT, ROWS, HD), BF16),
            pltpu.VMEM((ROWS, HD), BF16),
            pltpu.VMEM((NZ, ROWS, HD), BF16),
            pltpu.VMEM((NZ, ROWS, HD), BF16),
            pltpu.VMEM((2, NY, ROWS, HD), BF16),
            pltpu.VMEM((NY, ROWS, HD), BF16),
            pltpu.VMEM((ROWS + 16, HD), BF16),
            pltpu.VMEM((NZ, ROWS + 16, HD), BF16),
            pltpu.VMEM((NZ, ROWS + 16, HD), BF16),
            pltpu.VMEM((2, NY, ROWS + 16, HD), BF16),
            pltpu.VMEM((NY, ROWS + 16, HD), BF16),
            dma((5,)), dma((PARTS,)), dma((PARTS,)), dma((2,)), dma((NT,)), dma((NT,)),
            dma((NZ,)), dma((2, NZ)), dma((2, NY)), dma((NY,)),
            dma((NZ,)), dma((2, NZ)), dma((2, NY)), dma((NY,)),
        ],
        compiler_params=pltpu.CompilerParams(
            collective_id=0, has_side_effects=True, vmem_limit_bytes=VMEM_BYTES),
    )(
        lengths.reshape(1, -1), page_table, rows_of(queries), rows_of(new_states),
        key_weight.reshape(NT, GROUP * HD, HD), value_weight.reshape(NT, GROUP * HD, HD),
        key_pool, value_pool,
    )
    return (
        jnp.transpose(out.reshape(GROUP, STEPS, HD), (1, 0, 2))
        .reshape(1, STEPS, GROUP * HD)
        .astype(BF16)
    )


def solution(mesh):
    placed = (
        P("inst", None, "tensor"),
        P("inst", None, "tensor"),
        P(None, "tensor"),
        P(None, "tensor"),
        P("inst", None, "tensor"),
        P("inst", None, "tensor"),
        P(),
        P(),
    )
    return jax.shard_map(
        on_device, mesh=mesh, in_specs=placed, out_specs=P("inst", None, "tensor"), check_vma=False
    )
```

```python
import math

import jax
import jax.numpy as jnp
from jax import lax
from jax.experimental import pallas as pl
from jax.experimental.pallas import tpu as pltpu
from jax.sharding import PartitionSpec as P

HD = 128
STEPS = 4
GROUP = 8
ROWS = STEPS * GROUP
PAGE = 256
SLOTS = 64
CHUNK = 8
CHUNKS = SLOTS // CHUNK
PARTS = 4
PART = SLOTS // PARTS
LENT = 16
NY = 4
NZ = 8
NT = 8
NEG = -1e30
VMEM_BYTES = 60 * 1024 * 1024
Z_ORDER = (4, 3, 5, 2, 6, 1, 7)
Y_ORDER = (2, 1, 3)
T_ORDER = (4, 5, 3, 2, 6, 7, 1)
R_ORDER = (4, 3, 5, 2, 6, 1, 7)
STRAIGHT = ((4, 2, 0),)
LOG2E_SCALE = math.log2(math.e) / math.sqrt(HD)
F32 = jnp.float32
BF16 = jnp.bfloat16
MESH = pl.DeviceIdType.MESH
NT_DIMS = (((1,), (1,)), ((), ()))


def remote_copy(src, dst, send_sem, recv_sem, target):
    return pltpu.make_async_remote_copy(
        src_ref=src, dst_ref=dst, send_sem=send_sem, recv_sem=recv_sem, device_id=target, device_id_type=MESH)


def lanes_sum(w):
    total = w[:, :HD]
    for b in range(1, w.shape[1] // HD):
        total = total + w[:, b * HD:(b + 1) * HD]
    return total


def kernel(
    len_hbm, tab_hbm, q_hbm, st_hbm, kw_hbm, vw_hbm, k_hbm, v_hbm,
    out_ref,
    len_smem, tab_smem, tab_ref, k_buf, v_buf, kw_buf, vw_buf, s_buf, guest_buf, bias_buf,
    st_all, q_own, q_relay_even, q_relay_odd, q_send, q_recv, p_own, p_near_even, p_near_odd, p_far_even, p_far_odd, p_send, p_recv, p_straight,
    small_sem, k_sem, v_sem, w_sem, st_send_sem, st_recv_sem,
    q1_send_sem, q1_recv_sem, q2_send_sem, q2_recv_sem,
    p1_send_sem, p1_recv_sem, p2_send_sem, p2_recv_sem, ps_send_sem, ps_recv_sem,
):
    inst = lax.axis_index("inst")
    tensor = lax.axis_index("tensor")
    z = inst // NY
    y = inst % NY
    odd = tensor % 2
    even_t = tensor - odd
    odd_t = even_t + 1
    is_relay = odd == 1
    z_peer = [((z + d) % NZ) * NY + y for d in range(NZ)]
    y_peer = [z * NY + (y + e) % NY for e in range(NY)]
    t_peer = [(tensor + d) % NT for d in range(NT)]

    barrier = pltpu.get_barrier_semaphore()

    @pl.when(is_relay)
    def _():
        for d in Z_ORDER:
            pl.semaphore_signal(barrier, inc=1, device_id=(z_peer[d], even_t), device_id_type=MESH)
            pl.semaphore_signal(barrier, inc=1, device_id=(z_peer[d], odd_t), device_id_type=MESH)

    for e in Y_ORDER:
        pl.semaphore_signal(barrier, inc=1, device_id=(y_peer[e], odd_t), device_id_type=MESH)
    for d in T_ORDER:
        pl.semaphore_signal(barrier, inc=1, device_id=(inst, t_peer[d]), device_id_type=MESH)

    small_copies = [
        pltpu.make_async_copy(q_hbm, q_own, small_sem.at[0]),
        pltpu.make_async_copy(st_hbm, st_all.at[0], small_sem.at[1]),
        pltpu.make_async_copy(tab_hbm, tab_ref, small_sem.at[2]),
        pltpu.make_async_copy(len_hbm, len_smem, small_sem.at[3]),
        pltpu.make_async_copy(tab_hbm, tab_smem, small_sem.at[4]),
    ]
    for copy in small_copies:
        copy.start()

    def k_copy(c):
        part = pl.ds(c * PART, PART)
        return pltpu.make_async_copy(k_hbm.at[part], k_buf.at[part], k_sem.at[c])

    def v_copy(c):
        part = pl.ds(c * PART, PART)
        return pltpu.make_async_copy(v_hbm.at[part], v_buf.at[part], v_sem.at[c])

    w_copies = [
        pltpu.make_async_copy(kw_hbm, kw_buf, w_sem.at[0]),
        pltpu.make_async_copy(vw_hbm, vw_buf, w_sem.at[1]),
    ]
    for c in range(PARTS):
        k_copy(c).start()
    for c in range(PARTS):
        v_copy(c).start()
    for copy in w_copies:
        copy.start()

    small_copies[0].wait()
    small_copies[1].wait()
    query = q_own[...]
    q_relay_odd[0] = query
    pl.semaphore_wait(barrier, NZ + NT - 2 + (NY + NY - 2) * odd)

    def relay_copy(own, relay, d, p, send_sem, recv_sem):
        return remote_copy(own, relay[p].at[d], send_sem.at[d], recv_sem.at[p, d], (z_peer[d], odd_t))

    def to_relays(own, relay, send_sem, recv_sem):
        @pl.when(is_relay)
        def _():
            for d in Z_ORDER:
                relay_copy(own, relay, d, 1, send_sem, recv_sem).start()

        @pl.when(jnp.logical_not(is_relay))
        def _():
            for d in Z_ORDER + (0,):
                relay_copy(own, relay, d, 0, send_sem, recv_sem).start()

    def to_relays_done(own, relay, send_sem, recv_sem):
        for d in Z_ORDER:
            relay_copy(own, relay, d, 0, send_sem, recv_sem).wait_send()

        @pl.when(jnp.logical_not(is_relay))
        def _():
            relay_copy(own, relay, 0, 0, send_sem, recv_sem).wait_send()

    def relayed(relay, source, sent, received, arrive_sem, send_sem, recv_sem):
        @pl.when(is_relay)
        def _():
            for p in (1, 0):
                for d in Z_ORDER + (0,) * (1 - p):
                    relay_copy(sent.at[p, 0], relay, d, p, arrive_sem.at[p], arrive_sem).wait_recv()
                for e in Y_ORDER + (0,):
                    picked = relay[p][source[e]]
                    if p == 1 and e == 0:
                        received[0] = picked
                    else:
                        sent[p, e] = picked
                        remote_copy(
                            sent.at[p, e], received.at[e], send_sem.at[p, e], recv_sem.at[e], (y_peer[e], even_t + p)
                        ).start()

    def relay_done(sent, received, send_sem, recv_sem):
        for p in range(2):
            for e in Y_ORDER + (0,) * (1 - p):
                remote_copy(
                    sent.at[p, e], received.at[e], send_sem.at[p, e], recv_sem.at[e], (y_peer[e], even_t + p)
                ).wait_send()

    def arrived(received, recv_sem):
        for e in Y_ORDER:
            remote_copy(
                received.at[e], received.at[e], recv_sem.at[e], recv_sem.at[e], (y_peer[e], odd_t)
            ).wait_recv()

        @pl.when(jnp.logical_not(is_relay))
        def _():
            remote_copy(
                received.at[0], received.at[0], recv_sem.at[0], recv_sem.at[0], (inst, odd_t)
            ).wait_recv()

    q_relay = (q_relay_even, q_relay_odd)
    to_relays(q_own, q_relay, q1_send_sem, q1_recv_sem)
    st_copies = [
        remote_copy(st_all.at[0], st_all.at[d], st_send_sem.at[d], st_recv_sem.at[d], (inst, t_peer[d]))
        for d in T_ORDER
    ]
    for copy in st_copies:
        copy.start()

    for copy in small_copies[2:]:
        copy.wait()
    table = tab_ref[...]
    holder = table >> 6
    row_id = lax.broadcasted_iota(jnp.int32, table.shape, 0)
    page_id = lax.broadcasted_iota(jnp.int32, table.shape, 1)
    lent = (table >= 0) & (holder != row_id)
    lent_code = jnp.where(lent, row_id * SLOTS + (SLOTS - 1) - page_id, -1)
    lent_holder = jnp.where(lent, holder, -1)
    guest_code = [jnp.max(jnp.where(holder == y_peer[e], lent_code, -1)) for e in range(NY)]
    lender = [jnp.max(jnp.where(row_id == y_peer[e], lent_holder, -1)) for e in range(NY)]

    own_length = len_smem[0, inst]
    own_row = jnp.broadcast_to(tab_ref[pl.ds(inst, 1), :] - inst * SLOTS, (SLOTS, SLOTS))
    slot_id = lax.broadcasted_iota(jnp.int32, (SLOTS, SLOTS), 0)
    page_of = lax.broadcasted_iota(jnp.int32, (SLOTS, SLOTS), 1)
    counted = jnp.clip(own_length - page_of * PAGE, 0, PAGE).astype(F32)
    valid = jnp.sum(jnp.where(own_row == slot_id, counted, 0.0), axis=1, keepdims=True)
    token = lax.broadcasted_iota(jnp.int32, (SLOTS, PAGE), 1).astype(F32)
    bias_buf[...] = jnp.where(token < valid, 0.0, NEG)

    guest = guest_code[0] >> 6
    first_page = (SLOTS - 1) - (guest_code[0] & (SLOTS - 1))
    guest_row = jnp.maximum(guest, 0)
    guest_length = jnp.where(guest >= 0, len_smem[0, guest_row], 0)
    guest_pages = ((guest_length + PAGE - 1) // PAGE) // 4
    page_token = lax.broadcasted_iota(jnp.int32, (1, PAGE), 1)
    slots = []
    limits = []
    for i in range(LENT):
        page = jnp.minimum(first_page + i, SLOTS - 1)
        slots.append(jnp.clip(tab_smem[guest_row, page] - inst * SLOTS, 0, SLOTS - 1))
        limits.append(jnp.where(i < guest_pages, guest_length - page * PAGE, 0))

    def scores_chunk(c, top):
        for p in range(CHUNK):
            slot = c * CHUNK + p
            s = lax.dot_general(query, k_buf[slot], NT_DIMS, preferred_element_type=F32)
            s = s + bias_buf[pl.ds(slot, 1), :]
            s_buf[c, :, p * PAGE:(p + 1) * PAGE] = s
            top = jnp.maximum(top, jnp.maximum(s[:, :HD], s[:, HD:]))
        return top

    def values_chunk(c, carry):
        total, numerator = carry
        half = CHUNK // 2
        for h in range(2):
            s = s_buf[c, :, h * half * PAGE:(h + 1) * half * PAGE]
            w = jnp.exp2(s * LOG2E_SCALE - own_top)
            total = total + lanes_sum(w)
            v = v_buf[pl.ds(c * CHUNK + h * half, half)].reshape(half * PAGE, HD)
            numerator = numerator + jnp.dot(w.astype(BF16), v, preferred_element_type=F32)
        return total, numerator

    per_part = CHUNKS // PARTS
    top = jnp.full((ROWS, HD), NEG, F32)
    for c in range(PARTS):
        k_copy(c).wait()
        top = lax.fori_loop(c * per_part, (c + 1) * per_part, scores_chunk, top)
    own_top = jnp.max(top, axis=1, keepdims=True) * LOG2E_SCALE

    relayed(
        q_relay, [(z - (guest_code[e] >> 8)) & (NZ - 1) for e in range(NY)], q_send, q_recv,
        q1_recv_sem, q2_send_sem, q2_recv_sem)

    carry = (jnp.zeros((ROWS, HD), F32), jnp.zeros((ROWS, HD), F32))
    for c in range(PARTS):
        v_copy(c).wait()
        carry = lax.fori_loop(c * per_part, (c + 1) * per_part, values_chunk, carry)
    total, own_out = carry
    own_total = jnp.sum(total, axis=1, keepdims=True)

    arrived(q_recv, q2_recv_sem)
    guest_query = q_recv[(y - guest) & (NY - 1)]
    guest_top = jnp.full((ROWS, HD), NEG, F32)
    for i in range(LENT):
        s = lax.dot_general(guest_query, k_buf[slots[i]], NT_DIMS, preferred_element_type=F32)
        s = jnp.where(page_token < limits[i], s, NEG)
        guest_buf[:, i * PAGE:(i + 1) * PAGE] = s
        guest_top = jnp.maximum(guest_top, jnp.maximum(s[:, :HD], s[:, HD:]))
    guest_top = jnp.max(guest_top, axis=1, keepdims=True) * LOG2E_SCALE
    total = jnp.zeros((ROWS, HD), F32)
    guest_out = jnp.zeros((ROWS, HD), F32)
    for i in range(LENT):
        s = guest_buf[:, i * PAGE:(i + 1) * PAGE]
        w = jnp.exp2(s * LOG2E_SCALE - guest_top)
        total = total + lanes_sum(w)
        guest_out = guest_out + jnp.dot(w.astype(BF16), v_buf[slots[i]], preferred_element_type=F32)
    guest_total = jnp.sum(total, axis=1, keepdims=True)
    level = jnp.broadcast_to(guest_top + jnp.log2(guest_total), (ROWS, HD))
    lane = lax.broadcasted_iota(jnp.int32, (ROWS, HD), 1)
    high = level.astype(BF16).astype(F32)
    middle = (level - high).astype(BF16).astype(F32)
    low = level - high - middle
    place = lane & 63
    coded = jnp.where(place == 0, high, jnp.where(place == 1, middle, jnp.where(place == 2, low, 0.0)))
    half_rows = ROWS // 2
    coded = jnp.where(lane[:half_rows] < 64, coded[:half_rows], coded[half_rows:])
    result = jnp.concatenate([guest_out / guest_total, coded], axis=0).astype(BF16)
    p_own[...] = result
    p_near, p_far = (p_near_even, p_near_odd), (p_far_even, p_far_odd)

    def p_slot(p, d):
        if d == 4:
            return p_far[p].at[0]
        return p_near[p].at[d if d < 4 else d - 1]

    def p1_copy(p, d):
        return remote_copy(p_own, p_slot(p, d), p1_send_sem.at[d], p1_recv_sem.at[p, d], (z_peer[d], odd_t))

    straight_copies = [
        remote_copy(
            p_own, p_straight.at[k], ps_send_sem.at[k], ps_recv_sem.at[k],
            (((z + dz) % NZ) * NY + (y + dy) % NY, tensor))
        for dz, dy, k in STRAIGHT
    ]

    @pl.when(is_relay)
    def _():
        p1_copy(1, 4).start()
        straight_copies[0].start()
        for d in R_ORDER[1:]:
            p1_copy(1, d).start()

    @pl.when(jnp.logical_not(is_relay))
    def _():
        p1_copy(0, 4).start()
        straight_copies[0].start()
        for d in R_ORDER[1:] + (0,):
            p1_copy(0, d).start()

    p_near_odd[0] = result

    for copy in w_copies:
        copy.wait()
    for copy in st_copies:
        copy.wait_recv()
    row16 = lax.broadcasted_iota(jnp.int32, (16, HD), 0) // STEPS

    def project(d, acc):
        source = (tensor - d + NT) % NT
        for h in range(2):
            x = st_all[d, h * 16:(h + 1) * 16, :].astype(F32)
            left = jnp.concatenate([jnp.where(row16 == g, x, 0.0) for g in range(4)], axis=1).astype(BF16)
            weight = jnp.concatenate(
                [kw_buf[source, h * 512:(h + 1) * 512, :], vw_buf[source, h * 512:(h + 1) * 512, :]], axis=1)
            acc = acc + jnp.dot(left, weight, preferred_element_type=F32)
        return acc

    acc = lax.fori_loop(0, NT, project, jnp.zeros((16, 2 * HD), F32))
    acc = acc[:8] + acc[8:]
    acc = acc[:4] + acc[4:]
    padded = jnp.concatenate([acc, jnp.zeros((12, 2 * HD), F32)], axis=0).astype(BF16)
    new_keys = padded[:, :HD]
    new_values = padded[:, HD:]
    s = lax.dot_general(query, new_keys, NT_DIMS, preferred_element_type=F32)
    step = lax.broadcasted_iota(jnp.int32, (ROWS, 16), 0) % STEPS
    other = lax.broadcasted_iota(jnp.int32, (ROWS, 16), 1)
    s = jnp.where(other <= step, s * LOG2E_SCALE, NEG)
    merged_top = jnp.maximum(own_top, jnp.max(s, axis=1, keepdims=True))
    w = jnp.exp2(s - merged_top)
    kept = jnp.exp2(own_top - merged_top)
    merged_total = own_total * kept + jnp.sum(w, axis=1, keepdims=True)
    merged_out = own_out * kept + jnp.dot(w.astype(BF16), new_values, preferred_element_type=F32)

    @pl.when(is_relay)
    def _():
        for p in (1, 0):
            for group, targets in (((3, 5, 2, 6, 1, 7), (2,)), ((4,), (1, 3, 0))):
                for d in group + ((0,) if p == 0 and 2 in targets else ()):
                    p1_copy(p, d).wait_recv()
                for e in targets:
                    source = (z - (lender[e] >> 2)) & (NZ - 1)
                    picked = p_near[p][jnp.where(source <= 3, source, source - 1)]
                    if e != 2:
                        picked = lax.select(source == 4, p_far[p][0], picked)
                    if p == 1 and e == 0:
                        p_recv[0] = picked
                    else:
                        p_send[p, e] = picked
                        remote_copy(
                            p_send.at[p, e], p_recv.at[e], p2_send_sem.at[p, e], p2_recv_sem.at[e],
                            (y_peer[e], even_t + p)
                        ).start()

    arrived(p_recv, p2_recv_sem)
    for copy in straight_copies:
        copy.wait_recv()
    from_z = (z - (lender[0] >> 2)) & (NZ - 1)
    from_y = (y - lender[0]) & (NY - 1)
    straight = (from_z == 4) & (from_y == 2)
    lent_part = lax.select(straight, p_straight[0], p_recv[from_y]).astype(F32)
    coded = lent_part[ROWS:]
    lane16 = lane[:half_rows]
    level = jnp.concatenate([
        jnp.sum(jnp.where(lane16 < 64, coded, 0.0), axis=1, keepdims=True),
        jnp.sum(jnp.where(lane16 < 64, 0.0, coded), axis=1, keepdims=True)], axis=0)
    level = jnp.where(lender[0] >= 0, level, NEG)
    highest = jnp.maximum(merged_top, level)
    kept = jnp.exp2(merged_top - highest)
    added = jnp.exp2(level - highest)
    out_ref[...] = (merged_out * kept + lent_part[:ROWS] * added) / (merged_total * kept + added)

    for copy in st_copies:
        copy.wait_send()
    to_relays_done(q_own, q_relay, q1_send_sem, q1_recv_sem)
    for d in Z_ORDER:
        p1_copy(0, d).wait_send()

    @pl.when(jnp.logical_not(is_relay))
    def _():
        p1_copy(0, 0).wait_send()

    for copy in straight_copies:
        copy.wait_send()

    @pl.when(is_relay)
    def _():
        relay_done(q_send, q_recv, q2_send_sem, q2_recv_sem)
        relay_done(p_send, p_recv, p2_send_sem, p2_recv_sem)


def on_device(queries, new_states, key_weight, value_weight, key_pool, value_pool, lengths, page_table):
    hbm = pl.BlockSpec(memory_space=pltpu.HBM)
    dma = pltpu.SemaphoreType.DMA

    def rows_of(x):
        return jnp.transpose(x.reshape(STEPS, GROUP, HD), (1, 0, 2)).reshape(ROWS, HD)

    out = pl.pallas_call(
        kernel,
        out_shape=pltpu.VMEM((ROWS, HD), F32),
        in_specs=[hbm] * 8,
        out_specs=pl.BlockSpec(memory_space=pltpu.VMEM),
        scratch_shapes=[
            pltpu.SMEM((1, 32), jnp.int32),
            pltpu.SMEM((32, SLOTS), jnp.int32),
            pltpu.VMEM((32, SLOTS), jnp.int32),
            pltpu.VMEM((SLOTS, PAGE, HD), BF16),
            pltpu.VMEM((SLOTS, PAGE, HD), BF16),
            pltpu.VMEM((NT, GROUP * HD, HD), BF16),
            pltpu.VMEM((NT, GROUP * HD, HD), BF16),
            pltpu.VMEM((CHUNKS, ROWS, CHUNK * PAGE), F32),
            pltpu.VMEM((ROWS, LENT * PAGE), F32),
            pltpu.VMEM((SLOTS, PAGE), F32),
            pltpu.VMEM((NT, ROWS, HD), BF16),
            pltpu.VMEM((ROWS, HD), BF16),
            pltpu.VMEM((NZ, ROWS, HD), BF16),
            pltpu.VMEM((NZ, ROWS, HD), BF16),
            pltpu.VMEM((2, NY, ROWS, HD), BF16),
            pltpu.VMEM((NY, ROWS, HD), BF16),
            pltpu.VMEM((ROWS + 16, HD), BF16),
            pltpu.VMEM((7, ROWS + 16, HD), BF16),
            pltpu.VMEM((7, ROWS + 16, HD), BF16),
            pltpu.VMEM((1, ROWS + 16, HD), BF16),
            pltpu.VMEM((1, ROWS + 16, HD), BF16),
            pltpu.VMEM((2, NY, ROWS + 16, HD), BF16),
            pltpu.VMEM((NY, ROWS + 16, HD), BF16),
            pltpu.VMEM((1, ROWS + 16, HD), BF16),
            dma((5,)), dma((PARTS,)), dma((PARTS,)), dma((2,)), dma((NT,)), dma((NT,)),
            dma((NZ,)), dma((2, NZ)), dma((2, NY)), dma((NY,)),
            dma((NZ,)), dma((2, NZ)), dma((2, NY)), dma((NY,)), dma((1,)), dma((1,)),
        ],
        compiler_params=pltpu.CompilerParams(
            collective_id=0, has_side_effects=True, vmem_limit_bytes=VMEM_BYTES),
    )(
        lengths.reshape(1, -1), page_table, rows_of(queries), rows_of(new_states),
        key_weight.reshape(NT, GROUP * HD, HD), value_weight.reshape(NT, GROUP * HD, HD),
        key_pool, value_pool,
    )
    return (
        jnp.transpose(out.reshape(GROUP, STEPS, HD), (1, 0, 2))
        .reshape(1, STEPS, GROUP * HD)
        .astype(BF16)
    )


def solution(mesh):
    placed = (
        P("inst", None, "tensor"),
        P("inst", None, "tensor"),
        P(None, "tensor"),
        P(None, "tensor"),
        P("inst", None, "tensor"),
        P("inst", None, "tensor"),
        P(),
        P(),
    )
    return jax.shard_map(
        on_device, mesh=mesh, in_specs=placed, out_specs=P("inst", None, "tensor"), check_vma=False
    )
```

```python
import math

import jax
import jax.numpy as jnp
from jax import lax
from jax.experimental import pallas as pl
from jax.experimental.pallas import tpu as pltpu
from jax.sharding import PartitionSpec as P

HD = 128
STEPS = 4
GROUP = 8
ROWS = STEPS * GROUP
PAGE = 256
SLOTS = 64
CHUNK = 8
CHUNKS = SLOTS // CHUNK
PARTS = 4
PART = SLOTS // PARTS
LENT = 16
NY = 4
NZ = 8
NT = 8
EARLY = 2
HOMES = (0, 1)
GUESTS = 3
FIRST_ORDER = (0, 1)
NEG = -1e30
VMEM_BYTES = 60 * 1024 * 1024
Z_ORDER = (4, 3, 5, 2, 6, 1, 7)
Y_ORDER = (2, 1, 3)
T_ORDER = (4, 5, 3, 2, 6, 7, 1)
LOG2E_SCALE = math.log2(math.e) / math.sqrt(HD)
F32 = jnp.float32
BF16 = jnp.bfloat16
MESH = pl.DeviceIdType.MESH
NT_DIMS = (((1,), (1,)), ((), ()))


def remote_copy(src, dst, send_sem, recv_sem, target):
    return pltpu.make_async_remote_copy(
        src_ref=src, dst_ref=dst, send_sem=send_sem, recv_sem=recv_sem, device_id=target, device_id_type=MESH)


def lanes_sum(w):
    total = w[:, :HD]
    for b in range(1, w.shape[1] // HD):
        total = total + w[:, b * HD:(b + 1) * HD]
    return total


def kernel(
    len_hbm, tab_hbm, q_hbm, st_hbm, kw_hbm, vw_hbm, k_hbm, v_hbm,
    out_ref,
    len_smem, tab_smem, tab_ref, k_buf, v_buf, kw_buf, vw_buf, s_buf, guest_buf, bias_buf, st_all,
    q_own, q_row_even, q_row_odd, q_late_even, q_late_odd, q_send_first, q_send_second, q_recv_first, q_recv_second,
    p_own_first, p_own_second, p_relay_even, p_relay_odd, p_send, p_recv,
    small_sem, k_sem, v_sem, w_sem, st_send_sem, st_recv_sem, ready_sem, plane_sem, go_sem,
    q1_send_sem, q1_row_sem, q1_late_sem, qa_send_sem, qa_recv_sem, qb_send_sem, qb_recv_sem,
    p1_send_sem, p1_recv_sem, p2_send_sem, p2_recv_sem,
):
    inst = lax.axis_index("inst")
    tensor = lax.axis_index("tensor")
    z = inst // NY
    y = inst % NY
    odd = tensor % 2
    even_t = tensor - odd
    odd_t = even_t + 1
    is_relay = odd == 1
    is_even = odd == 0
    early = z < EARLY
    late = z >= EARLY
    early_relay = early & is_relay
    home_relay = is_relay & ((z == HOMES[0]) | (z == HOMES[1]))
    row = jnp.minimum(z, EARLY - 1)
    home_place = jnp.where(z == HOMES[0], 0, 1)
    home_row = jnp.where(z >= 5, HOMES[0], HOMES[1])
    guests_from = jnp.where(z == HOMES[0], 5, 2)

    def at(zz, yy):
        return zz * NY + yy

    z_peer = [at((z + d) % NZ, y) for d in range(NZ)]
    ys = [(y + e) % NY for e in range(NY)]
    y_peer = [at(z, ys[e]) for e in range(NY)]
    t_peer = [(tensor + d) % NT for d in range(NT)]

    barrier = pltpu.get_barrier_semaphore()

    def greet(where, which):
        pl.semaphore_signal(barrier, inc=1, device_id=(where, which), device_id_type=MESH)

    @pl.when(early_relay)
    def _():
        for zz in range(NZ - 1, EARLY - 1, -1):
            greet(at(zz, y), even_t)
            greet(at(zz, y), odd_t)

    @pl.when(home_relay)
    def _():
        for j in range(GUESTS):
            for e in Y_ORDER:
                greet(at(guests_from + j, ys[e]), even_t)
                greet(at(guests_from + j, ys[e]), odd_t)

    @pl.when(early)
    def _():
        for c in range(1, EARLY):
            greet(at((z + c) % EARLY, y), odd_t)
        for d in T_ORDER:
            greet(inst, t_peer[d])

    @pl.when(early_relay)
    def _():
        for e in Y_ORDER:
            greet(y_peer[e], even_t)
            greet(y_peer[e], odd_t)

    small_copies = [
        pltpu.make_async_copy(q_hbm, q_own, small_sem.at[0]),
        pltpu.make_async_copy(st_hbm, st_all.at[0], small_sem.at[1]),
        pltpu.make_async_copy(tab_hbm, tab_ref, small_sem.at[2]),
        pltpu.make_async_copy(len_hbm, len_smem, small_sem.at[3]),
        pltpu.make_async_copy(tab_hbm, tab_smem, small_sem.at[4]),
    ]
    for copy in small_copies:
        copy.start()

    def k_copy(c):
        part = pl.ds(c * PART, PART)
        return pltpu.make_async_copy(k_hbm.at[part], k_buf.at[part], k_sem.at[c])

    def v_copy(c):
        part = pl.ds(c * PART, PART)
        return pltpu.make_async_copy(v_hbm.at[part], v_buf.at[part], v_sem.at[c])

    w_copies = [
        pltpu.make_async_copy(kw_hbm, kw_buf, w_sem.at[0]),
        pltpu.make_async_copy(vw_hbm, vw_buf, w_sem.at[1]),
    ]

    pl.semaphore_wait(barrier, jnp.where(late, EARLY + NY - 1, jnp.where(is_relay, NY - 1 + 2 * (EARLY - 1) + NT - 1, NY + NT - 2)))

    @pl.when(late)
    def _():
        for c in range(EARLY):
            pl.semaphore_signal(
                ready_sem, inc=1, device_id=(at((z + c) % EARLY, y), odd_t), device_id_type=MESH)

    small_copies[0].wait()

    def q1_copy(place, e, target):
        buffer, slot, sem = place
        return remote_copy(q_own, buffer.at[slot], q1_send_sem.at[e], sem.at[slot], (target, odd_t))

    def q1_row(p, e):
        return q1_copy(((q_row_even, q_row_odd)[p], e, q1_row_sem.at[p]), e, y_peer[e])

    def q1_late(p, e):
        return q1_copy(
            ((q_late_even, q_late_odd)[p], ((z + 1) % GUESTS) * NY + e, q1_late_sem.at[p]), e, at(home_row, ys[e]))

    for p in range(2):
        @pl.when(early & (odd == p))
        def _():
            for e in Y_ORDER + (0,) * (1 - p):
                q1_row(p, e).start()

        @pl.when(late & (odd == p))
        def _():
            for e in Y_ORDER + (0,):
                q1_late(p, e).start()

    for c in range(PARTS):
        k_copy(c).start()
    for c in range(PARTS):
        v_copy(c).start()
    for copy in w_copies:
        copy.start()

    small_copies[1].wait()
    st_copies = [
        remote_copy(st_all.at[0], st_all.at[d], st_send_sem.at[d], st_recv_sem.at[d], (inst, t_peer[d]))
        for d in T_ORDER
    ]

    @pl.when(early)
    def _():
        for copy in st_copies:
            copy.start()

    query = q_own[...]
    q_row_odd[0] = query

    def relay_copy(own, relay, d, p, send_sem, recv_sem):
        return remote_copy(own, relay[p].at[d], send_sem.at[d], recv_sem.at[p, d], (z_peer[d], odd_t))

    for copy in small_copies[2:]:
        copy.wait()
    table = tab_ref[...]
    holder = table >> 6
    row_id = lax.broadcasted_iota(jnp.int32, table.shape, 0)
    page_id = lax.broadcasted_iota(jnp.int32, table.shape, 1)
    lent = (table >= 0) & (holder != row_id)
    lent_code = jnp.where(lent, row_id * SLOTS + (SLOTS - 1) - page_id, -1)
    lent_holder = jnp.where(lent, holder, -1)
    guest_code = [jnp.max(jnp.where(holder == z_peer[d], lent_code, -1)) for d in range(NZ)]
    lender = [jnp.max(jnp.where(row_id == y_peer[e], lent_holder, -1)) for e in range(NY)]

    own_length = len_smem[0, inst]
    own_row = jnp.broadcast_to(tab_ref[pl.ds(inst, 1), :] - inst * SLOTS, (SLOTS, SLOTS))
    slot_id = lax.broadcasted_iota(jnp.int32, (SLOTS, SLOTS), 0)
    page_of = lax.broadcasted_iota(jnp.int32, (SLOTS, SLOTS), 1)
    counted = jnp.clip(own_length - page_of * PAGE, 0, PAGE).astype(F32)
    valid = jnp.sum(jnp.where(own_row == slot_id, counted, 0.0), axis=1, keepdims=True)
    token = lax.broadcasted_iota(jnp.int32, (SLOTS, PAGE), 1).astype(F32)
    bias_buf[...] = jnp.where(token < valid, 0.0, NEG)

    guest = guest_code[0] >> 6
    first_page = (SLOTS - 1) - (guest_code[0] & (SLOTS - 1))
    guest_row = jnp.maximum(guest, 0)
    guest_length = jnp.where(guest >= 0, len_smem[0, guest_row], 0)
    guest_pages = ((guest_length + PAGE - 1) // PAGE) // 4
    page_token = lax.broadcasted_iota(jnp.int32, (1, PAGE), 1)
    slots = []
    limits = []
    for i in range(LENT):
        page = jnp.minimum(first_page + i, SLOTS - 1)
        slots.append(jnp.clip(tab_smem[guest_row, page] - inst * SLOTS, 0, SLOTS - 1))
        limits.append(jnp.where(i < guest_pages, guest_length - page * PAGE, 0))

    def scores_chunk(c, top):
        for p in range(CHUNK):
            slot = c * CHUNK + p
            s = lax.dot_general(query, k_buf[slot], NT_DIMS, preferred_element_type=F32)
            s = s + bias_buf[pl.ds(slot, 1), :]
            s_buf[c, :, p * PAGE:(p + 1) * PAGE] = s
            top = jnp.maximum(top, jnp.maximum(s[:, :HD], s[:, HD:]))
        return top

    def values_chunk(c, carry):
        total, numerator = carry
        half = CHUNK // 2
        for h in range(2):
            s = s_buf[c, :, h * half * PAGE:(h + 1) * half * PAGE]
            w = jnp.exp2(s * LOG2E_SCALE - own_top)
            total = total + lanes_sum(w)
            v = v_buf[pl.ds(c * CHUNK + h * half, half)].reshape(half * PAGE, HD)
            numerator = numerator + jnp.dot(w.astype(BF16), v, preferred_element_type=F32)
        return total, numerator

    per_part = CHUNKS // PARTS
    top = jnp.full((ROWS, HD), NEG, F32)
    for c in range(PARTS):
        k_copy(c).wait()
        top = lax.fori_loop(c * per_part, (c + 1) * per_part, scores_chunk, top)
    own_top = jnp.max(top, axis=1, keepdims=True) * LOG2E_SCALE

    def push(p, d, sent, received, slot, send_sem, recv_sem):
        return remote_copy(
            sent.at[p, d], received.at[slot], send_sem.at[p, d], recv_sem.at[slot], (z_peer[d], even_t + p))

    def push_all(p, source, pick, sent, received, slot, send_sem, recv_sem):
        for d in Z_ORDER + (0,):
            picked = source[pick(guest_code[d] >> 6)]
            if p == 1 and d == 0:
                received[slot] = picked
            else:
                sent[p, d] = picked
                push(p, d, sent, received, slot, send_sem, recv_sem).start()

    def push_done(sent, received, slot, send_sem, recv_sem):
        for p in range(2):
            for d in Z_ORDER + (0,) * (1 - p):
                push(p, d, sent, received, slot, send_sem, recv_sem).wait_send()

    @pl.when(early_relay)
    def _():
        for p in (1, 0):
            for e in Y_ORDER + (0,) * (1 - p):
                q1_row(p, e).wait_recv()
        pl.semaphore_wait(ready_sem, 2 * (NZ - EARLY))
        for p in FIRST_ORDER:
            push_all(
                p, (q_row_even, q_row_odd)[p], lambda r: (y - r) & (NY - 1),
                q_send_first, q_recv_first, row, qa_send_sem, qa_recv_sem)

    carry = (jnp.zeros((ROWS, HD), F32), jnp.zeros((ROWS, HD), F32))
    for c in range(PARTS):
        v_copy(c).wait()
        carry = lax.fori_loop(c * per_part, (c + 1) * per_part, values_chunk, carry)
    total, own_out = carry
    own_total = jnp.sum(total, axis=1, keepdims=True)

    @pl.when(home_relay)
    def _():
        for p in (1, 0):
            for j in range(GUESTS):
                for e in Y_ORDER + (0,):
                    slot = j * NY + e
                    remote_copy(
                        q_own, (q_late_even, q_late_odd)[p].at[slot], q1_send_sem.at[e], q1_late_sem.at[p, slot],
                        (inst, odd_t)).wait_recv()
            push_all(
                p, (q_late_even, q_late_odd)[p], lambda r: (((r >> 2) + 1) % GUESTS) * NY + ((y - r) & (NY - 1)),
                q_send_second, q_recv_second, home_place, qb_send_sem, qb_recv_sem)

    @pl.when(early_relay & (z == 0))
    def _():
        for d in (2, 4, 6):
            pl.semaphore_signal(plane_sem, inc=1, device_id=(inst, t_peer[d]), device_id_type=MESH)
        pl.semaphore_wait(plane_sem, NT // 2 - 1)
        for zz in range(EARLY, NZ):
            for which in (even_t, odd_t):
                pl.semaphore_signal(go_sem, inc=1, device_id=(at(zz, y), which), device_id_type=MESH)

    lane = lax.broadcasted_iota(jnp.int32, (ROWS, HD), 1)
    half_rows = ROWS // 2

    def lent_result(guest_query):
        guest_top = jnp.full((ROWS, HD), NEG, F32)
        for i in range(LENT):
            s = lax.dot_general(guest_query, k_buf[slots[i]], NT_DIMS, preferred_element_type=F32)
            s = jnp.where(page_token < limits[i], s, NEG)
            guest_buf[:, i * PAGE:(i + 1) * PAGE] = s
            guest_top = jnp.maximum(guest_top, jnp.maximum(s[:, :HD], s[:, HD:]))
        guest_top = jnp.max(guest_top, axis=1, keepdims=True) * LOG2E_SCALE
        total = jnp.zeros((ROWS, HD), F32)
        guest_out = jnp.zeros((ROWS, HD), F32)
        for i in range(LENT):
            s = guest_buf[:, i * PAGE:(i + 1) * PAGE]
            w = jnp.exp2(s * LOG2E_SCALE - guest_top)
            total = total + lanes_sum(w)
            guest_out = guest_out + jnp.dot(w.astype(BF16), v_buf[slots[i]], preferred_element_type=F32)
        guest_total = jnp.sum(total, axis=1, keepdims=True)
        level = jnp.broadcast_to(guest_top + jnp.log2(guest_total), (ROWS, HD))
        high = level.astype(BF16).astype(F32)
        middle = (level - high).astype(BF16).astype(F32)
        low = level - high - middle
        place = lane & 63
        coded = jnp.where(place == 0, high, jnp.where(place == 1, middle, jnp.where(place == 2, low, 0.0)))
        coded = jnp.where(lane[:half_rows] < 64, coded[:half_rows], coded[half_rows:])
        return jnp.concatenate([guest_out / guest_total, coded], axis=0).astype(BF16)

    p_relay = (p_relay_even, p_relay_odd)

    def send_result(own, wanted):
        for d in Z_ORDER:
            for p in range(2):
                @pl.when(wanted((z + d) % NZ) & (odd == p))
                def _():
                    relay_copy(own, p_relay, d, p, p1_send_sem, p1_recv_sem).start()

        @pl.when(wanted(z) & is_even)
        def _():
            relay_copy(own, p_relay, 0, 0, p1_send_sem, p1_recv_sem).start()

    def wait_arrival(received, slot, recv_sem, source):
        @pl.when(jnp.logical_not(is_relay & (z == source)))
        def _():
            remote_copy(
                received.at[slot], received.at[slot], recv_sem.at[slot], recv_sem.at[slot], (inst, odd_t)
            ).wait_recv()

    guest_z = guest_row >> 2
    for zz in range(EARLY):
        wait_arrival(q_recv_first, zz, qa_recv_sem, zz)
    result = lent_result(q_recv_first[jnp.minimum(guest_z, EARLY - 1)])
    p_own_first[...] = result
    send_result(p_own_first, lambda zz: zz < EARLY)

    @pl.when(early)
    def _():
        p_relay_odd[0] = result

    for j in range(2):
        wait_arrival(q_recv_second, j, qb_recv_sem, HOMES[j])
    result = lent_result(q_recv_second[jnp.where(guest_z >= 5, 0, 1)])
    p_own_second[...] = result
    send_result(p_own_second, lambda zz: zz >= EARLY)

    @pl.when(late)
    def _():
        p_relay_odd[0] = result
        pl.semaphore_wait(go_sem, 1)
        for copy in st_copies:
            copy.start()

    def relayed(relay, source, sent, received, arrive_sem, send_sem, recv_sem):
        @pl.when(is_relay)
        def _():
            for p in (1, 0):
                for d in Z_ORDER + (0,) * (1 - p):
                    relay_copy(sent.at[p, 0], relay, d, p, arrive_sem.at[p], arrive_sem).wait_recv()
                for e in Y_ORDER + (0,):
                    picked = relay[p][source[e]]
                    if p == 1 and e == 0:
                        received[0] = picked
                    else:
                        sent[p, e] = picked
                        remote_copy(
                            sent.at[p, e], received.at[e], send_sem.at[p, e], recv_sem.at[e], (y_peer[e], even_t + p)
                        ).start()

    def relay_done(sent, received, send_sem, recv_sem):
        for p in range(2):
            for e in Y_ORDER + (0,) * (1 - p):
                remote_copy(
                    sent.at[p, e], received.at[e], send_sem.at[p, e], recv_sem.at[e], (y_peer[e], even_t + p)
                ).wait_send()

    def arrived(received, recv_sem):
        for e in Y_ORDER:
            remote_copy(
                received.at[e], received.at[e], recv_sem.at[e], recv_sem.at[e], (y_peer[e], odd_t)
            ).wait_recv()

        @pl.when(jnp.logical_not(is_relay))
        def _():
            remote_copy(
                received.at[0], received.at[0], recv_sem.at[0], recv_sem.at[0], (inst, odd_t)
            ).wait_recv()

    relayed(
        p_relay, [(z - (lender[e] >> 2)) & (NZ - 1) for e in range(NY)], p_send, p_recv,
        p1_recv_sem, p2_send_sem, p2_recv_sem)
    for copy in w_copies:
        copy.wait()
    for copy in st_copies:
        copy.wait_recv()
    row16 = lax.broadcasted_iota(jnp.int32, (16, HD), 0) // STEPS

    def project(d, acc):
        source = (tensor - d + NT) % NT
        for h in range(2):
            x = st_all[d, h * 16:(h + 1) * 16, :].astype(F32)
            left = jnp.concatenate([jnp.where(row16 == g, x, 0.0) for g in range(4)], axis=1).astype(BF16)
            weight = jnp.concatenate(
                [kw_buf[source, h * 512:(h + 1) * 512, :], vw_buf[source, h * 512:(h + 1) * 512, :]], axis=1)
            acc = acc + jnp.dot(left, weight, preferred_element_type=F32)
        return acc

    acc = lax.fori_loop(0, NT, project, jnp.zeros((16, 2 * HD), F32))
    acc = acc[:8] + acc[8:]
    acc = acc[:4] + acc[4:]
    padded = jnp.concatenate([acc, jnp.zeros((12, 2 * HD), F32)], axis=0).astype(BF16)
    new_keys = padded[:, :HD]
    new_values = padded[:, HD:]
    s = lax.dot_general(query, new_keys, NT_DIMS, preferred_element_type=F32)
    step = lax.broadcasted_iota(jnp.int32, (ROWS, 16), 0) % STEPS
    other = lax.broadcasted_iota(jnp.int32, (ROWS, 16), 1)
    s = jnp.where(other <= step, s * LOG2E_SCALE, NEG)
    merged_top = jnp.maximum(own_top, jnp.max(s, axis=1, keepdims=True))
    w = jnp.exp2(s - merged_top)
    kept = jnp.exp2(own_top - merged_top)
    merged_total = own_total * kept + jnp.sum(w, axis=1, keepdims=True)
    merged_out = own_out * kept + jnp.dot(w.astype(BF16), new_values, preferred_element_type=F32)

    arrived(p_recv, p2_recv_sem)
    lent_part = p_recv[(y - lender[0]) & (NY - 1)].astype(F32)
    coded = lent_part[ROWS:]
    lane16 = lane[:half_rows]
    level = jnp.concatenate([
        jnp.sum(jnp.where(lane16 < 64, coded, 0.0), axis=1, keepdims=True),
        jnp.sum(jnp.where(lane16 < 64, 0.0, coded), axis=1, keepdims=True)], axis=0)
    level = jnp.where(lender[0] >= 0, level, NEG)
    highest = jnp.maximum(merged_top, level)
    kept = jnp.exp2(merged_top - highest)
    added = jnp.exp2(level - highest)
    out_ref[...] = (merged_out * kept + lent_part[:ROWS] * added) / (merged_total * kept + added)

    for copy in st_copies:
        copy.wait_send()
    for e in range(1, NY):
        q1_row(0, e).wait_send()

    @pl.when(late | is_even)
    def _():
        q1_row(0, 0).wait_send()

    for d in Z_ORDER:
        relay_copy(p_own_first, p_relay, d, 0, p1_send_sem, p1_recv_sem).wait_send()

    @pl.when(is_even)
    def _():
        relay_copy(p_own_first, p_relay, 0, 0, p1_send_sem, p1_recv_sem).wait_send()

    @pl.when(early_relay)
    def _():
        push_done(q_send_first, q_recv_first, row, qa_send_sem, qa_recv_sem)

    @pl.when(home_relay)
    def _():
        push_done(q_send_second, q_recv_second, home_place, qb_send_sem, qb_recv_sem)

    @pl.when(is_relay)
    def _():
        relay_done(p_send, p_recv, p2_send_sem, p2_recv_sem)


def on_device(queries, new_states, key_weight, value_weight, key_pool, value_pool, lengths, page_table):
    hbm = pl.BlockSpec(memory_space=pltpu.HBM)
    dma = pltpu.SemaphoreType.DMA

    def rows_of(x):
        return jnp.transpose(x.reshape(STEPS, GROUP, HD), (1, 0, 2)).reshape(ROWS, HD)

    out = pl.pallas_call(
        kernel,
        out_shape=pltpu.VMEM((ROWS, HD), F32),
        in_specs=[hbm] * 8,
        out_specs=pl.BlockSpec(memory_space=pltpu.VMEM),
        scratch_shapes=[
            pltpu.SMEM((1, 32), jnp.int32),
            pltpu.SMEM((32, SLOTS), jnp.int32),
            pltpu.VMEM((32, SLOTS), jnp.int32),
            pltpu.VMEM((SLOTS, PAGE, HD), BF16),
            pltpu.VMEM((SLOTS, PAGE, HD), BF16),
            pltpu.VMEM((NT, GROUP * HD, HD), BF16),
            pltpu.VMEM((NT, GROUP * HD, HD), BF16),
            pltpu.VMEM((CHUNKS, ROWS, CHUNK * PAGE), F32),
            pltpu.VMEM((ROWS, LENT * PAGE), F32),
            pltpu.VMEM((SLOTS, PAGE), F32),
            pltpu.VMEM((NT, ROWS, HD), BF16),
            pltpu.VMEM((ROWS, HD), BF16),
            pltpu.VMEM((NY, ROWS, HD), BF16),
            pltpu.VMEM((NY, ROWS, HD), BF16),
            pltpu.VMEM((GUESTS * NY, ROWS, HD), BF16),
            pltpu.VMEM((GUESTS * NY, ROWS, HD), BF16),
            pltpu.VMEM((2, NZ, ROWS, HD), BF16),
            pltpu.VMEM((2, NZ, ROWS, HD), BF16),
            pltpu.VMEM((EARLY, ROWS, HD), BF16),
            pltpu.VMEM((2, ROWS, HD), BF16),
            pltpu.VMEM((ROWS + 16, HD), BF16),
            pltpu.VMEM((ROWS + 16, HD), BF16),
            pltpu.VMEM((NZ, ROWS + 16, HD), BF16),
            pltpu.VMEM((NZ, ROWS + 16, HD), BF16),
            pltpu.VMEM((2, NY, ROWS + 16, HD), BF16),
            pltpu.VMEM((NY, ROWS + 16, HD), BF16),
            dma((5,)), dma((PARTS,)), dma((PARTS,)), dma((2,)), dma((NT,)), dma((NT,)),
            pltpu.SemaphoreType.REGULAR, pltpu.SemaphoreType.REGULAR, pltpu.SemaphoreType.REGULAR,
            dma((NY,)), dma((2, NY)), dma((2, GUESTS * NY)),
            dma((2, NZ)), dma((EARLY,)), dma((2, NZ)), dma((2,)),
            dma((NZ,)), dma((2, NZ)), dma((2, NY)), dma((NY,)),
        ],
        compiler_params=pltpu.CompilerParams(
            collective_id=0, has_side_effects=True, vmem_limit_bytes=VMEM_BYTES),
    )(
        lengths.reshape(1, -1), page_table, rows_of(queries), rows_of(new_states),
        key_weight.reshape(NT, GROUP * HD, HD), value_weight.reshape(NT, GROUP * HD, HD),
        key_pool, value_pool,
    )
    return (
        jnp.transpose(out.reshape(GROUP, STEPS, HD), (1, 0, 2))
        .reshape(1, STEPS, GROUP * HD)
        .astype(BF16)
    )


def solution(mesh):
    placed = (
        P("inst", None, "tensor"),
        P("inst", None, "tensor"),
        P(None, "tensor"),
        P(None, "tensor"),
        P("inst", None, "tensor"),
        P("inst", None, "tensor"),
        P(),
        P(),
    )
    return jax.shard_map(
        on_device, mesh=mesh, in_specs=placed, out_specs=P("inst", None, "tensor"), check_vma=False
    )
```

```python
import functools
import math

import jax
import jax.numpy as jnp
from jax import lax
from jax.experimental import pallas as pl
from jax.experimental.pallas import tpu as pltpu
from jax.sharding import PartitionSpec as P

HD = 128
STEPS = 4
GROUP = 8
ROWS = STEPS * GROUP
PAGE = 256
SLOTS = 64
CHUNK = 8
CHUNKS = SLOTS // CHUNK
PARTS = 4
PART = SLOTS // PARTS
LENT = 16
NY = 4
NZ = 8
NT = 8
EARLY = 2
HOMES = (0, 1)
GUESTS = 3
FIRST = 3
NEG = -1e30
VMEM_BYTES = 60 * 1024 * 1024
Z_ORDER = (4, 3, 5, 2, 6, 1, 7)
Y_ORDER = (2, 1, 3)
T_ORDER = (4, 5, 3, 2, 6, 7, 1)
LOG2E_SCALE = math.log2(math.e) / math.sqrt(HD)
F32 = jnp.float32
BF16 = jnp.bfloat16
MESH = pl.DeviceIdType.MESH
NT_DIMS = (((1,), (1,)), ((), ()))


def remote_copy(src, dst, send_sem, recv_sem, target):
    return pltpu.make_async_remote_copy(
        src_ref=src, dst_ref=dst, send_sem=send_sem, recv_sem=recv_sem, device_id=target, device_id_type=MESH)


def lanes_sum(w):
    total = w[:, :HD]
    for b in range(1, w.shape[1] // HD):
        total = total + w[:, b * HD:(b + 1) * HD]
    return total


def kernel(
    len_hbm, tab_hbm, q_hbm, st_hbm, kw_hbm, vw_hbm, k_hbm, v_hbm,
    out_ref,
    len_smem, tab_smem, tab_ref, k_buf, v_buf, kw_buf, vw_buf, s_buf, guest_buf, bias_buf, st_all,
    kt_buf, new_buf, own_buf, q_own, q_row_even, q_row_odd, q_mid_even, q_mid_odd, q_late_even, q_late_odd, q_send_first, q_send_second, q_recv_first, q_recv_second,
    p_own_first, p_own_second, p_relay_even, p_relay_odd, p_send, p_recv,
    small_sem, k_sem, v_sem, w_sem, st_send_sem, st_recv_sem, ready_sem, plane_sem, go_sem,
    q1_send_sem, q1_row_sem, q1_mid_sem, q1_late_sem, qa_send_sem, qa_recv_sem, qb_send_sem, qb_recv_sem,
    p1_send_sem, p1_recv_sem, p2_send_sem, p2_recv_sem,
):
    inst = lax.axis_index("inst")
    tensor = lax.axis_index("tensor")
    z = inst // NY
    y = inst % NY
    odd = tensor % 2
    even_t = tensor - odd
    odd_t = even_t + 1
    is_relay = odd == 1
    is_even = odd == 0
    early = z < EARLY
    late = z >= EARLY
    early_relay = early & is_relay
    home_relay = is_relay & ((z == HOMES[0]) | (z == HOMES[1]))
    row = jnp.minimum(z, EARLY - 1)
    home_place = jnp.where(z == HOMES[0], 0, 1)
    home_row = jnp.where(z >= 5, HOMES[0], HOMES[1])
    guests_from = jnp.where(z == HOMES[0], 5, 2)

    def at(zz, yy):
        return zz * NY + yy

    z_peer = [at((z + d) % NZ, y) for d in range(NZ)]
    ys = [(y + e) % NY for e in range(NY)]
    y_peer = [at(z, ys[e]) for e in range(NY)]
    t_peer = [(tensor + d) % NT for d in range(NT)]

    barrier = pltpu.get_barrier_semaphore()

    def greet(where, which):
        pl.semaphore_signal(barrier, inc=1, device_id=(where, which), device_id_type=MESH)

    @pl.when(late)
    def _():
        pl.semaphore_wait(barrier, EARLY + NY - 1)
        for c in range(EARLY):
            pl.semaphore_signal(
                ready_sem, inc=1, device_id=(at((z + c) % EARLY, y), odd_t), device_id_type=MESH)

    @pl.when(early_relay)
    def _():
        for zz in range(NZ - 1, EARLY - 1, -1):
            greet(at(zz, y), even_t)
            greet(at(zz, y), odd_t)

    @pl.when(home_relay)
    def _():
        for j in range(GUESTS):
            for e in Y_ORDER:
                greet(at(guests_from + j, ys[e]), even_t)
                greet(at(guests_from + j, ys[e]), odd_t)

    @pl.when(early)
    def _():
        for c in range(1, EARLY):
            greet(at((z + c) % EARLY, y), odd_t)

    @pl.when(z == 0)
    def _():
        for d in T_ORDER:
            greet(inst, t_peer[d])

    @pl.when(early_relay)
    def _():
        for e in Y_ORDER:
            greet(y_peer[e], even_t)
            greet(y_peer[e], odd_t)

    @pl.when(early_relay & (z > 0))
    def _():
        greet(inst, even_t)

    small_copies = [
        pltpu.make_async_copy(q_hbm, q_own, small_sem.at[0]),
        pltpu.make_async_copy(st_hbm, st_all.at[0], small_sem.at[1]),
        pltpu.make_async_copy(tab_hbm, tab_ref, small_sem.at[2]),
        pltpu.make_async_copy(len_hbm, len_smem, small_sem.at[3]),
        pltpu.make_async_copy(tab_hbm, tab_smem, small_sem.at[4]),
    ]
    for copy in small_copies:
        copy.start()

    def k_copy(c):
        part = pl.ds(c * PART, PART)
        return pltpu.make_async_copy(k_hbm.at[part], k_buf.at[part], k_sem.at[c])

    def v_copy(c):
        part = pl.ds(c * PART, PART)
        return pltpu.make_async_copy(v_hbm.at[part], v_buf.at[part], v_sem.at[c])

    w_copies = [
        pltpu.make_async_copy(kw_hbm, kw_buf, w_sem.at[0]),
        pltpu.make_async_copy(vw_hbm, vw_buf, w_sem.at[1]),
    ]

    @pl.when(early)
    def _():
        pl.semaphore_wait(
            barrier, NY - 1 + odd * 2 * (EARLY - 1) + jnp.where(z == 0, NT - 1, 1 - odd))

    small_copies[0].wait()

    def q1_copy(place, e, target):
        buffer, slot, sem = place
        return remote_copy(q_own, buffer.at[slot], q1_send_sem.at[e], sem.at[slot], (target, odd_t))

    def q1_row(p, e):
        return q1_copy(((q_row_even, q_row_odd)[p], e, q1_row_sem.at[p]), e, y_peer[e])

    def q1_mid(p, e):
        return q1_copy(((q_mid_even, q_mid_odd)[p], e, q1_mid_sem.at[p]), e, at(home_row, ys[e]))

    def q1_late(p, e):
        return q1_copy(
            ((q_late_even, q_late_odd)[p], ((z + 1) % GUESTS) * NY + e, q1_late_sem.at[p]), e, at(home_row, ys[e]))

    @pl.when(z == 0)
    def _():
        q_mid_even[...] = jnp.zeros_like(q_mid_even)
        q_mid_odd[...] = jnp.zeros_like(q_mid_odd)

    for p in range(2):
        @pl.when(early & (odd == p))
        def _():
            for e in Y_ORDER + (0,) * (1 - p):
                q1_row(p, e).start()

        @pl.when((z == EARLY) & (odd == p))
        def _():
            for e in Y_ORDER + (0,):
                q1_mid(p, e).start()

        @pl.when((z > EARLY) & (odd == p))
        def _():
            for e in Y_ORDER + (0,):
                q1_late(p, e).start()

    for c in range(PARTS):
        k_copy(c).start()
    for c in range(PARTS):
        v_copy(c).start()

    small_copies[1].wait()
    st_copies = [
        remote_copy(st_all.at[0], st_all.at[d], st_send_sem.at[d], st_recv_sem.at[d], (inst, t_peer[d]))
        for d in T_ORDER
    ]

    @pl.when(z == 0)
    def _():
        for copy in st_copies:
            copy.start()

    query = q_own[...]
    q_row_odd[0] = query

    def relay_copy(own, relay, d, p, send_sem, recv_sem):
        return remote_copy(own, relay[p].at[d], send_sem.at[d], recv_sem.at[p, d], (z_peer[d], odd_t))

    for copy in small_copies[2:]:
        copy.wait()
    table = tab_ref[...]
    holder = table >> 6
    row_id = lax.broadcasted_iota(jnp.int32, table.shape, 0)
    page_id = lax.broadcasted_iota(jnp.int32, table.shape, 1)
    lent = (table >= 0) & (holder != row_id)
    lent_code = jnp.where(lent, row_id * SLOTS + (SLOTS - 1) - page_id, -1)
    lent_holder = jnp.where(lent, holder, -1)
    guest_code = [jnp.max(jnp.where(holder == z_peer[d], lent_code, -1)) for d in range(NZ)]
    lender = [jnp.max(jnp.where(row_id == y_peer[e], lent_holder, -1)) for e in range(NY)]

    own_length = len_smem[0, inst]
    own_row = jnp.broadcast_to(tab_ref[pl.ds(inst, 1), :] - inst * SLOTS, (SLOTS, SLOTS))
    slot_id = lax.broadcasted_iota(jnp.int32, (SLOTS, SLOTS), 0)
    page_of = lax.broadcasted_iota(jnp.int32, (SLOTS, SLOTS), 1)
    counted = jnp.clip(own_length - page_of * PAGE, 0, PAGE).astype(F32)
    valid = jnp.sum(jnp.where(own_row == slot_id, counted, 0.0), axis=1, keepdims=True)
    token = lax.broadcasted_iota(jnp.int32, (SLOTS, PAGE), 1).astype(F32)
    bias_buf[...] = jnp.where(token < valid, 0.0, NEG)

    guest = guest_code[0] >> 6
    first_page = (SLOTS - 1) - (guest_code[0] & (SLOTS - 1))
    guest_row = jnp.maximum(guest, 0)
    guest_length = jnp.where(guest >= 0, len_smem[0, guest_row], 0)
    guest_pages = ((guest_length + PAGE - 1) // PAGE) // 4
    page_token = lax.broadcasted_iota(jnp.int32, (1, PAGE), 1)
    slots = []
    limits = []
    for i in range(LENT):
        page = jnp.minimum(first_page + i, SLOTS - 1)
        slots.append(jnp.clip(tab_smem[guest_row, page] - inst * SLOTS, 0, SLOTS - 1))
        limits.append(jnp.where(i < guest_pages, guest_length - page * PAGE, 0))

    def scores_chunk(c, top):
        for p in range(CHUNK):
            slot = c * CHUNK + p
            s = lax.dot_general(query, k_buf[slot], NT_DIMS, preferred_element_type=F32)
            s = s + bias_buf[pl.ds(slot, 1), :]
            s_buf[c, :, p * PAGE:(p + 1) * PAGE] = s
            top = jnp.maximum(top, jnp.maximum(s[:, :HD], s[:, HD:]))
        return top

    def values_chunk(c, carry):
        total, numerator = carry
        half = CHUNK // 2
        for h in range(2):
            s = s_buf[c, :, h * half * PAGE:(h + 1) * half * PAGE]
            w = jnp.exp2(s * LOG2E_SCALE - own_top)
            total = total + lanes_sum(w)
            v = v_buf[pl.ds(c * CHUNK + h * half, half)].reshape(half * PAGE, HD)
            numerator = numerator + jnp.dot(w.astype(BF16), v, preferred_element_type=F32)
        return total, numerator

    per_part = CHUNKS // PARTS
    top = jnp.full((ROWS, HD), NEG, F32)
    for c in range(PARTS):
        k_copy(c).wait()
        top = lax.fori_loop(c * per_part, (c + 1) * per_part, scores_chunk, top)
    own_top = jnp.max(top, axis=1, keepdims=True) * LOG2E_SCALE

    def pick_first(p, r):
        e = (y - r) & (NY - 1)
        return lax.select((r >> 2) == EARLY, (q_mid_even, q_mid_odd)[p][e], (q_row_even, q_row_odd)[p][e])

    def pick_second(p, r):
        return (q_late_even, q_late_odd)[p][(((r >> 2) + 1) % GUESTS) * NY + ((y - r) & (NY - 1))]

    def push(p, d, sent, received, slot, send_sem, recv_sem):
        return remote_copy(
            sent.at[p, d], received.at[slot], send_sem.at[p, d], recv_sem.at[slot], (z_peer[d], even_t + p))

    def push_all(p, pick, sent, received, slot, send_sem, recv_sem):
        for d in Z_ORDER + (0,):
            picked = pick(guest_code[d] >> 6)
            if p == 1 and d == 0:
                received[slot] = picked
            else:
                sent[p, d] = picked
                push(p, d, sent, received, slot, send_sem, recv_sem).start()

    def push_done(sent, received, slot, send_sem, recv_sem):
        for p in range(2):
            for d in Z_ORDER + (0,) * (1 - p):
                push(p, d, sent, received, slot, send_sem, recv_sem).wait_send()

    for copy in w_copies:
        copy.start()

    @pl.when(early_relay)
    def _():
        for p in (1, 0):
            for e in Y_ORDER + (0,) * (1 - p):
                q1_row(p, e).wait_recv()

        @pl.when(z == HOMES[1])
        def _():
            for p in (1, 0):
                for e in Y_ORDER + (0,):
                    q1_mid(p, e).wait_recv()

        for p in range(2):
            for d in range(NZ):
                picked = pick_first(p, guest_code[d] >> 6)
                if p == 1 and d == 0:
                    q_recv_first[row] = picked
                else:
                    q_send_first[p, d] = picked
        pl.semaphore_wait(ready_sem, 2 * (NZ - EARLY))
        for d in Z_ORDER + (0,):
            for p in range(2 if d else 1):
                push(p, d, q_send_first, q_recv_first, row, qa_send_sem, qa_recv_sem).start()

    @pl.when(early_relay & (z == 0))
    def _():
        for d in (2, 4, 6):
            pl.semaphore_signal(plane_sem, inc=1, device_id=(inst, t_peer[d]), device_id_type=MESH)

    def own_values():
        total, numerator = lax.fori_loop(
            0, CHUNKS, values_chunk, (jnp.zeros((ROWS, HD), F32), jnp.zeros((ROWS, HD), F32)))
        own_buf[0] = total
        own_buf[1] = numerator

    for c in range(PARTS):
        v_copy(c).wait()
    pl.when(early)(own_values)

    @pl.when(home_relay)
    def _():
        for p in (1, 0):
            for j in range(GUESTS):
                @pl.when((z == HOMES[0]) | (j > 0))
                def _():
                    for e in Y_ORDER + (0,):
                        slot = j * NY + e
                        remote_copy(
                            q_own, (q_late_even, q_late_odd)[p].at[slot], q1_send_sem.at[e],
                            q1_late_sem.at[p, slot], (inst, odd_t)).wait_recv()

            push_all(
                p, functools.partial(pick_second, p),
                q_send_second, q_recv_second, home_place, qb_send_sem, qb_recv_sem)

    lane = lax.broadcasted_iota(jnp.int32, (ROWS, HD), 1)
    half_rows = ROWS // 2

    def lent_result(guest_query):
        guest_top = jnp.full((ROWS, HD), NEG, F32)
        for i in range(LENT):
            s = jnp.dot(guest_query, kt_buf[:, i * PAGE:(i + 1) * PAGE], preferred_element_type=F32)
            s = jnp.where(page_token < limits[i], s, NEG)
            guest_buf[:, i * PAGE:(i + 1) * PAGE] = s
            guest_top = jnp.maximum(guest_top, jnp.maximum(s[:, :HD], s[:, HD:]))
        guest_top = jnp.max(guest_top, axis=1, keepdims=True) * LOG2E_SCALE
        total = jnp.zeros((ROWS, HD), F32)
        guest_out = jnp.zeros((ROWS, HD), F32)
        for i in range(LENT):
            s = guest_buf[:, i * PAGE:(i + 1) * PAGE]
            w = jnp.exp2(s * LOG2E_SCALE - guest_top)
            total = total + lanes_sum(w)
            guest_out = guest_out + jnp.dot(w.astype(BF16), v_buf[slots[i]], preferred_element_type=F32)
        guest_total = jnp.sum(total, axis=1, keepdims=True)
        level = jnp.broadcast_to(guest_top + jnp.log2(guest_total), (ROWS, HD))
        high = level.astype(BF16).astype(F32)
        middle = (level - high).astype(BF16).astype(F32)
        low = level - high - middle
        place = lane & 63
        coded = jnp.where(place == 0, high, jnp.where(place == 1, middle, jnp.where(place == 2, low, 0.0)))
        coded = jnp.where(lane[:half_rows] < 64, coded[:half_rows], coded[half_rows:])
        return jnp.concatenate([guest_out / guest_total, coded], axis=0).astype(BF16)

    p_relay = (p_relay_even, p_relay_odd)

    def result_copy(own, zz, p):
        slot = (zz - z) & (NZ - 1)
        return remote_copy(
            own, p_relay[p].at[slot], p1_send_sem.at[zz], p1_recv_sem.at[p, slot], (at(zz, y), odd_t))

    def send_result(own, rows):
        @pl.when(is_even)
        def _():
            for zz in rows:
                result_copy(own, zz, 0).start()

        for zz in rows:
            @pl.when(is_relay & (z != zz))
            def _():
                result_copy(own, zz, 1).start()

    def wait_arrival(received, slot, recv_sem, source):
        @pl.when(jnp.logical_not(is_relay & (z == source)))
        def _():
            remote_copy(
                received.at[slot], received.at[slot], recv_sem.at[slot], recv_sem.at[slot], (inst, odd_t)
            ).wait_recv()

    guest_z = guest_row >> 2
    for i in range(LENT):
        kt_buf[:, i * PAGE:(i + 1) * PAGE] = k_buf[slots[i]].T

    @pl.when(early_relay & (z == 0))
    def _():
        pl.semaphore_wait(plane_sem, NT // 2 - 1)
        for zz in range(1, NZ):
            for which in (even_t, odd_t):
                pl.semaphore_signal(go_sem, inc=1, device_id=(at(zz, y), which), device_id_type=MESH)

    for zz in range(EARLY):
        wait_arrival(q_recv_first, zz, qa_recv_sem, zz)
    result = lent_result(q_recv_first[jnp.minimum(guest_z, EARLY - 1)])
    p_own_first[...] = result
    send_result(p_own_first, range(FIRST))

    @pl.when(z < FIRST)
    def _():
        p_relay_odd[0] = result

    pl.when(late)(own_values)
    for j in range(2):
        wait_arrival(q_recv_second, j, qb_recv_sem, HOMES[j])
    result = lent_result(q_recv_second[jnp.where(guest_z >= 5, 0, 1)])
    p_own_second[...] = result
    send_result(p_own_second, range(FIRST, NZ))

    @pl.when(z >= FIRST)
    def _():
        p_relay_odd[0] = result

    @pl.when(z > 0)
    def _():
        pl.semaphore_wait(go_sem, 1)
        for copy in st_copies:
            copy.start()

    def project_all():
        for copy in w_copies:
            copy.wait()
        for copy in st_copies:
            copy.wait_recv()
        row16 = lax.broadcasted_iota(jnp.int32, (16, HD), 0) // STEPS

        def project(d, acc):
            source = (tensor - d + NT) % NT
            for h in range(2):
                x = st_all[d, h * 16:(h + 1) * 16, :].astype(F32)
                left = jnp.concatenate([jnp.where(row16 == g, x, 0.0) for g in range(4)], axis=1).astype(BF16)
                weight = jnp.concatenate(
                    [kw_buf[source, h * 512:(h + 1) * 512, :], vw_buf[source, h * 512:(h + 1) * 512, :]], axis=1)
                acc = acc + jnp.dot(left, weight, preferred_element_type=F32)
            return acc

        acc = lax.fori_loop(0, NT, project, jnp.zeros((16, 2 * HD), F32))
        acc = acc[:8] + acc[8:]
        acc = acc[:4] + acc[4:]
        new_buf[...] = jnp.concatenate([acc, jnp.zeros((12, 2 * HD), F32)], axis=0).astype(BF16)

    pl.when(z == 0)(project_all)

    def relayed(relay, source, sent, received, arrive_sem, send_sem, recv_sem):
        @pl.when(is_relay)
        def _():
            for p in (1, 0):
                for d in Z_ORDER + (0,) * (1 - p):
                    relay_copy(sent.at[p, 0], relay, d, p, arrive_sem.at[p], arrive_sem).wait_recv()
                for e in Y_ORDER + (0,):
                    picked = relay[p][source[e]]
                    if p == 1 and e == 0:
                        received[0] = picked
                    else:
                        sent[p, e] = picked
                        remote_copy(
                            sent.at[p, e], received.at[e], send_sem.at[p, e], recv_sem.at[e], (y_peer[e], even_t + p)
                        ).start()

    def relay_done(sent, received, send_sem, recv_sem):
        for p in range(2):
            for e in Y_ORDER + (0,) * (1 - p):
                remote_copy(
                    sent.at[p, e], received.at[e], send_sem.at[p, e], recv_sem.at[e], (y_peer[e], even_t + p)
                ).wait_send()

    def arrived(received, recv_sem):
        for e in Y_ORDER:
            remote_copy(
                received.at[e], received.at[e], recv_sem.at[e], recv_sem.at[e], (y_peer[e], odd_t)
            ).wait_recv()

        @pl.when(jnp.logical_not(is_relay))
        def _():
            remote_copy(
                received.at[0], received.at[0], recv_sem.at[0], recv_sem.at[0], (inst, odd_t)
            ).wait_recv()

    relayed(
        p_relay, [(z - (lender[e] >> 2)) & (NZ - 1) for e in range(NY)], p_send, p_recv,
        p1_recv_sem, p2_send_sem, p2_recv_sem)
    pl.when(z > 0)(project_all)
    own_total = jnp.sum(own_buf[0], axis=1, keepdims=True)
    own_out = own_buf[1]
    new_keys = new_buf[:, :HD]
    new_values = new_buf[:, HD:]
    s = lax.dot_general(query, new_keys, NT_DIMS, preferred_element_type=F32)
    step = lax.broadcasted_iota(jnp.int32, (ROWS, 16), 0) % STEPS
    other = lax.broadcasted_iota(jnp.int32, (ROWS, 16), 1)
    s = jnp.where(other <= step, s * LOG2E_SCALE, NEG)
    merged_top = jnp.maximum(own_top, jnp.max(s, axis=1, keepdims=True))
    w = jnp.exp2(s - merged_top)
    kept = jnp.exp2(own_top - merged_top)
    merged_total = own_total * kept + jnp.sum(w, axis=1, keepdims=True)
    merged_out = own_out * kept + jnp.dot(w.astype(BF16), new_values, preferred_element_type=F32)

    arrived(p_recv, p2_recv_sem)
    lent_part = p_recv[(y - lender[0]) & (NY - 1)].astype(F32)
    coded = lent_part[ROWS:]
    lane16 = lane[:half_rows]
    level = jnp.concatenate([
        jnp.sum(jnp.where(lane16 < 64, coded, 0.0), axis=1, keepdims=True),
        jnp.sum(jnp.where(lane16 < 64, 0.0, coded), axis=1, keepdims=True)], axis=0)
    level = jnp.where(lender[0] >= 0, level, NEG)
    highest = jnp.maximum(merged_top, level)
    kept = jnp.exp2(merged_top - highest)
    added = jnp.exp2(level - highest)
    out_ref[...] = (merged_out * kept + lent_part[:ROWS] * added) / (merged_total * kept + added)

    for copy in st_copies:
        copy.wait_send()
    for e in range(1, NY):
        q1_row(0, e).wait_send()

    @pl.when(late | is_even)
    def _():
        q1_row(0, 0).wait_send()

    for zz in range(NZ):
        @pl.when(is_even | (z != zz))
        def _():
            result_copy(p_own_first, zz, 0).wait_send()

    @pl.when(early_relay)
    def _():
        push_done(q_send_first, q_recv_first, row, qa_send_sem, qa_recv_sem)

    @pl.when(home_relay)
    def _():
        push_done(q_send_second, q_recv_second, home_place, qb_send_sem, qb_recv_sem)

    @pl.when(is_relay)
    def _():
        relay_done(p_send, p_recv, p2_send_sem, p2_recv_sem)


def on_device(queries, new_states, key_weight, value_weight, key_pool, value_pool, lengths, page_table):
    hbm = pl.BlockSpec(memory_space=pltpu.HBM)
    dma = pltpu.SemaphoreType.DMA

    def rows_of(x):
        return jnp.transpose(x.reshape(STEPS, GROUP, HD), (1, 0, 2)).reshape(ROWS, HD)

    out = pl.pallas_call(
        kernel,
        out_shape=pltpu.VMEM((ROWS, HD), F32),
        in_specs=[hbm] * 8,
        out_specs=pl.BlockSpec(memory_space=pltpu.VMEM),
        scratch_shapes=[
            pltpu.SMEM((1, 32), jnp.int32),
            pltpu.SMEM((32, SLOTS), jnp.int32),
            pltpu.VMEM((32, SLOTS), jnp.int32),
            pltpu.VMEM((SLOTS, PAGE, HD), BF16),
            pltpu.VMEM((SLOTS, PAGE, HD), BF16),
            pltpu.VMEM((NT, GROUP * HD, HD), BF16),
            pltpu.VMEM((NT, GROUP * HD, HD), BF16),
            pltpu.VMEM((CHUNKS, ROWS, CHUNK * PAGE), F32),
            pltpu.VMEM((ROWS, LENT * PAGE), F32),
            pltpu.VMEM((SLOTS, PAGE), F32),
            pltpu.VMEM((NT, ROWS, HD), BF16),
            pltpu.VMEM((HD, LENT * PAGE), BF16),
            pltpu.VMEM((16, 2 * HD), BF16),
            pltpu.VMEM((2, ROWS, HD), F32),
            pltpu.VMEM((ROWS, HD), BF16),
            pltpu.VMEM((NY, ROWS, HD), BF16),
            pltpu.VMEM((NY, ROWS, HD), BF16),
            pltpu.VMEM((NY, ROWS, HD), BF16),
            pltpu.VMEM((NY, ROWS, HD), BF16),
            pltpu.VMEM((GUESTS * NY, ROWS, HD), BF16),
            pltpu.VMEM((GUESTS * NY, ROWS, HD), BF16),
            pltpu.VMEM((2, NZ, ROWS, HD), BF16),
            pltpu.VMEM((2, NZ, ROWS, HD), BF16),
            pltpu.VMEM((EARLY, ROWS, HD), BF16),
            pltpu.VMEM((2, ROWS, HD), BF16),
            pltpu.VMEM((ROWS + 16, HD), BF16),
            pltpu.VMEM((ROWS + 16, HD), BF16),
            pltpu.VMEM((NZ, ROWS + 16, HD), BF16),
            pltpu.VMEM((NZ, ROWS + 16, HD), BF16),
            pltpu.VMEM((2, NY, ROWS + 16, HD), BF16),
            pltpu.VMEM((NY, ROWS + 16, HD), BF16),
            dma((5,)), dma((PARTS,)), dma((PARTS,)), dma((2,)), dma((NT,)), dma((NT,)),
            pltpu.SemaphoreType.REGULAR, pltpu.SemaphoreType.REGULAR, pltpu.SemaphoreType.REGULAR,
            dma((NY,)), dma((2, NY)), dma((2, NY)), dma((2, GUESTS * NY)),
            dma((2, NZ)), dma((EARLY,)), dma((2, NZ)), dma((2,)),
            dma((NZ,)), dma((2, NZ)), dma((2, NY)), dma((NY,)),
        ],
        compiler_params=pltpu.CompilerParams(
            collective_id=0, has_side_effects=True, vmem_limit_bytes=VMEM_BYTES),
    )(
        lengths.reshape(1, -1), page_table, rows_of(queries), rows_of(new_states),
        key_weight.reshape(NT, GROUP * HD, HD), value_weight.reshape(NT, GROUP * HD, HD),
        key_pool, value_pool,
    )
    return (
        jnp.transpose(out.reshape(GROUP, STEPS, HD), (1, 0, 2))
        .reshape(1, STEPS, GROUP * HD)
        .astype(BF16)
    )


def solution(mesh):
    placed = (
        P("inst", None, "tensor"),
        P("inst", None, "tensor"),
        P(None, "tensor"),
        P(None, "tensor"),
        P("inst", None, "tensor"),
        P("inst", None, "tensor"),
        P(),
        P(),
    )
    return jax.shard_map(
        on_device, mesh=mesh, in_specs=placed, out_specs=P("inst", None, "tensor"), check_vma=False
    )
```

```python
import functools
import math

import jax
import jax.numpy as jnp
from jax import lax
from jax.experimental import pallas as pl
from jax.experimental.pallas import tpu as pltpu
from jax.sharding import PartitionSpec as P

HD = 128
STEPS = 4
GROUP = 8
ROWS = STEPS * GROUP
PAGE = 256
SLOTS = 64
CHUNK = 8
CHUNKS = SLOTS // CHUNK
PARTS = 4
PART = SLOTS // PARTS
LENT = 16
NY = 4
NZ = 8
NT = 8
EARLY = 2
HOMES = (0, 1)
GUESTS = 3
FIRST = 3
NEG = -1e30
VMEM_BYTES = 60 * 1024 * 1024
Z_ORDER = (4, 3, 5, 2, 6, 1, 7)
Y_ORDER = (2, 1, 3)
T_ORDER = (4, 5, 3, 2, 6, 7, 1)
LOG2E_SCALE = math.log2(math.e) / math.sqrt(HD)
F32 = jnp.float32
BF16 = jnp.bfloat16
MESH = pl.DeviceIdType.MESH
NT_DIMS = (((1,), (1,)), ((), ()))


def remote_copy(src, dst, send_sem, recv_sem, target):
    return pltpu.make_async_remote_copy(
        src_ref=src, dst_ref=dst, send_sem=send_sem, recv_sem=recv_sem, device_id=target, device_id_type=MESH)


def lanes_sum(w):
    total = w[:, :HD]
    for b in range(1, w.shape[1] // HD):
        total = total + w[:, b * HD:(b + 1) * HD]
    return total


def kernel(
    len_hbm, tab_hbm, q_hbm, st_hbm, kw_hbm, vw_hbm, k_hbm, v_hbm,
    out_ref,
    len_smem, tab_smem, tab_ref, k_buf, v_buf, kw_buf, vw_buf, s_buf, guest_buf, bias_buf, st_all,
    kt_buf, vl_buf, lent_bias, new_buf, own_buf, q_own, q_row_even, q_row_odd, q_mid_even, q_mid_odd, q_late_even, q_late_odd, q_send_first, q_send_second, q_recv_first, q_recv_second,
    p_own_first, p_own_second, p_relay_even, p_relay_odd, p_send, p_recv,
    small_sem, k_sem, v_sem, w_sem, st_send_sem, st_recv_sem, ready_sem, plane_sem, go_sem,
    q1_send_sem, q1_row_sem, q1_mid_sem, q1_late_sem, qa_send_sem, qa_recv_sem, qb_send_sem, qb_recv_sem,
    p1_send_sem, p1_recv_sem, p2_send_sem, p2_recv_sem,
):
    inst = lax.axis_index("inst")
    tensor = lax.axis_index("tensor")
    z = inst // NY
    y = inst % NY
    odd = tensor % 2
    even_t = tensor - odd
    odd_t = even_t + 1
    is_relay = odd == 1
    is_even = odd == 0
    early = z < EARLY
    late = z >= EARLY
    early_relay = early & is_relay
    home_relay = is_relay & ((z == HOMES[0]) | (z == HOMES[1]))
    row = jnp.minimum(z, EARLY - 1)
    home_place = jnp.where(z == HOMES[0], 0, 1)
    home_row = jnp.where(z >= 5, HOMES[0], HOMES[1])
    guests_from = jnp.where(z == HOMES[0], 5, 2)

    def at(zz, yy):
        return zz * NY + yy

    z_peer = [at((z + d) % NZ, y) for d in range(NZ)]
    ys = [(y + e) % NY for e in range(NY)]
    y_peer = [at(z, ys[e]) for e in range(NY)]
    t_peer = [(tensor + d) % NT for d in range(NT)]

    barrier = pltpu.get_barrier_semaphore()

    def greet(where, which):
        pl.semaphore_signal(barrier, inc=1, device_id=(where, which), device_id_type=MESH)

    @pl.when(late)
    def _():
        pl.semaphore_wait(barrier, EARLY + NY - 1)
        for c in range(EARLY):
            pl.semaphore_signal(
                ready_sem.at[odd], inc=1, device_id=(at((z + c) % EARLY, y), odd_t), device_id_type=MESH)

    @pl.when(early_relay)
    def _():
        for zz in range(NZ - 1, EARLY - 1, -1):
            greet(at(zz, y), even_t)
            greet(at(zz, y), odd_t)

    @pl.when(home_relay)
    def _():
        for j in range(GUESTS):
            for e in Y_ORDER:
                greet(at(guests_from + j, ys[e]), even_t)
                greet(at(guests_from + j, ys[e]), odd_t)

    @pl.when(early)
    def _():
        for c in range(1, EARLY):
            greet(at((z + c) % EARLY, y), odd_t)

    @pl.when(z == 0)
    def _():
        for d in T_ORDER:
            greet(inst, t_peer[d])

    @pl.when(early_relay)
    def _():
        for e in Y_ORDER:
            greet(y_peer[e], even_t)
            greet(y_peer[e], odd_t)

    @pl.when(early_relay & (z > 0))
    def _():
        greet(inst, even_t)

    small_copies = [
        pltpu.make_async_copy(q_hbm, q_own, small_sem.at[0]),
        pltpu.make_async_copy(st_hbm, st_all.at[0], small_sem.at[1]),
        pltpu.make_async_copy(tab_hbm, tab_ref, small_sem.at[2]),
        pltpu.make_async_copy(len_hbm, len_smem, small_sem.at[3]),
        pltpu.make_async_copy(tab_hbm, tab_smem, small_sem.at[4]),
    ]
    for copy in small_copies:
        copy.start()

    def k_copy(c):
        part = pl.ds(c * PART, PART)
        return pltpu.make_async_copy(k_hbm.at[part], k_buf.at[part], k_sem.at[c])

    def v_copy(c):
        part = pl.ds(c * PART, PART)
        return pltpu.make_async_copy(v_hbm.at[part], v_buf.at[part], v_sem.at[c])

    w_copies = [
        pltpu.make_async_copy(kw_hbm, kw_buf, w_sem.at[0]),
        pltpu.make_async_copy(vw_hbm, vw_buf, w_sem.at[1]),
    ]

    @pl.when(early)
    def _():
        pl.semaphore_wait(
            barrier, NY - 1 + odd * 2 * (EARLY - 1) + jnp.where(z == 0, NT - 1, 1 - odd))

    small_copies[0].wait()

    def q1_copy(place, e, target):
        buffer, slot, sem = place
        return remote_copy(q_own, buffer.at[slot], q1_send_sem.at[e], sem.at[slot], (target, odd_t))

    def q1_row(p, e):
        return q1_copy(((q_row_even, q_row_odd)[p], e, q1_row_sem.at[p]), e, y_peer[e])

    def q1_mid(p, e):
        return q1_copy(((q_mid_even, q_mid_odd)[p], e, q1_mid_sem.at[p]), e, at(home_row, ys[e]))

    def q1_late(p, e):
        return q1_copy(
            ((q_late_even, q_late_odd)[p], ((z + 1) % GUESTS) * NY + e, q1_late_sem.at[p]), e, at(home_row, ys[e]))

    @pl.when(z == 0)
    def _():
        q_mid_even[...] = jnp.zeros_like(q_mid_even)
        q_mid_odd[...] = jnp.zeros_like(q_mid_odd)

    for p in range(2):
        @pl.when(early & (odd == p))
        def _():
            for e in Y_ORDER + (0,) * (1 - p):
                q1_row(p, e).start()

        @pl.when((z == EARLY) & (odd == p))
        def _():
            for e in Y_ORDER + (0,):
                q1_mid(p, e).start()

        @pl.when((z > EARLY) & (odd == p))
        def _():
            for e in Y_ORDER + (0,):
                q1_late(p, e).start()

    for c in range(PARTS):
        k_copy(c).start()
    for c in range(PARTS):
        v_copy(c).start()

    small_copies[1].wait()
    st_copies = [
        remote_copy(st_all.at[0], st_all.at[d], st_send_sem.at[d], st_recv_sem.at[d], (inst, t_peer[d]))
        for d in T_ORDER
    ]

    @pl.when(z == 0)
    def _():
        for copy in st_copies:
            copy.start()

    query = q_own[...]
    q_row_odd[0] = query

    def relay_copy(own, relay, d, p, send_sem, recv_sem):
        return remote_copy(own, relay[p].at[d], send_sem.at[d], recv_sem.at[p, d], (z_peer[d], odd_t))

    for copy in small_copies[2:]:
        copy.wait()
    table = tab_ref[...]
    holder = table >> 6
    row_id = lax.broadcasted_iota(jnp.int32, table.shape, 0)
    page_id = lax.broadcasted_iota(jnp.int32, table.shape, 1)
    lent = (table >= 0) & (holder != row_id)
    lent_code = jnp.where(lent, row_id * SLOTS + (SLOTS - 1) - page_id, -1)
    lent_holder = jnp.where(lent, holder, -1)
    guest_code = [jnp.max(jnp.where(holder == z_peer[d], lent_code, -1)) for d in range(NZ)]
    lender = [jnp.max(jnp.where(row_id == y_peer[e], lent_holder, -1)) for e in range(NY)]

    own_length = len_smem[0, inst]
    own_row = jnp.broadcast_to(tab_ref[pl.ds(inst, 1), :] - inst * SLOTS, (SLOTS, SLOTS))
    slot_id = lax.broadcasted_iota(jnp.int32, (SLOTS, SLOTS), 0)
    page_of = lax.broadcasted_iota(jnp.int32, (SLOTS, SLOTS), 1)
    counted = jnp.clip(own_length - page_of * PAGE, 0, PAGE).astype(F32)
    valid = jnp.sum(jnp.where(own_row == slot_id, counted, 0.0), axis=1, keepdims=True)
    token = lax.broadcasted_iota(jnp.int32, (SLOTS, PAGE), 1).astype(F32)
    bias_buf[...] = jnp.where(token < valid, 0.0, NEG)

    guest = guest_code[0] >> 6
    first_page = (SLOTS - 1) - (guest_code[0] & (SLOTS - 1))
    guest_row = jnp.maximum(guest, 0)
    guest_length = jnp.where(guest >= 0, len_smem[0, guest_row], 0)
    guest_pages = ((guest_length + PAGE - 1) // PAGE) // 4
    page_token = lax.broadcasted_iota(jnp.int32, (1, PAGE), 1)
    slots = []
    limits = []
    for i in range(LENT):
        page = jnp.minimum(first_page + i, SLOTS - 1)
        slots.append(jnp.clip(tab_smem[guest_row, page] - inst * SLOTS, 0, SLOTS - 1))
        limits.append(jnp.where(i < guest_pages, guest_length - page * PAGE, 0))

    def scores_chunk(c, top):
        for p in range(CHUNK):
            slot = c * CHUNK + p
            s = lax.dot_general(query, k_buf[slot], NT_DIMS, preferred_element_type=F32)
            s = s + bias_buf[pl.ds(slot, 1), :]
            s_buf[c, :, p * PAGE:(p + 1) * PAGE] = s
            top = jnp.maximum(top, jnp.maximum(s[:, :HD], s[:, HD:]))
        return top

    def values_chunk(c, carry):
        total, numerator = carry
        half = CHUNK // 2
        for h in range(2):
            s = s_buf[c, :, h * half * PAGE:(h + 1) * half * PAGE]
            w = jnp.exp2(s * LOG2E_SCALE - own_top)
            total = total + lanes_sum(w)
            v = v_buf[pl.ds(c * CHUNK + h * half, half)].reshape(half * PAGE, HD)
            numerator = numerator + jnp.dot(w.astype(BF16), v, preferred_element_type=F32)
        return total, numerator

    per_part = CHUNKS // PARTS
    top = jnp.full((ROWS, HD), NEG, F32)
    for c in range(PARTS):
        k_copy(c).wait()
        top = lax.fori_loop(c * per_part, (c + 1) * per_part, scores_chunk, top)
    own_top = jnp.max(top, axis=1, keepdims=True) * LOG2E_SCALE

    def pick_first(p, r):
        e = (y - r) & (NY - 1)
        return lax.select((r >> 2) == EARLY, (q_mid_even, q_mid_odd)[p][e], (q_row_even, q_row_odd)[p][e])

    def pick_second(p, r):
        return (q_late_even, q_late_odd)[p][(((r >> 2) + 1) % GUESTS) * NY + ((y - r) & (NY - 1))]

    def push(p, d, sent, received, slot, send_sem, recv_sem):
        return remote_copy(
            sent.at[p, d], received.at[slot], send_sem.at[p, d], recv_sem.at[slot], (z_peer[d], even_t + p))

    def push_all(p, pick, sent, received, slot, send_sem, recv_sem):
        for d in Z_ORDER + (0,):
            picked = pick(guest_code[d] >> 6)
            if p == 1 and d == 0:
                received[slot] = picked
            else:
                sent[p, d] = picked
                push(p, d, sent, received, slot, send_sem, recv_sem).start()

    def push_done(sent, received, slot, send_sem, recv_sem):
        for p in range(2):
            for d in Z_ORDER + (0,) * (1 - p):
                push(p, d, sent, received, slot, send_sem, recv_sem).wait_send()

    for copy in w_copies:
        copy.start()

    @pl.when(early_relay)
    def _():
        for p in (1, 0):
            for e in Y_ORDER + (0,) * (1 - p):
                q1_row(p, e).wait_recv()

        @pl.when(z == HOMES[1])
        def _():
            for p in (1, 0):
                for e in Y_ORDER + (0,):
                    q1_mid(p, e).wait_recv()

        for p in range(2):
            for d in range(NZ):
                picked = pick_first(p, guest_code[d] >> 6)
                if p == 1 and d == 0:
                    q_recv_first[row] = picked
                else:
                    q_send_first[p, d] = picked
        for p in (1, 0):
            pl.semaphore_wait(ready_sem.at[p], NZ - EARLY)
            for d in Z_ORDER + (0,) * (1 - p):
                push(p, d, q_send_first, q_recv_first, row, qa_send_sem, qa_recv_sem).start()

    @pl.when(early_relay & (z == 0))
    def _():
        for d in (2, 4, 6):
            pl.semaphore_signal(plane_sem, inc=1, device_id=(inst, t_peer[d]), device_id_type=MESH)

    def own_values():
        total, numerator = lax.fori_loop(
            0, CHUNKS, values_chunk, (jnp.zeros((ROWS, HD), F32), jnp.zeros((ROWS, HD), F32)))
        own_buf[0] = total
        own_buf[1] = numerator

    for c in range(PARTS):
        v_copy(c).wait()
    pl.when(early)(own_values)

    @pl.when(home_relay)
    def _():
        for p in (1, 0):
            for j in range(GUESTS):
                @pl.when((z == HOMES[0]) | (j > 0))
                def _():
                    for e in Y_ORDER + (0,):
                        slot = j * NY + e
                        remote_copy(
                            q_own, (q_late_even, q_late_odd)[p].at[slot], q1_send_sem.at[e],
                            q1_late_sem.at[p, slot], (inst, odd_t)).wait_recv()

            push_all(
                p, functools.partial(pick_second, p),
                q_send_second, q_recv_second, home_place, qb_send_sem, qb_recv_sem)

    lane = lax.broadcasted_iota(jnp.int32, (ROWS, HD), 1)
    half_rows = ROWS // 2

    def lent_result(guest_query):
        tops = []
        for i in range(LENT):
            s = jnp.dot(guest_query, kt_buf[:, i * PAGE:(i + 1) * PAGE], preferred_element_type=F32)
            s = s + lent_bias[i:i + 1, :]
            guest_buf[:, i * PAGE:(i + 1) * PAGE] = s
            tops.append(jnp.maximum(s[:, :HD], s[:, HD:]))
        while len(tops) > 1:
            tops = [jnp.maximum(m, n) for m, n in zip(tops[::2], tops[1::2])]
        guest_top = jnp.max(tops[0], axis=1, keepdims=True) * LOG2E_SCALE
        totals = []
        guest_out = jnp.zeros((ROWS, HD), F32)
        wide = 4 * PAGE
        for i in range(LENT // 4):
            s = guest_buf[:, i * wide:(i + 1) * wide]
            w = jnp.exp2(s * LOG2E_SCALE - guest_top)
            totals.append(lanes_sum(w))
            guest_out = guest_out + jnp.dot(
                w.astype(BF16), vl_buf[i * wide:(i + 1) * wide, :], preferred_element_type=F32)
        total = (totals[0] + totals[1]) + (totals[2] + totals[3])
        guest_total = jnp.sum(total, axis=1, keepdims=True)
        level = jnp.broadcast_to(guest_top + jnp.log2(guest_total), (ROWS, HD))
        high = level.astype(BF16).astype(F32)
        middle = (level - high).astype(BF16).astype(F32)
        low = level - high - middle
        place = lane & 63
        coded = jnp.where(place == 0, high, jnp.where(place == 1, middle, jnp.where(place == 2, low, 0.0)))
        coded = jnp.where(lane[:half_rows] < 64, coded[:half_rows], coded[half_rows:])
        return jnp.concatenate([guest_out / guest_total, coded], axis=0).astype(BF16)

    p_relay = (p_relay_even, p_relay_odd)

    def result_copy(own, zz, p):
        slot = (zz - z) & (NZ - 1)
        return remote_copy(
            own, p_relay[p].at[slot], p1_send_sem.at[zz], p1_recv_sem.at[p, slot], (at(zz, y), odd_t))

    def send_result(own, rows):
        @pl.when(is_even)
        def _():
            for zz in rows:
                result_copy(own, zz, 0).start()

        for zz in rows:
            @pl.when(is_relay & (z != zz))
            def _():
                result_copy(own, zz, 1).start()

    def wait_arrival(received, slot, recv_sem, source):
        @pl.when(jnp.logical_not(is_relay & (z == source)))
        def _():
            remote_copy(
                received.at[slot], received.at[slot], recv_sem.at[slot], recv_sem.at[slot], (inst, odd_t)
            ).wait_recv()

    guest_z = guest_row >> 2
    for i in range(LENT):
        kt_buf[:, i * PAGE:(i + 1) * PAGE] = k_buf[slots[i]].T
        vl_buf[i * PAGE:(i + 1) * PAGE, :] = v_buf[slots[i]]
        lent_bias[i:i + 1, :] = jnp.where(page_token < limits[i], 0.0, NEG)

    @pl.when(early_relay & (z == 0))
    def _():
        pl.semaphore_wait(plane_sem, NT // 2 - 1)
        for zz in range(1, NZ):
            for which in (even_t, odd_t):
                pl.semaphore_signal(go_sem, inc=1, device_id=(at(zz, y), which), device_id_type=MESH)

    for zz in range(EARLY):
        wait_arrival(q_recv_first, zz, qa_recv_sem, zz)
    result = lent_result(q_recv_first[jnp.minimum(guest_z, EARLY - 1)])
    p_own_first[...] = result
    send_result(p_own_first, range(FIRST))

    @pl.when(z < FIRST)
    def _():
        p_relay_odd[0] = result

    pl.when(late)(own_values)
    for j in range(2):
        wait_arrival(q_recv_second, j, qb_recv_sem, HOMES[j])
    result = lent_result(q_recv_second[jnp.where(guest_z >= 5, 0, 1)])
    p_own_second[...] = result
    send_result(p_own_second, range(FIRST, NZ))

    @pl.when(z >= FIRST)
    def _():
        p_relay_odd[0] = result

    @pl.when(z > 0)
    def _():
        pl.semaphore_wait(go_sem, 1)
        for copy in st_copies:
            copy.start()

    def project_all():
        for copy in w_copies:
            copy.wait()
        for copy in st_copies:
            copy.wait_recv()
        row16 = lax.broadcasted_iota(jnp.int32, (16, HD), 0) // STEPS

        def project(d, acc):
            source = (tensor - d + NT) % NT
            for h in range(2):
                x = st_all[d, h * 16:(h + 1) * 16, :].astype(F32)
                left = jnp.concatenate([jnp.where(row16 == g, x, 0.0) for g in range(4)], axis=1).astype(BF16)
                weight = jnp.concatenate(
                    [kw_buf[source, h * 512:(h + 1) * 512, :], vw_buf[source, h * 512:(h + 1) * 512, :]], axis=1)
                acc = acc + jnp.dot(left, weight, preferred_element_type=F32)
            return acc

        acc = lax.fori_loop(0, NT, project, jnp.zeros((16, 2 * HD), F32))
        acc = acc[:8] + acc[8:]
        acc = acc[:4] + acc[4:]
        new_buf[...] = jnp.concatenate([acc, jnp.zeros((12, 2 * HD), F32)], axis=0).astype(BF16)

    pl.when(z == 0)(project_all)

    def relayed(relay, source, sent, received, arrive_sem, send_sem, recv_sem):
        @pl.when(is_relay)
        def _():
            for p in (1, 0):
                for d in Z_ORDER + (0,) * (1 - p):
                    relay_copy(sent.at[p, 0], relay, d, p, arrive_sem.at[p], arrive_sem).wait_recv()
                for e in Y_ORDER + (0,):
                    picked = relay[p][source[e]]
                    if p == 1 and e == 0:
                        received[0] = picked
                    else:
                        sent[p, e] = picked
                        remote_copy(
                            sent.at[p, e], received.at[e], send_sem.at[p, e], recv_sem.at[e], (y_peer[e], even_t + p)
                        ).start()

    def relay_done(sent, received, send_sem, recv_sem):
        for p in range(2):
            for e in Y_ORDER + (0,) * (1 - p):
                remote_copy(
                    sent.at[p, e], received.at[e], send_sem.at[p, e], recv_sem.at[e], (y_peer[e], even_t + p)
                ).wait_send()

    def arrived(received, recv_sem):
        for e in Y_ORDER:
            remote_copy(
                received.at[e], received.at[e], recv_sem.at[e], recv_sem.at[e], (y_peer[e], odd_t)
            ).wait_recv()

        @pl.when(jnp.logical_not(is_relay))
        def _():
            remote_copy(
                received.at[0], received.at[0], recv_sem.at[0], recv_sem.at[0], (inst, odd_t)
            ).wait_recv()

    relayed(
        p_relay, [(z - (lender[e] >> 2)) & (NZ - 1) for e in range(NY)], p_send, p_recv,
        p1_recv_sem, p2_send_sem, p2_recv_sem)
    pl.when(z > 0)(project_all)
    own_total = jnp.sum(own_buf[0], axis=1, keepdims=True)
    own_out = own_buf[1]
    new_keys = new_buf[:, :HD]
    new_values = new_buf[:, HD:]
    s = lax.dot_general(query, new_keys, NT_DIMS, preferred_element_type=F32)
    step = lax.broadcasted_iota(jnp.int32, (ROWS, 16), 0) % STEPS
    other = lax.broadcasted_iota(jnp.int32, (ROWS, 16), 1)
    s = jnp.where(other <= step, s * LOG2E_SCALE, NEG)
    merged_top = jnp.maximum(own_top, jnp.max(s, axis=1, keepdims=True))
    w = jnp.exp2(s - merged_top)
    kept = jnp.exp2(own_top - merged_top)
    merged_total = own_total * kept + jnp.sum(w, axis=1, keepdims=True)
    merged_out = own_out * kept + jnp.dot(w.astype(BF16), new_values, preferred_element_type=F32)

    arrived(p_recv, p2_recv_sem)
    lent_part = p_recv[(y - lender[0]) & (NY - 1)].astype(F32)
    coded = lent_part[ROWS:]
    lane16 = lane[:half_rows]
    level = jnp.concatenate([
        jnp.sum(jnp.where(lane16 < 64, coded, 0.0), axis=1, keepdims=True),
        jnp.sum(jnp.where(lane16 < 64, 0.0, coded), axis=1, keepdims=True)], axis=0)
    level = jnp.where(lender[0] >= 0, level, NEG)
    highest = jnp.maximum(merged_top, level)
    kept = jnp.exp2(merged_top - highest)
    added = jnp.exp2(level - highest)
    out_ref[...] = (merged_out * kept + lent_part[:ROWS] * added) / (merged_total * kept + added)

    for copy in st_copies:
        copy.wait_send()
    for e in range(1, NY):
        q1_row(0, e).wait_send()

    @pl.when(late | is_even)
    def _():
        q1_row(0, 0).wait_send()

    for zz in range(NZ):
        @pl.when(is_even | (z != zz))
        def _():
            result_copy(p_own_first, zz, 0).wait_send()

    @pl.when(early_relay)
    def _():
        push_done(q_send_first, q_recv_first, row, qa_send_sem, qa_recv_sem)

    @pl.when(home_relay)
    def _():
        push_done(q_send_second, q_recv_second, home_place, qb_send_sem, qb_recv_sem)

    @pl.when(is_relay)
    def _():
        relay_done(p_send, p_recv, p2_send_sem, p2_recv_sem)


def on_device(queries, new_states, key_weight, value_weight, key_pool, value_pool, lengths, page_table):
    hbm = pl.BlockSpec(memory_space=pltpu.HBM)
    dma = pltpu.SemaphoreType.DMA

    def rows_of(x):
        return jnp.transpose(x.reshape(STEPS, GROUP, HD), (1, 0, 2)).reshape(ROWS, HD)

    out = pl.pallas_call(
        kernel,
        out_shape=pltpu.VMEM((ROWS, HD), F32),
        in_specs=[hbm] * 8,
        out_specs=pl.BlockSpec(memory_space=pltpu.VMEM),
        scratch_shapes=[
            pltpu.SMEM((1, 32), jnp.int32),
            pltpu.SMEM((32, SLOTS), jnp.int32),
            pltpu.VMEM((32, SLOTS), jnp.int32),
            pltpu.VMEM((SLOTS, PAGE, HD), BF16),
            pltpu.VMEM((SLOTS, PAGE, HD), BF16),
            pltpu.VMEM((NT, GROUP * HD, HD), BF16),
            pltpu.VMEM((NT, GROUP * HD, HD), BF16),
            pltpu.VMEM((CHUNKS, ROWS, CHUNK * PAGE), F32),
            pltpu.VMEM((ROWS, LENT * PAGE), F32),
            pltpu.VMEM((SLOTS, PAGE), F32),
            pltpu.VMEM((NT, ROWS, HD), BF16),
            pltpu.VMEM((HD, LENT * PAGE), BF16),
            pltpu.VMEM((LENT * PAGE, HD), BF16),
            pltpu.VMEM((LENT, PAGE), F32),
            pltpu.VMEM((16, 2 * HD), BF16),
            pltpu.VMEM((2, ROWS, HD), F32),
            pltpu.VMEM((ROWS, HD), BF16),
            pltpu.VMEM((NY, ROWS, HD), BF16),
            pltpu.VMEM((NY, ROWS, HD), BF16),
            pltpu.VMEM((NY, ROWS, HD), BF16),
            pltpu.VMEM((NY, ROWS, HD), BF16),
            pltpu.VMEM((GUESTS * NY, ROWS, HD), BF16),
            pltpu.VMEM((GUESTS * NY, ROWS, HD), BF16),
            pltpu.VMEM((2, NZ, ROWS, HD), BF16),
            pltpu.VMEM((2, NZ, ROWS, HD), BF16),
            pltpu.VMEM((EARLY, ROWS, HD), BF16),
            pltpu.VMEM((2, ROWS, HD), BF16),
            pltpu.VMEM((ROWS + 16, HD), BF16),
            pltpu.VMEM((ROWS + 16, HD), BF16),
            pltpu.VMEM((NZ, ROWS + 16, HD), BF16),
            pltpu.VMEM((NZ, ROWS + 16, HD), BF16),
            pltpu.VMEM((2, NY, ROWS + 16, HD), BF16),
            pltpu.VMEM((NY, ROWS + 16, HD), BF16),
            dma((5,)), dma((PARTS,)), dma((PARTS,)), dma((2,)), dma((NT,)), dma((NT,)),
            pltpu.SemaphoreType.REGULAR((2,)), pltpu.SemaphoreType.REGULAR, pltpu.SemaphoreType.REGULAR,
            dma((NY,)), dma((2, NY)), dma((2, NY)), dma((2, GUESTS * NY)),
            dma((2, NZ)), dma((EARLY,)), dma((2, NZ)), dma((2,)),
            dma((NZ,)), dma((2, NZ)), dma((2, NY)), dma((NY,)),
        ],
        compiler_params=pltpu.CompilerParams(
            collective_id=0, has_side_effects=True, vmem_limit_bytes=VMEM_BYTES),
    )(
        lengths.reshape(1, -1), page_table, rows_of(queries), rows_of(new_states),
        key_weight.reshape(NT, GROUP * HD, HD), value_weight.reshape(NT, GROUP * HD, HD),
        key_pool, value_pool,
    )
    return (
        jnp.transpose(out.reshape(GROUP, STEPS, HD), (1, 0, 2))
        .reshape(1, STEPS, GROUP * HD)
        .astype(BF16)
    )


def solution(mesh):
    placed = (
        P("inst", None, "tensor"),
        P("inst", None, "tensor"),
        P(None, "tensor"),
        P(None, "tensor"),
        P("inst", None, "tensor"),
        P("inst", None, "tensor"),
        P(),
        P(),
    )
    return jax.shard_map(
        on_device, mesh=mesh, in_specs=placed, out_specs=P("inst", None, "tensor"), check_vma=False
    )
```

```python
import functools
import math

import jax
import jax.numpy as jnp
from jax import lax
from jax.experimental import pallas as pl
from jax.experimental.pallas import tpu as pltpu
from jax.sharding import PartitionSpec as P

HD = 128
STEPS = 4
GROUP = 8
ROWS = STEPS * GROUP
PAGE = 256
SLOTS = 64
CHUNK = 8
CHUNKS = SLOTS // CHUNK
PARTS = 4
PART = SLOTS // PARTS
LENT = 16
NY = 4
NZ = 8
NT = 8
EARLY = 2
HOMES = (0, 1)
GUESTS = 3
FIRST = 3
NEG = -1e30
VMEM_BYTES = 60 * 1024 * 1024
Z_ORDER = (4, 3, 5, 2, 6, 1, 7)
Y_ORDER = (2, 1, 3)
T_ORDER = (4, 5, 3, 2, 6, 7, 1)
LOG2E_SCALE = math.log2(math.e) / math.sqrt(HD)
F32 = jnp.float32
BF16 = jnp.bfloat16
MESH = pl.DeviceIdType.MESH
NT_DIMS = (((1,), (1,)), ((), ()))


def remote_copy(src, dst, send_sem, recv_sem, target):
    return pltpu.make_async_remote_copy(
        src_ref=src, dst_ref=dst, send_sem=send_sem, recv_sem=recv_sem, device_id=target, device_id_type=MESH)


def lanes_sum(w):
    total = w[:, :HD]
    for b in range(1, w.shape[1] // HD):
        total = total + w[:, b * HD:(b + 1) * HD]
    return total


def kernel(
    len_hbm, tab_hbm, q_hbm, st_hbm, kw_hbm, vw_hbm, k_hbm, v_hbm,
    out_ref,
    len_smem, tab_smem, tab_ref, k_buf, v_buf, kw_buf, vw_buf, s_buf, guest_buf, bias_buf, st_all,
    kt_buf, vl_buf, lent_bias, new_buf, own_buf, q_own, q_row_even, q_row_odd, q_mid_even, q_mid_odd, q_late_even, q_late_odd, q_send_first, q_send_second, q_recv_first, q_recv_second,
    p_own_first, p_own_second, p_relay_even, p_relay_odd, p_send, p_recv,
    small_sem, k_sem, v_sem, w_sem, st_send_sem, st_recv_sem, ready_sem, plane_sem, go_sem,
    q1_send_sem, q1_row_sem, q1_mid_sem, q1_late_sem, qa_send_sem, qa_recv_sem, qb_send_sem, qb_recv_sem,
    p1_send_sem, p1_recv_sem, p2_send_sem, p2_recv_sem,
):
    inst = lax.axis_index("inst")
    tensor = lax.axis_index("tensor")
    z = inst // NY
    y = inst % NY
    odd = tensor % 2
    even_t = tensor - odd
    odd_t = even_t + 1
    is_relay = odd == 1
    is_even = odd == 0
    early = z < EARLY
    late = z >= EARLY
    early_relay = early & is_relay
    home_relay = is_relay & ((z == HOMES[0]) | (z == HOMES[1]))
    row = jnp.minimum(z, EARLY - 1)
    home_place = jnp.where(z == HOMES[0], 0, 1)
    home_row = jnp.where(z >= 5, HOMES[0], HOMES[1])
    guests_from = jnp.where(z == HOMES[0], 5, 2)

    def at(zz, yy):
        return zz * NY + yy

    z_peer = [at((z + d) % NZ, y) for d in range(NZ)]
    ys = [(y + e) % NY for e in range(NY)]
    y_peer = [at(z, ys[e]) for e in range(NY)]
    t_peer = [(tensor + d) % NT for d in range(NT)]

    barrier = pltpu.get_barrier_semaphore()

    def greet(where, which):
        pl.semaphore_signal(barrier, inc=1, device_id=(where, which), device_id_type=MESH)

    @pl.when(late)
    def _():
        pl.semaphore_wait(barrier, EARLY + NY - 1)
        for c in range(EARLY):
            pl.semaphore_signal(
                ready_sem.at[odd], inc=1, device_id=(at((z + c) % EARLY, y), odd_t), device_id_type=MESH)

    @pl.when(early_relay)
    def _():
        for zz in range(NZ - 1, EARLY - 1, -1):
            greet(at(zz, y), even_t)
            greet(at(zz, y), odd_t)

    @pl.when(home_relay)
    def _():
        for j in range(GUESTS):
            for e in Y_ORDER:
                greet(at(guests_from + j, ys[e]), even_t)
                greet(at(guests_from + j, ys[e]), odd_t)

    @pl.when(early)
    def _():
        for c in range(1, EARLY):
            greet(at((z + c) % EARLY, y), odd_t)

    @pl.when(z == 0)
    def _():
        for d in T_ORDER:
            greet(inst, t_peer[d])

    @pl.when(early_relay)
    def _():
        for e in Y_ORDER:
            greet(y_peer[e], even_t)
            greet(y_peer[e], odd_t)

    @pl.when(early_relay & (z > 0))
    def _():
        greet(inst, even_t)

    small_copies = [
        pltpu.make_async_copy(q_hbm, q_own, small_sem.at[0]),
        pltpu.make_async_copy(st_hbm, st_all.at[0], small_sem.at[1]),
        pltpu.make_async_copy(tab_hbm, tab_ref, small_sem.at[2]),
        pltpu.make_async_copy(len_hbm, len_smem, small_sem.at[3]),
        pltpu.make_async_copy(tab_hbm, tab_smem, small_sem.at[4]),
    ]
    for copy in small_copies:
        copy.start()

    def k_copy(c):
        part = pl.ds(c * PART, PART)
        return pltpu.make_async_copy(k_hbm.at[part], k_buf.at[part], k_sem.at[c])

    def v_copy(c):
        part = pl.ds(c * PART, PART)
        return pltpu.make_async_copy(v_hbm.at[part], v_buf.at[part], v_sem.at[c])

    w_copies = [
        pltpu.make_async_copy(kw_hbm, kw_buf, w_sem.at[0]),
        pltpu.make_async_copy(vw_hbm, vw_buf, w_sem.at[1]),
    ]

    @pl.when(early)
    def _():
        pl.semaphore_wait(
            barrier, NY - 1 + odd * 2 * (EARLY - 1) + jnp.where(z == 0, NT - 1, 1 - odd))

    small_copies[0].wait()

    def q1_copy(place, e, target):
        buffer, slot, sem = place
        return remote_copy(q_own, buffer.at[slot], q1_send_sem.at[e], sem.at[slot], (target, odd_t))

    def q1_row(p, e):
        return q1_copy(((q_row_even, q_row_odd)[p], e, q1_row_sem.at[p]), e, y_peer[e])

    def q1_mid(p, e):
        return q1_copy(((q_mid_even, q_mid_odd)[p], e, q1_mid_sem.at[p]), e, at(home_row, ys[e]))

    def q1_late(p, e):
        return q1_copy(
            ((q_late_even, q_late_odd)[p], ((z + 1) % GUESTS) * NY + e, q1_late_sem.at[p]), e, at(home_row, ys[e]))

    @pl.when(z == 0)
    def _():
        q_mid_even[...] = jnp.zeros_like(q_mid_even)
        q_mid_odd[...] = jnp.zeros_like(q_mid_odd)

    for p in range(2):
        @pl.when(early & (odd == p))
        def _():
            for e in Y_ORDER + (0,) * (1 - p):
                q1_row(p, e).start()

        @pl.when((z == EARLY) & (odd == p))
        def _():
            for e in Y_ORDER + (0,):
                q1_mid(p, e).start()

        @pl.when((z > EARLY) & (odd == p))
        def _():
            for e in Y_ORDER + (0,):
                q1_late(p, e).start()

    for c in range(PARTS):
        k_copy(c).start()
    for c in range(PARTS):
        v_copy(c).start()

    small_copies[1].wait()
    st_copies = [
        remote_copy(st_all.at[0], st_all.at[d], st_send_sem.at[d], st_recv_sem.at[d], (inst, t_peer[d]))
        for d in T_ORDER
    ]

    @pl.when(z == 0)
    def _():
        for copy in st_copies:
            copy.start()

    query = q_own[...]
    q_row_odd[0] = query

    def relay_copy(own, relay, d, p, send_sem, recv_sem):
        return remote_copy(own, relay[p].at[d], send_sem.at[d], recv_sem.at[p, d], (z_peer[d], odd_t))

    for copy in small_copies[2:]:
        copy.wait()
    table = tab_ref[...]
    holder = table >> 6
    row_id = lax.broadcasted_iota(jnp.int32, table.shape, 0)
    page_id = lax.broadcasted_iota(jnp.int32, table.shape, 1)
    lent = (table >= 0) & (holder != row_id)
    lent_code = jnp.where(lent, row_id * SLOTS + (SLOTS - 1) - page_id, -1)
    lent_holder = jnp.where(lent, holder, -1)
    guest_code = [jnp.max(jnp.where(holder == z_peer[d], lent_code, -1)) for d in range(NZ)]
    lender = [jnp.max(jnp.where(row_id == y_peer[e], lent_holder, -1)) for e in range(NY)]

    own_length = len_smem[0, inst]
    own_row = jnp.broadcast_to(tab_ref[pl.ds(inst, 1), :] - inst * SLOTS, (SLOTS, SLOTS))
    slot_id = lax.broadcasted_iota(jnp.int32, (SLOTS, SLOTS), 0)
    page_of = lax.broadcasted_iota(jnp.int32, (SLOTS, SLOTS), 1)
    counted = jnp.clip(own_length - page_of * PAGE, 0, PAGE).astype(F32)
    valid = jnp.sum(jnp.where(own_row == slot_id, counted, 0.0), axis=1, keepdims=True)
    token = lax.broadcasted_iota(jnp.int32, (SLOTS, PAGE), 1).astype(F32)
    bias_buf[...] = jnp.where(token < valid, 0.0, NEG)

    guest = guest_code[0] >> 6
    first_page = (SLOTS - 1) - (guest_code[0] & (SLOTS - 1))
    guest_row = jnp.maximum(guest, 0)
    guest_length = jnp.where(guest >= 0, len_smem[0, guest_row], 0)
    guest_pages = ((guest_length + PAGE - 1) // PAGE) // 4
    page_token = lax.broadcasted_iota(jnp.int32, (1, PAGE), 1)
    slots = []
    limits = []
    for i in range(LENT):
        page = jnp.minimum(first_page + i, SLOTS - 1)
        slots.append(jnp.clip(tab_smem[guest_row, page] - inst * SLOTS, 0, SLOTS - 1))
        limits.append(jnp.where(i < guest_pages, guest_length - page * PAGE, 0))

    def scores_chunk(c, top):
        for p in range(CHUNK):
            slot = c * CHUNK + p
            s = lax.dot_general(query, k_buf[slot], NT_DIMS, preferred_element_type=F32)
            s = s + bias_buf[pl.ds(slot, 1), :]
            s_buf[c, :, p * PAGE:(p + 1) * PAGE] = s
            top = jnp.maximum(top, jnp.maximum(s[:, :HD], s[:, HD:]))
        return top

    def values_chunk(c, carry):
        total, numerator = carry
        half = CHUNK // 2
        for h in range(2):
            s = s_buf[c, :, h * half * PAGE:(h + 1) * half * PAGE]
            w = jnp.exp2(s * LOG2E_SCALE - own_top)
            total = total + lanes_sum(w)
            v = v_buf[pl.ds(c * CHUNK + h * half, half)].reshape(half * PAGE, HD)
            numerator = numerator + jnp.dot(w.astype(BF16), v, preferred_element_type=F32)
        return total, numerator

    per_part = CHUNKS // PARTS
    top = jnp.full((ROWS, HD), NEG, F32)
    for c in range(PARTS):
        k_copy(c).wait()
        top = lax.fori_loop(c * per_part, (c + 1) * per_part, scores_chunk, top)
    own_top = jnp.max(top, axis=1, keepdims=True) * LOG2E_SCALE

    def pick_first(p, r):
        e = (y - r) & (NY - 1)
        return lax.select((r >> 2) == EARLY, (q_mid_even, q_mid_odd)[p][e], (q_row_even, q_row_odd)[p][e])

    def pick_second(p, r):
        return (q_late_even, q_late_odd)[p][(((r >> 2) + 1) % GUESTS) * NY + ((y - r) & (NY - 1))]

    def push(p, d, sent, received, slot, send_sem, recv_sem):
        return remote_copy(
            sent.at[p, d], received.at[slot], send_sem.at[p, d], recv_sem.at[slot], (z_peer[d], even_t + p))

    def push_all(p, pick, sent, received, slot, send_sem, recv_sem):
        for d in Z_ORDER + (0,):
            picked = pick(guest_code[d] >> 6)
            if p == 1 and d == 0:
                received[slot] = picked
            else:
                sent[p, d] = picked
                push(p, d, sent, received, slot, send_sem, recv_sem).start()

    def push_done(sent, received, slot, send_sem, recv_sem):
        for p in range(2):
            for d in Z_ORDER + (0,) * (1 - p):
                push(p, d, sent, received, slot, send_sem, recv_sem).wait_send()

    for copy in w_copies:
        copy.start()

    @pl.when(early_relay)
    def _():
        for p in (1, 0):
            for e in Y_ORDER + (0,) * (1 - p):
                q1_row(p, e).wait_recv()

        @pl.when(z == HOMES[1])
        def _():
            for p in (1, 0):
                for e in Y_ORDER + (0,):
                    q1_mid(p, e).wait_recv()

        for p in range(2):
            for d in range(NZ):
                picked = pick_first(p, guest_code[d] >> 6)
                if p == 1 and d == 0:
                    q_recv_first[row] = picked
                else:
                    q_send_first[p, d] = picked
        for p in (1, 0):
            pl.semaphore_wait(ready_sem.at[p], NZ - EARLY)
            for d in Z_ORDER + (0,) * (1 - p):
                push(p, d, q_send_first, q_recv_first, row, qa_send_sem, qa_recv_sem).start()

    @pl.when(early_relay & (z == 0))
    def _():
        for d in (2, 4, 6):
            pl.semaphore_signal(plane_sem, inc=1, device_id=(inst, t_peer[d]), device_id_type=MESH)

    def own_values():
        total, numerator = lax.fori_loop(
            0, CHUNKS, values_chunk, (jnp.zeros((ROWS, HD), F32), jnp.zeros((ROWS, HD), F32)))
        own_buf[0] = total
        own_buf[1] = numerator

    for c in range(PARTS):
        v_copy(c).wait()
    pl.when(early)(own_values)

    @pl.when(home_relay)
    def _():
        for p in (1, 0):
            for j in range(GUESTS):
                @pl.when((z == HOMES[0]) | (j > 0))
                def _():
                    for e in Y_ORDER + (0,):
                        slot = j * NY + e
                        remote_copy(
                            q_own, (q_late_even, q_late_odd)[p].at[slot], q1_send_sem.at[e],
                            q1_late_sem.at[p, slot], (inst, odd_t)).wait_recv()

            push_all(
                p, functools.partial(pick_second, p),
                q_send_second, q_recv_second, home_place, qb_send_sem, qb_recv_sem)

    lane = lax.broadcasted_iota(jnp.int32, (ROWS, HD), 1)
    half_rows = ROWS // 2

    def lent_result(guest_query):
        tops = []
        for i in range(LENT):
            s = jnp.dot(guest_query, kt_buf[:, i * PAGE:(i + 1) * PAGE], preferred_element_type=F32)
            s = s + lent_bias[i:i + 1, :]
            guest_buf[:, i * PAGE:(i + 1) * PAGE] = s
            tops.append(jnp.maximum(s[:, :HD], s[:, HD:]))
        while len(tops) > 1:
            tops = [jnp.maximum(m, n) for m, n in zip(tops[::2], tops[1::2])]
        guest_top = jnp.max(tops[0], axis=1, keepdims=True) * LOG2E_SCALE
        totals = []
        guest_out = jnp.zeros((ROWS, HD), F32)
        wide = 4 * PAGE
        for i in range(LENT // 4):
            s = guest_buf[:, i * wide:(i + 1) * wide]
            w = jnp.exp2(s * LOG2E_SCALE - guest_top)
            totals.append(lanes_sum(w))
            guest_out = guest_out + jnp.dot(
                w.astype(BF16), vl_buf[i * wide:(i + 1) * wide, :], preferred_element_type=F32)
        total = (totals[0] + totals[1]) + (totals[2] + totals[3])
        guest_total = jnp.sum(total, axis=1, keepdims=True)
        level = jnp.broadcast_to(guest_top + jnp.log2(guest_total), (ROWS, HD))
        high = level.astype(BF16).astype(F32)
        middle = (level - high).astype(BF16).astype(F32)
        low = level - high - middle
        place = lane & 63
        coded = jnp.where(place == 0, high, jnp.where(place == 1, middle, jnp.where(place == 2, low, 0.0)))
        coded = jnp.where(lane[:half_rows] < 64, coded[:half_rows], coded[half_rows:])
        return jnp.concatenate([guest_out / guest_total, coded], axis=0).astype(BF16)

    p_relay = (p_relay_even, p_relay_odd)

    def result_copy(own, zz, p):
        slot = (zz - z) & (NZ - 1)
        return remote_copy(
            own, p_relay[p].at[slot], p1_send_sem.at[zz], p1_recv_sem.at[p, slot], (at(zz, y), odd_t))

    def send_result(own, rows):
        @pl.when(is_even)
        def _():
            for zz in rows:
                result_copy(own, zz, 0).start()

        for zz in rows:
            @pl.when(is_relay & (z != zz))
            def _():
                result_copy(own, zz, 1).start()

    def wait_arrival(received, slot, recv_sem, source):
        @pl.when(jnp.logical_not(is_relay & (z == source)))
        def _():
            remote_copy(
                received.at[slot], received.at[slot], recv_sem.at[slot], recv_sem.at[slot], (inst, odd_t)
            ).wait_recv()

    guest_z = guest_row >> 2
    for i in range(LENT):
        kt_buf[:, i * PAGE:(i + 1) * PAGE] = k_buf[slots[i]].T
        vl_buf[i * PAGE:(i + 1) * PAGE, :] = v_buf[slots[i]]
        lent_bias[i:i + 1, :] = jnp.where(page_token < limits[i], 0.0, NEG)

    @pl.when(early_relay & (z == 0))
    def _():
        pl.semaphore_wait(plane_sem, NT // 2 - 1)
        for zz in range(1, NZ):
            for which in (even_t, odd_t):
                pl.semaphore_signal(go_sem, inc=1, device_id=(at(zz, y), which), device_id_type=MESH)

    for zz in range(EARLY):
        wait_arrival(q_recv_first, zz, qa_recv_sem, zz)
    result = lent_result(q_recv_first[jnp.minimum(guest_z, EARLY - 1)])
    p_own_first[...] = result
    send_result(p_own_first, range(FIRST))

    @pl.when(z < FIRST)
    def _():
        p_relay_odd[0] = result

    pl.when(late)(own_values)
    for j in range(2):
        wait_arrival(q_recv_second, j, qb_recv_sem, HOMES[j])
    result = lent_result(q_recv_second[jnp.where(guest_z >= 5, 0, 1)])
    p_own_second[...] = result
    send_result(p_own_second, range(FIRST, NZ))

    @pl.when(z >= FIRST)
    def _():
        p_relay_odd[0] = result

    @pl.when(z > 0)
    def _():
        pl.semaphore_wait(go_sem, 1)
        for copy in st_copies:
            copy.start()

    def project_all():
        for copy in w_copies:
            copy.wait()
        for copy in st_copies:
            copy.wait_recv()
        row16 = lax.broadcasted_iota(jnp.int32, (16, HD), 0) // STEPS

        def project(d, acc):
            source = (tensor - d + NT) % NT
            for h in range(2):
                x = st_all[d, h * 16:(h + 1) * 16, :].astype(F32)
                left = jnp.concatenate([jnp.where(row16 == g, x, 0.0) for g in range(4)], axis=1).astype(BF16)
                weight = jnp.concatenate(
                    [kw_buf[source, h * 512:(h + 1) * 512, :], vw_buf[source, h * 512:(h + 1) * 512, :]], axis=1)
                acc = acc + jnp.dot(left, weight, preferred_element_type=F32)
            return acc

        acc = lax.fori_loop(0, NT, project, jnp.zeros((16, 2 * HD), F32))
        acc = acc[:8] + acc[8:]
        acc = acc[:4] + acc[4:]
        new_buf[...] = jnp.concatenate([acc, jnp.zeros((12, 2 * HD), F32)], axis=0).astype(BF16)

    pl.when(z == 0)(project_all)

    def relayed(relay, source, sent, received, arrive_sem, send_sem, recv_sem):
        @pl.when(is_relay)
        def _():
            for p in (1, 0):
                for d in Z_ORDER + (0,) * (1 - p):
                    relay_copy(sent.at[p, 0], relay, d, p, arrive_sem.at[p], arrive_sem).wait_recv()
                for e in Y_ORDER + (0,):
                    picked = relay[p][source[e]]
                    if p == 1 and e == 0:
                        received[0] = picked
                    else:
                        sent[p, e] = picked
                        remote_copy(
                            sent.at[p, e], received.at[e], send_sem.at[p, e], recv_sem.at[e], (y_peer[e], even_t + p)
                        ).start()

    def relay_done(sent, received, send_sem, recv_sem):
        for p in range(2):
            for e in Y_ORDER + (0,) * (1 - p):
                remote_copy(
                    sent.at[p, e], received.at[e], send_sem.at[p, e], recv_sem.at[e], (y_peer[e], even_t + p)
                ).wait_send()

    def arrived(received, recv_sem):
        for e in Y_ORDER:
            remote_copy(
                received.at[e], received.at[e], recv_sem.at[e], recv_sem.at[e], (y_peer[e], odd_t)
            ).wait_recv()

        @pl.when(jnp.logical_not(is_relay))
        def _():
            remote_copy(
                received.at[0], received.at[0], recv_sem.at[0], recv_sem.at[0], (inst, odd_t)
            ).wait_recv()

    relayed(
        p_relay, [(z - (lender[e] >> 2)) & (NZ - 1) for e in range(NY)], p_send, p_recv,
        p1_recv_sem, p2_send_sem, p2_recv_sem)
    pl.when(z > 0)(project_all)
    own_total = jnp.sum(own_buf[0], axis=1, keepdims=True)
    own_out = own_buf[1]
    new_keys = new_buf[:, :HD]
    new_values = new_buf[:, HD:]
    s = lax.dot_general(query, new_keys, NT_DIMS, preferred_element_type=F32)
    step = lax.broadcasted_iota(jnp.int32, (ROWS, 16), 0) % STEPS
    other = lax.broadcasted_iota(jnp.int32, (ROWS, 16), 1)
    s = jnp.where(other <= step, s * LOG2E_SCALE, NEG)
    merged_top = jnp.maximum(own_top, jnp.max(s, axis=1, keepdims=True))
    w = jnp.exp2(s - merged_top)
    kept = jnp.exp2(own_top - merged_top)
    merged_total = own_total * kept + jnp.sum(w, axis=1, keepdims=True)
    merged_out = own_out * kept + jnp.dot(w.astype(BF16), new_values, preferred_element_type=F32)

    arrived(p_recv, p2_recv_sem)
    lent_part = p_recv[(y - lender[0]) & (NY - 1)].astype(F32)
    coded = lent_part[ROWS:]
    lane16 = lane[:half_rows]
    level = jnp.concatenate([
        jnp.sum(jnp.where(lane16 < 64, coded, 0.0), axis=1, keepdims=True),
        jnp.sum(jnp.where(lane16 < 64, 0.0, coded), axis=1, keepdims=True)], axis=0)
    has_lender = lender[0] >= 0
    level = jnp.where(has_lender, level, NEG)
    lent_out = jnp.where(has_lender, lent_part[:ROWS], 0.0)
    highest = jnp.maximum(merged_top, level)
    kept = jnp.exp2(merged_top - highest)
    added = jnp.exp2(level - highest)
    out_ref[...] = (merged_out * kept + lent_out * added) / (merged_total * kept + added)

    for copy in st_copies:
        copy.wait_send()
    for e in range(1, NY):
        q1_row(0, e).wait_send()

    @pl.when(late | is_even)
    def _():
        q1_row(0, 0).wait_send()

    for zz in range(NZ):
        @pl.when(is_even | (z != zz))
        def _():
            result_copy(p_own_first, zz, 0).wait_send()

    @pl.when(early_relay)
    def _():
        push_done(q_send_first, q_recv_first, row, qa_send_sem, qa_recv_sem)

    @pl.when(home_relay)
    def _():
        push_done(q_send_second, q_recv_second, home_place, qb_send_sem, qb_recv_sem)

    @pl.when(is_relay)
    def _():
        relay_done(p_send, p_recv, p2_send_sem, p2_recv_sem)


def on_device(queries, new_states, key_weight, value_weight, key_pool, value_pool, lengths, page_table):
    hbm = pl.BlockSpec(memory_space=pltpu.HBM)
    dma = pltpu.SemaphoreType.DMA

    def rows_of(x):
        return jnp.transpose(x.reshape(STEPS, GROUP, HD), (1, 0, 2)).reshape(ROWS, HD)

    out = pl.pallas_call(
        kernel,
        out_shape=pltpu.VMEM((ROWS, HD), F32),
        in_specs=[hbm] * 8,
        out_specs=pl.BlockSpec(memory_space=pltpu.VMEM),
        scratch_shapes=[
            pltpu.SMEM((1, 32), jnp.int32),
            pltpu.SMEM((32, SLOTS), jnp.int32),
            pltpu.VMEM((32, SLOTS), jnp.int32),
            pltpu.VMEM((SLOTS, PAGE, HD), BF16),
            pltpu.VMEM((SLOTS, PAGE, HD), BF16),
            pltpu.VMEM((NT, GROUP * HD, HD), BF16),
            pltpu.VMEM((NT, GROUP * HD, HD), BF16),
            pltpu.VMEM((CHUNKS, ROWS, CHUNK * PAGE), F32),
            pltpu.VMEM((ROWS, LENT * PAGE), F32),
            pltpu.VMEM((SLOTS, PAGE), F32),
            pltpu.VMEM((NT, ROWS, HD), BF16),
            pltpu.VMEM((HD, LENT * PAGE), BF16),
            pltpu.VMEM((LENT * PAGE, HD), BF16),
            pltpu.VMEM((LENT, PAGE), F32),
            pltpu.VMEM((16, 2 * HD), BF16),
            pltpu.VMEM((2, ROWS, HD), F32),
            pltpu.VMEM((ROWS, HD), BF16),
            pltpu.VMEM((NY, ROWS, HD), BF16),
            pltpu.VMEM((NY, ROWS, HD), BF16),
            pltpu.VMEM((NY, ROWS, HD), BF16),
            pltpu.VMEM((NY, ROWS, HD), BF16),
            pltpu.VMEM((GUESTS * NY, ROWS, HD), BF16),
            pltpu.VMEM((GUESTS * NY, ROWS, HD), BF16),
            pltpu.VMEM((2, NZ, ROWS, HD), BF16),
            pltpu.VMEM((2, NZ, ROWS, HD), BF16),
            pltpu.VMEM((EARLY, ROWS, HD), BF16),
            pltpu.VMEM((2, ROWS, HD), BF16),
            pltpu.VMEM((ROWS + 16, HD), BF16),
            pltpu.VMEM((ROWS + 16, HD), BF16),
            pltpu.VMEM((NZ, ROWS + 16, HD), BF16),
            pltpu.VMEM((NZ, ROWS + 16, HD), BF16),
            pltpu.VMEM((2, NY, ROWS + 16, HD), BF16),
            pltpu.VMEM((NY, ROWS + 16, HD), BF16),
            dma((5,)), dma((PARTS,)), dma((PARTS,)), dma((2,)), dma((NT,)), dma((NT,)),
            pltpu.SemaphoreType.REGULAR((2,)), pltpu.SemaphoreType.REGULAR, pltpu.SemaphoreType.REGULAR,
            dma((NY,)), dma((2, NY)), dma((2, NY)), dma((2, GUESTS * NY)),
            dma((2, NZ)), dma((EARLY,)), dma((2, NZ)), dma((2,)),
            dma((NZ,)), dma((2, NZ)), dma((2, NY)), dma((NY,)),
        ],
        compiler_params=pltpu.CompilerParams(
            collective_id=0, has_side_effects=True, vmem_limit_bytes=VMEM_BYTES),
    )(
        lengths.reshape(1, -1), page_table, rows_of(queries), rows_of(new_states),
        key_weight.reshape(NT, GROUP * HD, HD), value_weight.reshape(NT, GROUP * HD, HD),
        key_pool, value_pool,
    )
    return (
        jnp.transpose(out.reshape(GROUP, STEPS, HD), (1, 0, 2))
        .reshape(1, STEPS, GROUP * HD)
        .astype(BF16)
    )


def solution(mesh):
    placed = (
        P("inst", None, "tensor"),
        P("inst", None, "tensor"),
        P(None, "tensor"),
        P(None, "tensor"),
        P("inst", None, "tensor"),
        P("inst", None, "tensor"),
        P(),
        P(),
    )
    return jax.shard_map(
        on_device, mesh=mesh, in_specs=placed, out_specs=P("inst", None, "tensor"), check_vma=False
    )
```

```python
import functools
import math

import jax
import jax.numpy as jnp
from jax import lax
from jax.experimental import pallas as pl
from jax.experimental.pallas import tpu as pltpu
from jax.sharding import PartitionSpec as P

HD = 128
STEPS = 4
GROUP = 8
ROWS = STEPS * GROUP
PAGE = 256
SLOTS = 64
CHUNK = 8
CHUNKS = SLOTS // CHUNK
PARTS = 4
PART = SLOTS // PARTS
LENT = 16
NY = 4
NZ = 8
NT = 8
EARLY = 2
HOMES = (0, 1)
GUESTS = 3
FIRST = 3
NEG = -1e30
VMEM_BYTES = 60 * 1024 * 1024
Z_ORDER = (4, 3, 5, 2, 6, 1, 7)
Y_ORDER = (2, 1, 3)
T_ORDER = (4, 5, 3, 2, 6, 7, 1)
LOG2E_SCALE = math.log2(math.e) / math.sqrt(HD)
F32 = jnp.float32
BF16 = jnp.bfloat16
MESH = pl.DeviceIdType.MESH
NT_DIMS = (((1,), (1,)), ((), ()))


def remote_copy(src, dst, send_sem, recv_sem, target):
    return pltpu.make_async_remote_copy(
        src_ref=src, dst_ref=dst, send_sem=send_sem, recv_sem=recv_sem, device_id=target, device_id_type=MESH)


def lanes_sum(w):
    total = w[:, :HD]
    for b in range(1, w.shape[1] // HD):
        total = total + w[:, b * HD:(b + 1) * HD]
    return total


def kernel(
    len_hbm, tab_hbm, q_hbm, st_hbm, kw_hbm, vw_hbm, k_hbm, v_hbm,
    out_ref,
    len_smem, tab_smem, tab_ref, k_buf, v_buf, kw_buf, vw_buf, s_buf, guest_buf, bias_buf, st_all,
    kt_buf, vl_buf, lent_bias, new_buf, own_buf, q_own, q_row_even, q_row_odd, q_mid_even, q_mid_odd, q_late_even, q_late_odd, q_send_first, q_send_second, q_recv_first, q_recv_second,
    p_own_first, p_own_second, p_relay_even, p_relay_odd, p_send, p_recv,
    small_sem, k_sem, v_sem, w_sem, st_send_sem, st_recv_sem, ready_sem, plane_sem, go_sem,
    q1_send_sem, q1_row_sem, q1_mid_sem, q1_late_sem, qa_send_sem, qa_recv_sem, qb_send_sem, qb_recv_sem,
    p1_send_sem, p1_recv_sem, p2_send_sem, p2_recv_sem,
):
    inst = lax.axis_index("inst")
    tensor = lax.axis_index("tensor")
    z = inst // NY
    y = inst % NY
    odd = tensor % 2
    even_t = tensor - odd
    odd_t = even_t + 1
    is_relay = odd == 1
    is_even = odd == 0
    early = z < EARLY
    late = z >= EARLY
    early_relay = early & is_relay
    home_relay = is_relay & ((z == HOMES[0]) | (z == HOMES[1]))
    row = jnp.minimum(z, EARLY - 1)
    home_place = jnp.where(z == HOMES[0], 0, 1)
    home_row = jnp.where(z >= 5, HOMES[0], HOMES[1])
    guests_from = jnp.where(z == HOMES[0], 5, 2)

    def at(zz, yy):
        return zz * NY + yy

    z_peer = [at((z + d) % NZ, y) for d in range(NZ)]
    ys = [(y + e) % NY for e in range(NY)]
    y_peer = [at(z, ys[e]) for e in range(NY)]
    t_peer = [(tensor + d) % NT for d in range(NT)]

    barrier = pltpu.get_barrier_semaphore()

    def greet(where, which):
        pl.semaphore_signal(barrier, inc=1, device_id=(where, which), device_id_type=MESH)

    @pl.when(late)
    def _():
        pl.semaphore_wait(barrier, EARLY + NY - 1)
        for c in range(EARLY):
            pl.semaphore_signal(
                ready_sem.at[odd], inc=1, device_id=(at((z + c) % EARLY, y), odd_t), device_id_type=MESH)

    @pl.when(early_relay)
    def _():
        for zz in range(NZ - 1, EARLY - 1, -1):
            greet(at(zz, y), even_t)
            greet(at(zz, y), odd_t)

    @pl.when(home_relay)
    def _():
        for j in range(GUESTS):
            for e in Y_ORDER:
                greet(at(guests_from + j, ys[e]), even_t)
                greet(at(guests_from + j, ys[e]), odd_t)

    @pl.when(early)
    def _():
        for c in range(1, EARLY):
            greet(at((z + c) % EARLY, y), odd_t)

    @pl.when(z == 0)
    def _():
        for d in T_ORDER:
            greet(inst, t_peer[d])

    @pl.when(early_relay)
    def _():
        for e in Y_ORDER:
            greet(y_peer[e], even_t)
            greet(y_peer[e], odd_t)

    @pl.when(early_relay & (z > 0))
    def _():
        greet(inst, even_t)

    small_copies = [
        pltpu.make_async_copy(q_hbm, q_own, small_sem.at[0]),
        pltpu.make_async_copy(st_hbm, st_all.at[0], small_sem.at[1]),
        pltpu.make_async_copy(tab_hbm, tab_ref, small_sem.at[2]),
        pltpu.make_async_copy(len_hbm, len_smem, small_sem.at[3]),
        pltpu.make_async_copy(tab_hbm, tab_smem, small_sem.at[4]),
    ]
    for copy in small_copies:
        copy.start()

    def k_copy(c):
        part = pl.ds(c * PART, PART)
        return pltpu.make_async_copy(k_hbm.at[part], k_buf.at[part], k_sem.at[c])

    def v_copy(c):
        part = pl.ds(c * PART, PART)
        return pltpu.make_async_copy(v_hbm.at[part], v_buf.at[part], v_sem.at[c])

    w_copies = [
        pltpu.make_async_copy(kw_hbm, kw_buf, w_sem.at[0]),
        pltpu.make_async_copy(vw_hbm, vw_buf, w_sem.at[1]),
    ]

    @pl.when(early)
    def _():
        pl.semaphore_wait(
            barrier, NY - 1 + odd * 2 * (EARLY - 1) + jnp.where(z == 0, NT - 1, 1 - odd))

    small_copies[0].wait()

    def q1_copy(place, e, target):
        buffer, slot, sem = place
        return remote_copy(q_own, buffer.at[slot], q1_send_sem.at[e], sem.at[slot], (target, odd_t))

    def q1_row(p, e):
        return q1_copy(((q_row_even, q_row_odd)[p], e, q1_row_sem.at[p]), e, y_peer[e])

    def q1_mid(p, e):
        return q1_copy(((q_mid_even, q_mid_odd)[p], e, q1_mid_sem.at[p]), e, at(home_row, ys[e]))

    def q1_late(p, e):
        return q1_copy(
            ((q_late_even, q_late_odd)[p], ((z + 1) % GUESTS) * NY + e, q1_late_sem.at[p]), e, at(home_row, ys[e]))

    @pl.when(z == 0)
    def _():
        q_mid_even[...] = jnp.zeros_like(q_mid_even)
        q_mid_odd[...] = jnp.zeros_like(q_mid_odd)

    for p in range(2):
        @pl.when(early & (odd == p))
        def _():
            for e in Y_ORDER + (0,) * (1 - p):
                q1_row(p, e).start()

        @pl.when((z == EARLY) & (odd == p))
        def _():
            for e in Y_ORDER + (0,):
                q1_mid(p, e).start()

        @pl.when((z > EARLY) & (odd == p))
        def _():
            for e in Y_ORDER + (0,):
                q1_late(p, e).start()

    for c in range(PARTS):
        k_copy(c).start()
    for c in range(PARTS):
        v_copy(c).start()

    small_copies[1].wait()
    st_copies = [
        remote_copy(st_all.at[0], st_all.at[d], st_send_sem.at[d], st_recv_sem.at[d], (inst, t_peer[d]))
        for d in T_ORDER
    ]

    @pl.when(z == 0)
    def _():
        for copy in st_copies:
            copy.start()

    query = q_own[...]
    q_row_odd[0] = query

    def relay_copy(own, relay, d, p, send_sem, recv_sem):
        return remote_copy(own, relay[p].at[d], send_sem.at[d], recv_sem.at[p, d], (z_peer[d], odd_t))

    for copy in small_copies[2:]:
        copy.wait()
    table = tab_ref[...]
    holder = table >> 6
    row_id = lax.broadcasted_iota(jnp.int32, table.shape, 0)
    page_id = lax.broadcasted_iota(jnp.int32, table.shape, 1)
    lent = (table >= 0) & (holder != row_id)
    lent_code = jnp.where(lent, row_id * SLOTS + (SLOTS - 1) - page_id, -1)
    lent_holder = jnp.where(lent, holder, -1)
    guest_code = [jnp.max(jnp.where(holder == z_peer[d], lent_code, -1)) for d in range(NZ)]
    lender = [jnp.max(jnp.where(row_id == y_peer[e], lent_holder, -1)) for e in range(NY)]

    own_length = len_smem[0, inst]
    own_row = jnp.broadcast_to(tab_ref[pl.ds(inst, 1), :] - inst * SLOTS, (SLOTS, SLOTS))
    slot_id = lax.broadcasted_iota(jnp.int32, (SLOTS, SLOTS), 0)
    page_of = lax.broadcasted_iota(jnp.int32, (SLOTS, SLOTS), 1)
    counted = jnp.clip(own_length - page_of * PAGE, 0, PAGE).astype(F32)
    valid = jnp.sum(jnp.where(own_row == slot_id, counted, 0.0), axis=1, keepdims=True)
    token = lax.broadcasted_iota(jnp.int32, (SLOTS, PAGE), 1).astype(F32)
    bias_buf[...] = jnp.where(token < valid, 0.0, NEG)

    guest = guest_code[0] >> 6
    first_page = (SLOTS - 1) - (guest_code[0] & (SLOTS - 1))
    guest_row = jnp.maximum(guest, 0)
    guest_length = jnp.where(guest >= 0, len_smem[0, guest_row], 0)
    guest_pages = ((guest_length + PAGE - 1) // PAGE) // 4
    page_token = lax.broadcasted_iota(jnp.int32, (1, PAGE), 1)
    slots = []
    limits = []
    for i in range(LENT):
        page = jnp.minimum(first_page + i, SLOTS - 1)
        slots.append(jnp.clip(tab_smem[guest_row, page] - inst * SLOTS, 0, SLOTS - 1))
        limits.append(jnp.where(i < guest_pages, guest_length - page * PAGE, 0))

    def scores_chunk(c, top):
        for p in range(CHUNK):
            slot = c * CHUNK + p
            s = lax.dot_general(query, k_buf[slot], NT_DIMS, preferred_element_type=F32)
            s = s + bias_buf[pl.ds(slot, 1), :]
            s_buf[c, :, p * PAGE:(p + 1) * PAGE] = s
            top = jnp.maximum(top, jnp.maximum(s[:, :HD], s[:, HD:]))
        return top

    def values_chunk(c, carry):
        total, numerator = carry
        half = CHUNK // 2
        for h in range(2):
            s = s_buf[c, :, h * half * PAGE:(h + 1) * half * PAGE]
            w = jnp.exp2(s * LOG2E_SCALE - own_top)
            total = total + lanes_sum(w)
            v = v_buf[pl.ds(c * CHUNK + h * half, half)].reshape(half * PAGE, HD)
            numerator = numerator + jnp.dot(w.astype(BF16), v, preferred_element_type=F32)
        return total, numerator

    per_part = CHUNKS // PARTS
    top = jnp.full((ROWS, HD), NEG, F32)
    for c in range(PARTS):
        k_copy(c).wait()
        top = lax.fori_loop(c * per_part, (c + 1) * per_part, scores_chunk, top)
    own_top = jnp.max(top, axis=1, keepdims=True) * LOG2E_SCALE

    def pick_first(p, r):
        e = (y - r) & (NY - 1)
        return lax.select((r >> 2) == EARLY, (q_mid_even, q_mid_odd)[p][e], (q_row_even, q_row_odd)[p][e])

    def pick_second(p, r):
        return (q_late_even, q_late_odd)[p][(((r >> 2) + 1) % GUESTS) * NY + ((y - r) & (NY - 1))]

    def push(p, d, sent, received, slot, send_sem, recv_sem):
        return remote_copy(
            sent.at[p, d], received.at[slot], send_sem.at[p, d], recv_sem.at[slot], (z_peer[d], even_t + p))

    def push_all(p, pick, sent, received, slot, send_sem, recv_sem):
        for d in Z_ORDER + (0,):
            picked = pick(guest_code[d] >> 6)
            if p == 1 and d == 0:
                received[slot] = picked
            else:
                sent[p, d] = picked
                push(p, d, sent, received, slot, send_sem, recv_sem).start()

    def push_done(sent, received, slot, send_sem, recv_sem):
        for p in range(2):
            for d in Z_ORDER + (0,) * (1 - p):
                push(p, d, sent, received, slot, send_sem, recv_sem).wait_send()

    for copy in w_copies:
        copy.start()

    @pl.when(early_relay)
    def _():
        for p in (1, 0):
            for e in Y_ORDER + (0,) * (1 - p):
                q1_row(p, e).wait_recv()

        @pl.when(z == HOMES[1])
        def _():
            for p in (1, 0):
                for e in Y_ORDER + (0,):
                    q1_mid(p, e).wait_recv()

        for p in range(2):
            for d in range(NZ):
                picked = pick_first(p, guest_code[d] >> 6)
                if p == 1 and d == 0:
                    q_recv_first[row] = picked
                else:
                    q_send_first[p, d] = picked
        pl.semaphore_wait(ready_sem.at[1], NZ - EARLY)
        for d in Z_ORDER[:3]:
            push(1, d, q_send_first, q_recv_first, row, qa_send_sem, qa_recv_sem).start()
        pl.semaphore_wait(ready_sem.at[0], NZ - EARLY)
        for d in Z_ORDER:
            push(0, d, q_send_first, q_recv_first, row, qa_send_sem, qa_recv_sem).start()
            if d not in Z_ORDER[:3]:
                push(1, d, q_send_first, q_recv_first, row, qa_send_sem, qa_recv_sem).start()
        push(0, 0, q_send_first, q_recv_first, row, qa_send_sem, qa_recv_sem).start()

    @pl.when(early_relay & (z == 0))
    def _():
        for d in (2, 4, 6):
            pl.semaphore_signal(plane_sem, inc=1, device_id=(inst, t_peer[d]), device_id_type=MESH)

    def own_values():
        total, numerator = lax.fori_loop(
            0, CHUNKS, values_chunk, (jnp.zeros((ROWS, HD), F32), jnp.zeros((ROWS, HD), F32)))
        own_buf[0] = total
        own_buf[1] = numerator

    for c in range(PARTS):
        v_copy(c).wait()
    pl.when(early)(own_values)

    @pl.when(home_relay)
    def _():
        for p in (1, 0):
            for j in range(GUESTS):
                @pl.when((z == HOMES[0]) | (j > 0))
                def _():
                    for e in Y_ORDER + (0,):
                        slot = j * NY + e
                        remote_copy(
                            q_own, (q_late_even, q_late_odd)[p].at[slot], q1_send_sem.at[e],
                            q1_late_sem.at[p, slot], (inst, odd_t)).wait_recv()

            push_all(
                p, functools.partial(pick_second, p),
                q_send_second, q_recv_second, home_place, qb_send_sem, qb_recv_sem)

    lane = lax.broadcasted_iota(jnp.int32, (ROWS, HD), 1)
    half_rows = ROWS // 2

    def lent_result(guest_query):
        tops = []
        for i in range(LENT):
            s = jnp.dot(guest_query, kt_buf[:, i * PAGE:(i + 1) * PAGE], preferred_element_type=F32)
            s = s + lent_bias[i:i + 1, :]
            guest_buf[:, i * PAGE:(i + 1) * PAGE] = s
            tops.append(jnp.maximum(s[:, :HD], s[:, HD:]))
        while len(tops) > 1:
            tops = [jnp.maximum(m, n) for m, n in zip(tops[::2], tops[1::2])]
        guest_top = jnp.max(tops[0], axis=1, keepdims=True) * LOG2E_SCALE
        totals = []
        guest_out = jnp.zeros((ROWS, HD), F32)
        wide = 4 * PAGE
        for i in range(LENT // 4):
            s = guest_buf[:, i * wide:(i + 1) * wide]
            w = jnp.exp2(s * LOG2E_SCALE - guest_top)
            totals.append(lanes_sum(w))
            guest_out = guest_out + jnp.dot(
                w.astype(BF16), vl_buf[i * wide:(i + 1) * wide, :], preferred_element_type=F32)
        total = (totals[0] + totals[1]) + (totals[2] + totals[3])
        guest_total = jnp.sum(total, axis=1, keepdims=True)
        level = jnp.broadcast_to(guest_top + jnp.log2(guest_total), (ROWS, HD))
        high = level.astype(BF16).astype(F32)
        middle = (level - high).astype(BF16).astype(F32)
        low = level - high - middle
        place = lane & 63
        coded = jnp.where(place == 0, high, jnp.where(place == 1, middle, jnp.where(place == 2, low, 0.0)))
        coded = jnp.where(lane[:half_rows] < 64, coded[:half_rows], coded[half_rows:])
        return jnp.concatenate([guest_out / guest_total, coded], axis=0).astype(BF16)

    p_relay = (p_relay_even, p_relay_odd)

    def result_copy(own, zz, p):
        slot = (zz - z) & (NZ - 1)
        return remote_copy(
            own, p_relay[p].at[slot], p1_send_sem.at[zz], p1_recv_sem.at[p, slot], (at(zz, y), odd_t))

    def send_result(own, rows):
        @pl.when(is_even)
        def _():
            for zz in rows:
                result_copy(own, zz, 0).start()

        for zz in rows:
            @pl.when(is_relay & (z != zz))
            def _():
                result_copy(own, zz, 1).start()

    def wait_arrival(received, slot, recv_sem, source):
        @pl.when(jnp.logical_not(is_relay & (z == source)))
        def _():
            remote_copy(
                received.at[slot], received.at[slot], recv_sem.at[slot], recv_sem.at[slot], (inst, odd_t)
            ).wait_recv()

    guest_z = guest_row >> 2
    for i in range(LENT):
        kt_buf[:, i * PAGE:(i + 1) * PAGE] = k_buf[slots[i]].T
        vl_buf[i * PAGE:(i + 1) * PAGE, :] = v_buf[slots[i]]
        lent_bias[i:i + 1, :] = jnp.where(page_token < limits[i], 0.0, NEG)

    @pl.when(early_relay & (z == 0))
    def _():
        pl.semaphore_wait(plane_sem, NT // 2 - 1)
        for zz in range(1, NZ):
            for which in (even_t, odd_t):
                pl.semaphore_signal(go_sem, inc=1, device_id=(at(zz, y), which), device_id_type=MESH)

    for zz in range(EARLY):
        wait_arrival(q_recv_first, zz, qa_recv_sem, zz)
    result = lent_result(q_recv_first[jnp.minimum(guest_z, EARLY - 1)])
    p_own_first[...] = result
    send_result(p_own_first, range(FIRST))

    @pl.when(z < FIRST)
    def _():
        p_relay_odd[0] = result

    pl.when(late)(own_values)
    for j in range(2):
        wait_arrival(q_recv_second, j, qb_recv_sem, HOMES[j])
    result = lent_result(q_recv_second[jnp.where(guest_z >= 5, 0, 1)])
    p_own_second[...] = result
    send_result(p_own_second, range(FIRST, NZ))

    @pl.when(z >= FIRST)
    def _():
        p_relay_odd[0] = result

    @pl.when(z > 0)
    def _():
        pl.semaphore_wait(go_sem, 1)
        for copy in st_copies:
            copy.start()

    def project_all():
        for copy in w_copies:
            copy.wait()
        for copy in st_copies:
            copy.wait_recv()
        row16 = lax.broadcasted_iota(jnp.int32, (16, HD), 0) // STEPS

        def project(d, acc):
            source = (tensor - d + NT) % NT
            for h in range(2):
                x = st_all[d, h * 16:(h + 1) * 16, :].astype(F32)
                left = jnp.concatenate([jnp.where(row16 == g, x, 0.0) for g in range(4)], axis=1).astype(BF16)
                weight = jnp.concatenate(
                    [kw_buf[source, h * 512:(h + 1) * 512, :], vw_buf[source, h * 512:(h + 1) * 512, :]], axis=1)
                acc = acc + jnp.dot(left, weight, preferred_element_type=F32)
            return acc

        acc = lax.fori_loop(0, NT, project, jnp.zeros((16, 2 * HD), F32))
        acc = acc[:8] + acc[8:]
        acc = acc[:4] + acc[4:]
        new_buf[...] = jnp.concatenate([acc, jnp.zeros((12, 2 * HD), F32)], axis=0).astype(BF16)

    pl.when(z == 0)(project_all)

    def relayed(relay, source, sent, received, arrive_sem, send_sem, recv_sem):
        @pl.when(is_relay)
        def _():
            for p in (1, 0):
                for d in Z_ORDER + (0,) * (1 - p):
                    relay_copy(sent.at[p, 0], relay, d, p, arrive_sem.at[p], arrive_sem).wait_recv()
                for e in Y_ORDER + (0,):
                    picked = relay[p][source[e]]
                    if p == 1 and e == 0:
                        received[0] = picked
                    else:
                        sent[p, e] = picked
                        remote_copy(
                            sent.at[p, e], received.at[e], send_sem.at[p, e], recv_sem.at[e], (y_peer[e], even_t + p)
                        ).start()

    def relay_done(sent, received, send_sem, recv_sem):
        for p in range(2):
            for e in Y_ORDER + (0,) * (1 - p):
                remote_copy(
                    sent.at[p, e], received.at[e], send_sem.at[p, e], recv_sem.at[e], (y_peer[e], even_t + p)
                ).wait_send()

    def arrived(received, recv_sem):
        for e in Y_ORDER:
            remote_copy(
                received.at[e], received.at[e], recv_sem.at[e], recv_sem.at[e], (y_peer[e], odd_t)
            ).wait_recv()

        @pl.when(jnp.logical_not(is_relay))
        def _():
            remote_copy(
                received.at[0], received.at[0], recv_sem.at[0], recv_sem.at[0], (inst, odd_t)
            ).wait_recv()

    relayed(
        p_relay, [(z - (lender[e] >> 2)) & (NZ - 1) for e in range(NY)], p_send, p_recv,
        p1_recv_sem, p2_send_sem, p2_recv_sem)
    pl.when(z > 0)(project_all)
    own_total = jnp.sum(own_buf[0], axis=1, keepdims=True)
    own_out = own_buf[1]
    new_keys = new_buf[:, :HD]
    new_values = new_buf[:, HD:]
    s = lax.dot_general(query, new_keys, NT_DIMS, preferred_element_type=F32)
    step = lax.broadcasted_iota(jnp.int32, (ROWS, 16), 0) % STEPS
    other = lax.broadcasted_iota(jnp.int32, (ROWS, 16), 1)
    s = jnp.where(other <= step, s * LOG2E_SCALE, NEG)
    merged_top = jnp.maximum(own_top, jnp.max(s, axis=1, keepdims=True))
    w = jnp.exp2(s - merged_top)
    kept = jnp.exp2(own_top - merged_top)
    merged_total = own_total * kept + jnp.sum(w, axis=1, keepdims=True)
    merged_out = own_out * kept + jnp.dot(w.astype(BF16), new_values, preferred_element_type=F32)

    arrived(p_recv, p2_recv_sem)
    lent_part = p_recv[(y - lender[0]) & (NY - 1)].astype(F32)
    coded = lent_part[ROWS:]
    lane16 = lane[:half_rows]
    level = jnp.concatenate([
        jnp.sum(jnp.where(lane16 < 64, coded, 0.0), axis=1, keepdims=True),
        jnp.sum(jnp.where(lane16 < 64, 0.0, coded), axis=1, keepdims=True)], axis=0)
    has_lender = lender[0] >= 0
    level = jnp.where(has_lender, level, NEG)
    lent_out = jnp.where(has_lender, lent_part[:ROWS], 0.0)
    highest = jnp.maximum(merged_top, level)
    kept = jnp.exp2(merged_top - highest)
    added = jnp.exp2(level - highest)
    out_ref[...] = (merged_out * kept + lent_out * added) / (merged_total * kept + added)

    for copy in st_copies:
        copy.wait_send()
    for e in range(1, NY):
        q1_row(0, e).wait_send()

    @pl.when(late | is_even)
    def _():
        q1_row(0, 0).wait_send()

    for zz in range(NZ):
        @pl.when(is_even | (z != zz))
        def _():
            result_copy(p_own_first, zz, 0).wait_send()

    @pl.when(early_relay)
    def _():
        push_done(q_send_first, q_recv_first, row, qa_send_sem, qa_recv_sem)

    @pl.when(home_relay)
    def _():
        push_done(q_send_second, q_recv_second, home_place, qb_send_sem, qb_recv_sem)

    @pl.when(is_relay)
    def _():
        relay_done(p_send, p_recv, p2_send_sem, p2_recv_sem)


def on_device(queries, new_states, key_weight, value_weight, key_pool, value_pool, lengths, page_table):
    hbm = pl.BlockSpec(memory_space=pltpu.HBM)
    dma = pltpu.SemaphoreType.DMA

    def rows_of(x):
        return jnp.transpose(x.reshape(STEPS, GROUP, HD), (1, 0, 2)).reshape(ROWS, HD)

    out = pl.pallas_call(
        kernel,
        out_shape=pltpu.VMEM((ROWS, HD), F32),
        in_specs=[hbm] * 8,
        out_specs=pl.BlockSpec(memory_space=pltpu.VMEM),
        scratch_shapes=[
            pltpu.SMEM((1, 32), jnp.int32),
            pltpu.SMEM((32, SLOTS), jnp.int32),
            pltpu.VMEM((32, SLOTS), jnp.int32),
            pltpu.VMEM((SLOTS, PAGE, HD), BF16),
            pltpu.VMEM((SLOTS, PAGE, HD), BF16),
            pltpu.VMEM((NT, GROUP * HD, HD), BF16),
            pltpu.VMEM((NT, GROUP * HD, HD), BF16),
            pltpu.VMEM((CHUNKS, ROWS, CHUNK * PAGE), F32),
            pltpu.VMEM((ROWS, LENT * PAGE), F32),
            pltpu.VMEM((SLOTS, PAGE), F32),
            pltpu.VMEM((NT, ROWS, HD), BF16),
            pltpu.VMEM((HD, LENT * PAGE), BF16),
            pltpu.VMEM((LENT * PAGE, HD), BF16),
            pltpu.VMEM((LENT, PAGE), F32),
            pltpu.VMEM((16, 2 * HD), BF16),
            pltpu.VMEM((2, ROWS, HD), F32),
            pltpu.VMEM((ROWS, HD), BF16),
            pltpu.VMEM((NY, ROWS, HD), BF16),
            pltpu.VMEM((NY, ROWS, HD), BF16),
            pltpu.VMEM((NY, ROWS, HD), BF16),
            pltpu.VMEM((NY, ROWS, HD), BF16),
            pltpu.VMEM((GUESTS * NY, ROWS, HD), BF16),
            pltpu.VMEM((GUESTS * NY, ROWS, HD), BF16),
            pltpu.VMEM((2, NZ, ROWS, HD), BF16),
            pltpu.VMEM((2, NZ, ROWS, HD), BF16),
            pltpu.VMEM((EARLY, ROWS, HD), BF16),
            pltpu.VMEM((2, ROWS, HD), BF16),
            pltpu.VMEM((ROWS + 16, HD), BF16),
            pltpu.VMEM((ROWS + 16, HD), BF16),
            pltpu.VMEM((NZ, ROWS + 16, HD), BF16),
            pltpu.VMEM((NZ, ROWS + 16, HD), BF16),
            pltpu.VMEM((2, NY, ROWS + 16, HD), BF16),
            pltpu.VMEM((NY, ROWS + 16, HD), BF16),
            dma((5,)), dma((PARTS,)), dma((PARTS,)), dma((2,)), dma((NT,)), dma((NT,)),
            pltpu.SemaphoreType.REGULAR((2,)), pltpu.SemaphoreType.REGULAR, pltpu.SemaphoreType.REGULAR,
            dma((NY,)), dma((2, NY)), dma((2, NY)), dma((2, GUESTS * NY)),
            dma((2, NZ)), dma((EARLY,)), dma((2, NZ)), dma((2,)),
            dma((NZ,)), dma((2, NZ)), dma((2, NY)), dma((NY,)),
        ],
        compiler_params=pltpu.CompilerParams(
            collective_id=0, has_side_effects=True, vmem_limit_bytes=VMEM_BYTES),
    )(
        lengths.reshape(1, -1), page_table, rows_of(queries), rows_of(new_states),
        key_weight.reshape(NT, GROUP * HD, HD), value_weight.reshape(NT, GROUP * HD, HD),
        key_pool, value_pool,
    )
    return (
        jnp.transpose(out.reshape(GROUP, STEPS, HD), (1, 0, 2))
        .reshape(1, STEPS, GROUP * HD)
        .astype(BF16)
    )


def solution(mesh):
    placed = (
        P("inst", None, "tensor"),
        P("inst", None, "tensor"),
        P(None, "tensor"),
        P(None, "tensor"),
        P("inst", None, "tensor"),
        P("inst", None, "tensor"),
        P(),
        P(),
    )
    return jax.shard_map(
        on_device, mesh=mesh, in_specs=placed, out_specs=P("inst", None, "tensor"), check_vma=False
    )
```

```python
import functools
import math

import jax
import jax.numpy as jnp
from jax import lax
from jax.experimental import pallas as pl
from jax.experimental.pallas import tpu as pltpu
from jax.sharding import PartitionSpec as P

HD = 128
STEPS = 4
GROUP = 8
ROWS = STEPS * GROUP
PAGE = 256
SLOTS = 64
CHUNK = 8
CHUNKS = SLOTS // CHUNK
PARTS = 4
PART = SLOTS // PARTS
LENT = 16
NY = 4
NZ = 8
NT = 8
EARLY = 2
HOMES = (0, 1)
GUESTS = 3
FIRST = 3
NEG = -1e30
VMEM_BYTES = 60 * 1024 * 1024
Z_ORDER = (4, 3, 5, 2, 6, 1, 7)
Y_ORDER = (2, 1, 3)
T_ORDER = (4, 5, 3, 2, 6, 7, 1)
LOG2E_SCALE = math.log2(math.e) / math.sqrt(HD)
F32 = jnp.float32
BF16 = jnp.bfloat16
MESH = pl.DeviceIdType.MESH
NT_DIMS = (((1,), (1,)), ((), ()))


def remote_copy(src, dst, send_sem, recv_sem, target):
    return pltpu.make_async_remote_copy(
        src_ref=src, dst_ref=dst, send_sem=send_sem, recv_sem=recv_sem, device_id=target, device_id_type=MESH)


def lanes_sum(w):
    total = w[:, :HD]
    for b in range(1, w.shape[1] // HD):
        total = total + w[:, b * HD:(b + 1) * HD]
    return total


def kernel(
    len_hbm, tab_hbm, q_hbm, st_hbm, kw_hbm, vw_hbm, k_hbm, v_hbm,
    out_ref,
    len_smem, tab_smem, tab_ref, k_buf, v_buf, kw_buf, vw_buf, s_buf, guest_buf, bias_buf, st_all,
    kt_buf, vl_buf, lent_bias, new_buf, own_buf, q_own, q_row_even, q_row_odd, q_mid_even, q_mid_odd, q_late_even, q_late_odd, q_send_first, q_send_second, q_recv_first, q_recv_second,
    p_own_first, p_own_second, p_relay_even, p_relay_odd, p_send, p_recv,
    small_sem, k_sem, v_sem, w_sem, st_send_sem, st_recv_sem, ready_sem, plane_sem, go_sem,
    q1_send_sem, q1_row_sem, q1_mid_sem, q1_late_sem, qa_send_sem, qa_recv_sem, qb_send_sem, qb_recv_sem,
    p1_send_sem, p1_recv_sem, p2_send_sem, p2_recv_sem,
):
    inst = lax.axis_index("inst")
    tensor = lax.axis_index("tensor")
    z = inst // NY
    y = inst % NY
    odd = tensor % 2
    even_t = tensor - odd
    odd_t = even_t + 1
    is_relay = odd == 1
    is_even = odd == 0
    early = z < EARLY
    late = z >= EARLY
    early_relay = early & is_relay
    home_relay = is_relay & ((z == HOMES[0]) | (z == HOMES[1]))
    row = jnp.minimum(z, EARLY - 1)
    home_place = jnp.where(z == HOMES[0], 0, 1)
    home_row = jnp.where(z >= 5, HOMES[0], HOMES[1])
    guests_from = jnp.where(z == HOMES[0], 5, 2)

    def at(zz, yy):
        return zz * NY + yy

    z_peer = [at((z + d) % NZ, y) for d in range(NZ)]
    ys = [(y + e) % NY for e in range(NY)]
    y_peer = [at(z, ys[e]) for e in range(NY)]
    t_peer = [(tensor + d) % NT for d in range(NT)]

    barrier = pltpu.get_barrier_semaphore()

    def greet(where, which):
        pl.semaphore_signal(barrier, inc=1, device_id=(where, which), device_id_type=MESH)

    @pl.when(late)
    def _():
        pl.semaphore_wait(barrier, EARLY + NY - 1)
        for c in range(EARLY):
            pl.semaphore_signal(
                ready_sem.at[odd], inc=1, device_id=(at((z + c) % EARLY, y), odd_t), device_id_type=MESH)

    @pl.when(early_relay)
    def _():
        for zz in range(NZ - 1, EARLY - 1, -1):
            greet(at(zz, y), even_t)
            greet(at(zz, y), odd_t)

    @pl.when(home_relay)
    def _():
        for j in range(GUESTS):
            for e in Y_ORDER:
                greet(at(guests_from + j, ys[e]), even_t)
                greet(at(guests_from + j, ys[e]), odd_t)

    @pl.when(early)
    def _():
        for c in range(1, EARLY):
            greet(at((z + c) % EARLY, y), odd_t)

    @pl.when(z == 0)
    def _():
        for d in T_ORDER:
            greet(inst, t_peer[d])

    @pl.when(early_relay)
    def _():
        for e in Y_ORDER:
            greet(y_peer[e], even_t)
            greet(y_peer[e], odd_t)

    @pl.when(early_relay & (z > 0))
    def _():
        greet(inst, even_t)

    small_copies = [
        pltpu.make_async_copy(q_hbm, q_own, small_sem.at[0]),
        pltpu.make_async_copy(st_hbm, st_all.at[0], small_sem.at[1]),
        pltpu.make_async_copy(tab_hbm, tab_ref, small_sem.at[2]),
        pltpu.make_async_copy(len_hbm, len_smem, small_sem.at[3]),
        pltpu.make_async_copy(tab_hbm, tab_smem, small_sem.at[4]),
    ]
    for copy in small_copies:
        copy.start()

    def k_copy(c):
        part = pl.ds(c * PART, PART)
        return pltpu.make_async_copy(k_hbm.at[part], k_buf.at[part], k_sem.at[c])

    def v_copy(c):
        part = pl.ds(c * PART, PART)
        return pltpu.make_async_copy(v_hbm.at[part], v_buf.at[part], v_sem.at[c])

    w_copies = [
        pltpu.make_async_copy(kw_hbm, kw_buf, w_sem.at[0]),
        pltpu.make_async_copy(vw_hbm, vw_buf, w_sem.at[1]),
    ]

    @pl.when(early)
    def _():
        pl.semaphore_wait(
            barrier, NY - 1 + odd * 2 * (EARLY - 1) + jnp.where(z == 0, NT - 1, 1 - odd))

    small_copies[0].wait()

    def q1_copy(place, e, target):
        buffer, slot, sem = place
        return remote_copy(q_own, buffer.at[slot], q1_send_sem.at[e], sem.at[slot], (target, odd_t))

    def q1_row(p, e):
        return q1_copy(((q_row_even, q_row_odd)[p], e, q1_row_sem.at[p]), e, y_peer[e])

    def q1_mid(p, e):
        return q1_copy(((q_mid_even, q_mid_odd)[p], e, q1_mid_sem.at[p]), e, at(home_row, ys[e]))

    def q1_late(p, e):
        return q1_copy(
            ((q_late_even, q_late_odd)[p], ((z + 1) % GUESTS) * NY + e, q1_late_sem.at[p]), e, at(home_row, ys[e]))

    @pl.when(z == 0)
    def _():
        q_mid_even[...] = jnp.zeros_like(q_mid_even)
        q_mid_odd[...] = jnp.zeros_like(q_mid_odd)

    for p in range(2):
        @pl.when(early & (odd == p))
        def _():
            for e in Y_ORDER + (0,) * (1 - p):
                q1_row(p, e).start()

        @pl.when((z == EARLY) & (odd == p))
        def _():
            for e in Y_ORDER + (0,):
                q1_mid(p, e).start()

        @pl.when((z > EARLY) & (odd == p))
        def _():
            for e in Y_ORDER + (0,):
                q1_late(p, e).start()

    for c in range(PARTS):
        k_copy(c).start()
    for c in range(PARTS):
        v_copy(c).start()

    small_copies[1].wait()
    st_copies = [
        remote_copy(st_all.at[0], st_all.at[d], st_send_sem.at[d], st_recv_sem.at[d], (inst, t_peer[d]))
        for d in T_ORDER
    ]

    @pl.when(z == 0)
    def _():
        for copy in st_copies:
            copy.start()

    query = q_own[...]
    q_row_odd[0] = query

    def relay_copy(own, relay, d, p, send_sem, recv_sem):
        return remote_copy(own, relay[p].at[d], send_sem.at[d], recv_sem.at[p, d], (z_peer[d], odd_t))

    for copy in small_copies[2:]:
        copy.wait()
    table = tab_ref[...]
    holder = table >> 6
    row_id = lax.broadcasted_iota(jnp.int32, table.shape, 0)
    page_id = lax.broadcasted_iota(jnp.int32, table.shape, 1)
    lent = (table >= 0) & (holder != row_id)
    lent_code = jnp.where(lent, row_id * SLOTS + (SLOTS - 1) - page_id, -1)
    lent_holder = jnp.where(lent, holder, -1)
    guest_code = [jnp.max(jnp.where(holder == z_peer[d], lent_code, -1)) for d in range(NZ)]
    lender = [jnp.max(jnp.where(row_id == y_peer[e], lent_holder, -1)) for e in range(NY)]

    own_length = len_smem[0, inst]
    own_row = jnp.broadcast_to(tab_ref[pl.ds(inst, 1), :] - inst * SLOTS, (SLOTS, SLOTS))
    slot_id = lax.broadcasted_iota(jnp.int32, (SLOTS, SLOTS), 0)
    page_of = lax.broadcasted_iota(jnp.int32, (SLOTS, SLOTS), 1)
    counted = jnp.clip(own_length - page_of * PAGE, 0, PAGE).astype(F32)
    valid = jnp.sum(jnp.where(own_row == slot_id, counted, 0.0), axis=1, keepdims=True)
    token = lax.broadcasted_iota(jnp.int32, (SLOTS, PAGE), 1).astype(F32)
    bias_buf[...] = jnp.where(token < valid, 0.0, NEG)

    guest = guest_code[0] >> 6
    first_page = (SLOTS - 1) - (guest_code[0] & (SLOTS - 1))
    guest_row = jnp.maximum(guest, 0)
    guest_length = jnp.where(guest >= 0, len_smem[0, guest_row], 0)
    guest_pages = ((guest_length + PAGE - 1) // PAGE) // 4
    page_token = lax.broadcasted_iota(jnp.int32, (1, PAGE), 1)
    slots = []
    limits = []
    for i in range(LENT):
        page = jnp.minimum(first_page + i, SLOTS - 1)
        slots.append(jnp.clip(tab_smem[guest_row, page] - inst * SLOTS, 0, SLOTS - 1))
        limits.append(jnp.where(i < guest_pages, guest_length - page * PAGE, 0))

    def scores_chunk(c, top):
        for p in range(CHUNK):
            slot = c * CHUNK + p
            s = lax.dot_general(query, k_buf[slot], NT_DIMS, preferred_element_type=F32)
            s = s + bias_buf[pl.ds(slot, 1), :]
            s_buf[c, :, p * PAGE:(p + 1) * PAGE] = s
            top = jnp.maximum(top, jnp.maximum(s[:, :HD], s[:, HD:]))
        return top

    def values_chunk(c, carry):
        total, numerator = carry
        half = CHUNK // 2
        for h in range(2):
            s = s_buf[c, :, h * half * PAGE:(h + 1) * half * PAGE]
            w = jnp.exp2(s * LOG2E_SCALE - own_top)
            total = total + lanes_sum(w)
            v = v_buf[pl.ds(c * CHUNK + h * half, half)].reshape(half * PAGE, HD)
            numerator = numerator + jnp.dot(w.astype(BF16), v, preferred_element_type=F32)
        return total, numerator

    per_part = CHUNKS // PARTS
    top = jnp.full((ROWS, HD), NEG, F32)
    for c in range(PARTS):
        k_copy(c).wait()
        top = lax.fori_loop(c * per_part, (c + 1) * per_part, scores_chunk, top)
    own_top = jnp.max(top, axis=1, keepdims=True) * LOG2E_SCALE

    def pick_first(p, r):
        e = (y - r) & (NY - 1)
        return lax.select((r >> 2) == EARLY, (q_mid_even, q_mid_odd)[p][e], (q_row_even, q_row_odd)[p][e])

    def pick_second(p, r):
        return (q_late_even, q_late_odd)[p][(((r >> 2) + 1) % GUESTS) * NY + ((y - r) & (NY - 1))]

    def push(p, d, sent, received, slot, send_sem, recv_sem):
        return remote_copy(
            sent.at[p, d], received.at[slot], send_sem.at[p, d], recv_sem.at[slot], (z_peer[d], even_t + p))

    def push_all(p, pick, sent, received, slot, send_sem, recv_sem):
        for d in Z_ORDER + (0,):
            picked = pick(guest_code[d] >> 6)
            if p == 1 and d == 0:
                received[slot] = picked
            else:
                sent[p, d] = picked
                push(p, d, sent, received, slot, send_sem, recv_sem).start()

    def push_done(sent, received, slot, send_sem, recv_sem):
        for p in range(2):
            for d in Z_ORDER + (0,) * (1 - p):
                push(p, d, sent, received, slot, send_sem, recv_sem).wait_send()

    for copy in w_copies:
        copy.start()

    @pl.when(early_relay)
    def _():
        for p in (1, 0):
            for e in Y_ORDER + (0,) * (1 - p):
                q1_row(p, e).wait_recv()

        @pl.when(z == HOMES[1])
        def _():
            for p in (1, 0):
                for e in Y_ORDER + (0,):
                    q1_mid(p, e).wait_recv()

        for p in range(2):
            for d in range(NZ):
                picked = pick_first(p, guest_code[d] >> 6)
                if p == 1 and d == 0:
                    q_recv_first[row] = picked
                else:
                    q_send_first[p, d] = picked
        for p in (1, 0):
            pl.semaphore_wait(ready_sem.at[p], NZ - EARLY)
            for d in Z_ORDER + (0,) * (1 - p):
                push(p, d, q_send_first, q_recv_first, row, qa_send_sem, qa_recv_sem).start()

    @pl.when(early_relay & (z == 0))
    def _():
        for d in (2, 4, 6):
            pl.semaphore_signal(plane_sem, inc=1, device_id=(inst, t_peer[d]), device_id_type=MESH)

    def own_values():
        total, numerator = lax.fori_loop(
            0, CHUNKS, values_chunk, (jnp.zeros((ROWS, HD), F32), jnp.zeros((ROWS, HD), F32)))
        own_buf[0] = total
        own_buf[1] = numerator

    for c in range(PARTS):
        v_copy(c).wait()
    pl.when(early)(own_values)

    @pl.when(home_relay)
    def _():
        for p in (1, 0):
            for j in range(GUESTS):
                @pl.when((z == HOMES[0]) | (j > 0))
                def _():
                    for e in Y_ORDER + (0,):
                        slot = j * NY + e
                        remote_copy(
                            q_own, (q_late_even, q_late_odd)[p].at[slot], q1_send_sem.at[e],
                            q1_late_sem.at[p, slot], (inst, odd_t)).wait_recv()

            push_all(
                p, functools.partial(pick_second, p),
                q_send_second, q_recv_second, home_place, qb_send_sem, qb_recv_sem)

    lane = lax.broadcasted_iota(jnp.int32, (ROWS, HD), 1)
    half_rows = ROWS // 2

    def lent_result(guest_query):
        tops = []
        span = 4 * PAGE
        for i in range(LENT // 4):
            s = jnp.dot(guest_query, kt_buf[:, i * span:(i + 1) * span], preferred_element_type=F32)
            s = s + lent_bias[:, i * span:(i + 1) * span]
            guest_buf[:, i * span:(i + 1) * span] = s
            tops += [s[:, b * HD:(b + 1) * HD] for b in range(span // HD)]
        while len(tops) > 1:
            tops = [jnp.maximum(m, n) for m, n in zip(tops[::2], tops[1::2])]
        guest_top = jnp.max(tops[0], axis=1, keepdims=True) * LOG2E_SCALE
        totals = []
        guest_out = jnp.zeros((ROWS, HD), F32)
        wide = 4 * PAGE
        for i in range(LENT // 4):
            s = guest_buf[:, i * wide:(i + 1) * wide]
            w = jnp.exp2(s * LOG2E_SCALE - guest_top)
            totals.append(lanes_sum(w))
            guest_out = guest_out + jnp.dot(
                w.astype(BF16), vl_buf[i * wide:(i + 1) * wide, :], preferred_element_type=F32)
        total = (totals[0] + totals[1]) + (totals[2] + totals[3])
        guest_total = jnp.sum(total, axis=1, keepdims=True)
        level = jnp.broadcast_to(guest_top + jnp.log2(guest_total), (ROWS, HD))
        high = level.astype(BF16).astype(F32)
        middle = (level - high).astype(BF16).astype(F32)
        low = level - high - middle
        place = lane & 63
        coded = jnp.where(place == 0, high, jnp.where(place == 1, middle, jnp.where(place == 2, low, 0.0)))
        coded = jnp.where(lane[:half_rows] < 64, coded[:half_rows], coded[half_rows:])
        return jnp.concatenate([guest_out / guest_total, coded], axis=0).astype(BF16)

    p_relay = (p_relay_even, p_relay_odd)

    def result_copy(own, zz, p):
        slot = (zz - z) & (NZ - 1)
        return remote_copy(
            own, p_relay[p].at[slot], p1_send_sem.at[zz], p1_recv_sem.at[p, slot], (at(zz, y), odd_t))

    def send_result(own, rows):
        @pl.when(is_even)
        def _():
            for zz in rows:
                result_copy(own, zz, 0).start()

        for zz in rows:
            @pl.when(is_relay & (z != zz))
            def _():
                result_copy(own, zz, 1).start()

    def wait_arrival(received, slot, recv_sem, source):
        @pl.when(jnp.logical_not(is_relay & (z == source)))
        def _():
            remote_copy(
                received.at[slot], received.at[slot], recv_sem.at[slot], recv_sem.at[slot], (inst, odd_t)
            ).wait_recv()

    guest_z = guest_row >> 2
    for i in range(LENT):
        kt_buf[:, i * PAGE:(i + 1) * PAGE] = k_buf[slots[i]].T
        vl_buf[i * PAGE:(i + 1) * PAGE, :] = v_buf[slots[i]]
        lent_bias[:, i * PAGE:(i + 1) * PAGE] = jnp.where(page_token < limits[i], 0.0, NEG)

    @pl.when(early_relay & (z == 0))
    def _():
        pl.semaphore_wait(plane_sem, NT // 2 - 1)
        for zz in range(1, NZ):
            for which in (even_t, odd_t):
                pl.semaphore_signal(go_sem, inc=1, device_id=(at(zz, y), which), device_id_type=MESH)

    for zz in range(EARLY):
        wait_arrival(q_recv_first, zz, qa_recv_sem, zz)
    result = lent_result(q_recv_first[jnp.minimum(guest_z, EARLY - 1)])
    p_own_first[...] = result
    send_result(p_own_first, range(FIRST))

    @pl.when(z < FIRST)
    def _():
        p_relay_odd[0] = result

    pl.when(late)(own_values)
    for j in range(2):
        wait_arrival(q_recv_second, j, qb_recv_sem, HOMES[j])
    result = lent_result(q_recv_second[jnp.where(guest_z >= 5, 0, 1)])
    p_own_second[...] = result
    send_result(p_own_second, range(FIRST, NZ))

    @pl.when(z >= FIRST)
    def _():
        p_relay_odd[0] = result

    @pl.when(z > 0)
    def _():
        pl.semaphore_wait(go_sem, 1)
        for copy in st_copies:
            copy.start()

    def project_all():
        for copy in w_copies:
            copy.wait()
        for copy in st_copies:
            copy.wait_recv()
        row16 = lax.broadcasted_iota(jnp.int32, (16, HD), 0) // STEPS

        def project(d, acc):
            source = (tensor - d + NT) % NT
            for h in range(2):
                x = st_all[d, h * 16:(h + 1) * 16, :].astype(F32)
                left = jnp.concatenate([jnp.where(row16 == g, x, 0.0) for g in range(4)], axis=1).astype(BF16)
                weight = jnp.concatenate(
                    [kw_buf[source, h * 512:(h + 1) * 512, :], vw_buf[source, h * 512:(h + 1) * 512, :]], axis=1)
                acc = acc + jnp.dot(left, weight, preferred_element_type=F32)
            return acc

        acc = lax.fori_loop(0, NT, project, jnp.zeros((16, 2 * HD), F32))
        acc = acc[:8] + acc[8:]
        acc = acc[:4] + acc[4:]
        new_buf[...] = jnp.concatenate([acc, jnp.zeros((12, 2 * HD), F32)], axis=0).astype(BF16)

    pl.when(z == 0)(project_all)

    def relayed(relay, source, sent, received, arrive_sem, send_sem, recv_sem):
        @pl.when(is_relay)
        def _():
            for p in (1, 0):
                for d in Z_ORDER + (0,) * (1 - p):
                    relay_copy(sent.at[p, 0], relay, d, p, arrive_sem.at[p], arrive_sem).wait_recv()
                for e in Y_ORDER + (0,):
                    picked = relay[p][source[e]]
                    if p == 1 and e == 0:
                        received[0] = picked
                    else:
                        sent[p, e] = picked
                        remote_copy(
                            sent.at[p, e], received.at[e], send_sem.at[p, e], recv_sem.at[e], (y_peer[e], even_t + p)
                        ).start()

    def relay_done(sent, received, send_sem, recv_sem):
        for p in range(2):
            for e in Y_ORDER + (0,) * (1 - p):
                remote_copy(
                    sent.at[p, e], received.at[e], send_sem.at[p, e], recv_sem.at[e], (y_peer[e], even_t + p)
                ).wait_send()

    def arrived(received, recv_sem):
        for e in Y_ORDER:
            remote_copy(
                received.at[e], received.at[e], recv_sem.at[e], recv_sem.at[e], (y_peer[e], odd_t)
            ).wait_recv()

        @pl.when(jnp.logical_not(is_relay))
        def _():
            remote_copy(
                received.at[0], received.at[0], recv_sem.at[0], recv_sem.at[0], (inst, odd_t)
            ).wait_recv()

    relayed(
        p_relay, [(z - (lender[e] >> 2)) & (NZ - 1) for e in range(NY)], p_send, p_recv,
        p1_recv_sem, p2_send_sem, p2_recv_sem)
    pl.when(z > 0)(project_all)
    own_total = jnp.sum(own_buf[0], axis=1, keepdims=True)
    own_out = own_buf[1]
    new_keys = new_buf[:, :HD]
    new_values = new_buf[:, HD:]
    s = lax.dot_general(query, new_keys, NT_DIMS, preferred_element_type=F32)
    step = lax.broadcasted_iota(jnp.int32, (ROWS, 16), 0) % STEPS
    other = lax.broadcasted_iota(jnp.int32, (ROWS, 16), 1)
    s = jnp.where(other <= step, s * LOG2E_SCALE, NEG)
    merged_top = jnp.maximum(own_top, jnp.max(s, axis=1, keepdims=True))
    w = jnp.exp2(s - merged_top)
    kept = jnp.exp2(own_top - merged_top)
    merged_total = own_total * kept + jnp.sum(w, axis=1, keepdims=True)
    merged_out = own_out * kept + jnp.dot(w.astype(BF16), new_values, preferred_element_type=F32)

    arrived(p_recv, p2_recv_sem)
    lent_part = p_recv[(y - lender[0]) & (NY - 1)].astype(F32)
    coded = lent_part[ROWS:]
    lane16 = lane[:half_rows]
    level = jnp.concatenate([
        jnp.sum(jnp.where(lane16 < 64, coded, 0.0), axis=1, keepdims=True),
        jnp.sum(jnp.where(lane16 < 64, 0.0, coded), axis=1, keepdims=True)], axis=0)
    has_lender = lender[0] >= 0
    level = jnp.where(has_lender, level, NEG)
    lent_out = jnp.where(has_lender, lent_part[:ROWS], 0.0)
    highest = jnp.maximum(merged_top, level)
    kept = jnp.exp2(merged_top - highest)
    added = jnp.exp2(level - highest)
    out_ref[...] = (merged_out * kept + lent_out * added) / (merged_total * kept + added)

    for copy in st_copies:
        copy.wait_send()
    for e in range(1, NY):
        q1_row(0, e).wait_send()

    @pl.when(late | is_even)
    def _():
        q1_row(0, 0).wait_send()

    for zz in range(NZ):
        @pl.when(is_even | (z != zz))
        def _():
            result_copy(p_own_first, zz, 0).wait_send()

    @pl.when(early_relay)
    def _():
        push_done(q_send_first, q_recv_first, row, qa_send_sem, qa_recv_sem)

    @pl.when(home_relay)
    def _():
        push_done(q_send_second, q_recv_second, home_place, qb_send_sem, qb_recv_sem)

    @pl.when(is_relay)
    def _():
        relay_done(p_send, p_recv, p2_send_sem, p2_recv_sem)


def on_device(queries, new_states, key_weight, value_weight, key_pool, value_pool, lengths, page_table):
    hbm = pl.BlockSpec(memory_space=pltpu.HBM)
    dma = pltpu.SemaphoreType.DMA

    def rows_of(x):
        return jnp.transpose(x.reshape(STEPS, GROUP, HD), (1, 0, 2)).reshape(ROWS, HD)

    out = pl.pallas_call(
        kernel,
        out_shape=pltpu.VMEM((ROWS, HD), F32),
        in_specs=[hbm] * 8,
        out_specs=pl.BlockSpec(memory_space=pltpu.VMEM),
        scratch_shapes=[
            pltpu.SMEM((1, 32), jnp.int32),
            pltpu.SMEM((32, SLOTS), jnp.int32),
            pltpu.VMEM((32, SLOTS), jnp.int32),
            pltpu.VMEM((SLOTS, PAGE, HD), BF16),
            pltpu.VMEM((SLOTS, PAGE, HD), BF16),
            pltpu.VMEM((NT, GROUP * HD, HD), BF16),
            pltpu.VMEM((NT, GROUP * HD, HD), BF16),
            pltpu.VMEM((CHUNKS, ROWS, CHUNK * PAGE), F32),
            pltpu.VMEM((ROWS, LENT * PAGE), F32),
            pltpu.VMEM((SLOTS, PAGE), F32),
            pltpu.VMEM((NT, ROWS, HD), BF16),
            pltpu.VMEM((HD, LENT * PAGE), BF16),
            pltpu.VMEM((LENT * PAGE, HD), BF16),
            pltpu.VMEM((1, LENT * PAGE), F32),
            pltpu.VMEM((16, 2 * HD), BF16),
            pltpu.VMEM((2, ROWS, HD), F32),
            pltpu.VMEM((ROWS, HD), BF16),
            pltpu.VMEM((NY, ROWS, HD), BF16),
            pltpu.VMEM((NY, ROWS, HD), BF16),
            pltpu.VMEM((NY, ROWS, HD), BF16),
            pltpu.VMEM((NY, ROWS, HD), BF16),
            pltpu.VMEM((GUESTS * NY, ROWS, HD), BF16),
            pltpu.VMEM((GUESTS * NY, ROWS, HD), BF16),
            pltpu.VMEM((2, NZ, ROWS, HD), BF16),
            pltpu.VMEM((2, NZ, ROWS, HD), BF16),
            pltpu.VMEM((EARLY, ROWS, HD), BF16),
            pltpu.VMEM((2, ROWS, HD), BF16),
            pltpu.VMEM((ROWS + 16, HD), BF16),
            pltpu.VMEM((ROWS + 16, HD), BF16),
            pltpu.VMEM((NZ, ROWS + 16, HD), BF16),
            pltpu.VMEM((NZ, ROWS + 16, HD), BF16),
            pltpu.VMEM((2, NY, ROWS + 16, HD), BF16),
            pltpu.VMEM((NY, ROWS + 16, HD), BF16),
            dma((5,)), dma((PARTS,)), dma((PARTS,)), dma((2,)), dma((NT,)), dma((NT,)),
            pltpu.SemaphoreType.REGULAR((2,)), pltpu.SemaphoreType.REGULAR, pltpu.SemaphoreType.REGULAR,
            dma((NY,)), dma((2, NY)), dma((2, NY)), dma((2, GUESTS * NY)),
            dma((2, NZ)), dma((EARLY,)), dma((2, NZ)), dma((2,)),
            dma((NZ,)), dma((2, NZ)), dma((2, NY)), dma((NY,)),
        ],
        compiler_params=pltpu.CompilerParams(
            collective_id=0, has_side_effects=True, vmem_limit_bytes=VMEM_BYTES),
    )(
        lengths.reshape(1, -1), page_table, rows_of(queries), rows_of(new_states),
        key_weight.reshape(NT, GROUP * HD, HD), value_weight.reshape(NT, GROUP * HD, HD),
        key_pool, value_pool,
    )
    return (
        jnp.transpose(out.reshape(GROUP, STEPS, HD), (1, 0, 2))
        .reshape(1, STEPS, GROUP * HD)
        .astype(BF16)
    )


def solution(mesh):
    placed = (
        P("inst", None, "tensor"),
        P("inst", None, "tensor"),
        P(None, "tensor"),
        P(None, "tensor"),
        P("inst", None, "tensor"),
        P("inst", None, "tensor"),
        P(),
        P(),
    )
    return jax.shard_map(
        on_device, mesh=mesh, in_specs=placed, out_specs=P("inst", None, "tensor"), check_vma=False
    )
```
